128 devices in a mesh: level: 4 (over z), space: 32 (over x, y, core).
Axes of the slice: x: 4, y: 4, z: 4, core: 2. Of those that a mesh axis runs over, the one named last changes fastest.
Arguments:
- features: bfloat16 [2048, 96, 512], P(('level', 'space')), may hold values from -6 to 6
- occupancy: int32 [2048, 512], P(('level', 'space')), may hold values from 0 to 1
- brick_coords: int32 [3, 2048], P(None, ('level', 'space')), may hold values from 0 to 15, as said below
- coarse_owner: int32 [256, 1], P(('level', 'space')), may hold values from 0 to 3; in each aligned block of 2 rows (0 to 1, 2 to 3, ...) at most 2 rows name the same one
- conv_weight: bfloat16 [27, 96, 96], replicated, may hold values from -0.125 to 0.125
- conv_gain: float32 [96], replicated, may hold values from 0.25 to 1.75
- conv_shift: float32 [96], replicated, may hold values from -2.5 to 2.5
- reduce_weight: bfloat16 [8, 192, 96], replicated, may hold values from -0.21875 to 0.21875
- down_gain: float32 [192], replicated, may hold values from 0.25 to 1.75
- down_shift: float32 [192], replicated, may hold values from -2.5 to 2.5
Outputs:
- coarse_map: bfloat16 [1024, 192, 512], P(('level', 'space'))
The draws below stay inside these ranges and needn't reach their ends.
Inputs may be any that keep to these rules, and one draw needn't show every extreme that they name: `brick_coords`: device s of level group l holds, in some order, all 2 x 4 x 2 bricks of tile (s // 4, s mod 4) of region l: x from 2 * (s // 4), y from 4 * (s mod 4), z from 0. `coarse_owner`: in the 2 rows of one device, no owner group is named more than 2 times.
All inputs are finite; a program needn't handle non-finite values.
Results may differ from the reference program's by a relative error of at most 0.0054.
Values may be sent and summed in bfloat16 or wider, within the bound.
No kernel may reach another device: no remote copies, remote signals or barrier semaphores. Data moves between devices by JAX's collectives and lax.ppermute only.
A program may use at most 192 MiB of HBM per device.

```python
import math
import jax
import jax.numpy as jnp
import numpy as np
from jax import lax

C = 96
C2 = 192
BRICK = 8
CELLS = 512
TX = 2
TY = 4
TZ = 2
CAPC = 2
GRID_Y = 4
GRID_X = 8
BRICKS_DEV = 16
FINE = 2048
QC = 2
COARSE = 1024
N_LEVEL = 4
N_SPACE = 32
DEVICES = 128


def row_factors(key, low, high, brick_low, brick_high):
    tile_key, brick_key = jax.random.split(key)
    tiles = FINE // BRICKS_DEV
    tile_scale = jnp.exp(jax.random.uniform(tile_key, (tiles,), jnp.float32, jnp.log(low), jnp.log(high)))
    brick_scale = jax.random.uniform(brick_key, (FINE,), jnp.float32, brick_low, brick_high)
    return jnp.repeat(tile_scale, BRICKS_DEV) * brick_scale


def draw_features(key, part):
    key = jax.random.fold_in(key, 11)
    base_key, scale_key = jax.random.split(key, 2)
    factors = row_factors(scale_key, 0.3, 2.8, 0.85, 1.15)
    values = jax.random.normal(base_key, (FINE, C, CELLS), jnp.float32) * factors[:, None, None]
    return jnp.clip(values, -6.0, 6.0).astype(jnp.bfloat16)


def draw_occupancy(key, part):
    key = jax.random.fold_in(key, 12)
    level_key, tile_key, brick_key = jax.random.split(key, 3)
    tiles = FINE // BRICKS_DEV
    levels = jax.random.randint(level_key, (FINE, CELLS), 0, 1000)
    tile_limit = jax.random.randint(tile_key, (tiles,), 250, 751)
    jitter = jax.random.randint(brick_key, (FINE,), -100, 101)
    limits = jnp.repeat(tile_limit, BRICKS_DEV) + jitter
    return (levels < limits[:, None]).astype(jnp.int32)


def draw_brick_coords(key, part):
    key = jax.random.fold_in(key, 13)
    device_total = N_LEVEL * N_SPACE
    subkeys = jax.random.split(key, device_total)
    orders = jax.vmap(lambda subkey: jax.random.permutation(subkey, BRICKS_DEV))(subkeys).astype(jnp.int32)
    space_index = jnp.arange(device_total, dtype=jnp.int32)[:, None] % N_SPACE
    local_x = orders // (TY * TZ)
    local_y = orders // TZ % TY
    local_z = orders % TZ
    coord_x = space_index // GRID_Y * TX + local_x
    coord_y = space_index % GRID_Y * TY + local_y
    return jnp.stack([coord_x.reshape(-1), coord_y.reshape(-1), local_z.reshape(-1)]).astype(jnp.int32)


def deal_out(stream_key, own, number, rows, number_of, top, bound, slope):
    ranking = jax.random.permutation(stream_key, number_of)
    packed, usual = shares(number_of, rows * top, bound, slope, True), shares(number_of, rows * top, bound, slope, False)
    places = jnp.arange(number_of)

    def named(lengths, rotation):
        used = int((lengths > 0).sum())
        fixed = max(1, used // 4)
        shifted = fixed + (places - fixed + rotation * (used - fixed)) % max(1, number_of - fixed)
        return jnp.zeros((number_of,), jnp.int32).at[ranking[jnp.where(places < fixed, places, shifted)]].set(jnp.asarray(lengths, jnp.int32))

    lengths = jnp.where(number % 4 == 0, named(packed, number // 4), named(usual, number - number // 4 - 1))
    mixed = jax.random.permutation(jax.random.fold_in(own, 3), number_of)
    giver, sink = mixed[0:number_of // 2 * 2:2], mixed[1:number_of // 2 * 2:2]
    slack = jnp.minimum(lengths[giver] - 1, bound - lengths[sink]) // 2
    slack = jnp.where((giver == ranking[0]) | (sink == ranking[0]) | (lengths[sink] == 0), 0, jnp.maximum(slack, 0))
    shifted = jax.random.randint(jax.random.fold_in(own, 4), (number_of // 2,), 0, 1 << 20) % (slack + 1)
    lengths = lengths.at[giver].add(-shifted).at[sink].add(shifted)
    labels = jnp.searchsorted(jnp.cumsum(lengths), jnp.arange(rows * top), side="right").astype(jnp.int32)
    grid = labels.reshape(top, rows).T
    grid = grid[jax.random.permutation(jax.random.fold_in(own, 1), rows)]
    rotation = jax.random.randint(jax.random.fold_in(own, 2), (rows, 1), 0, top)
    return jnp.take_along_axis(grid, (jnp.arange(top)[None, :] + rotation) % top, axis=1)


def shares(amount, total, bound, skew, full):
    loads = [(1 << 20) // math.isqrt(standing ** skew) + 1 for standing in range(1, amount + 1)]
    largest = bound if full else min(bound, max(-(-total // amount), total * loads[0] // sum(loads)))
    least = 1 if total - largest >= amount - 1 else 0
    given, rest = [largest] + [least] * (amount - 1), total - largest - least * (amount - 1)
    while rest > 0:
        movable = [i for i in range(1, amount) if given[i] < largest] or [i for i in range(1, amount) if given[i] < bound]
        whole, remaining = sum([loads[i] for i in movable]), rest
        for i in movable:
            more = min(bound - given[i], max(1, remaining * loads[i] // whole), rest)
            given[i] = given[i] + more
            rest = rest - more
    return np.array(given)


def bell_draw(rng, extent, scale, most, held_as=jnp.bfloat16):
    values = scale * jax.random.normal(rng, extent, jnp.float32)
    return jnp.clip(values, min=-most, max=most).astype(held_as)


def setup_inputs(seed: int = 0) -> dict:
    seeds = jax.random.split(jax.random.key(seed), 11)
    features = draw_features(jax.random.fold_in(seeds[10], 71), 0)
    occupancy = draw_occupancy(jax.random.fold_in(seeds[10], 71), 0)
    brick_coords = draw_brick_coords(jax.random.fold_in(seeds[10], 71), 0)
    coarse_owner_keys = jax.random.split(jax.random.fold_in(seeds[3], 1), (DEVICES * QC) // QC)
    coarse_owner_turns = jax.random.permutation(jax.random.fold_in(seeds[3], 3), (DEVICES * QC) // QC)
    coarse_owner = jax.vmap(lambda own, number: deal_out(jax.random.fold_in(seeds[3], 2), own, number, QC, N_LEVEL, 1, CAPC, 2))(coarse_owner_keys, coarse_owner_turns).reshape((DEVICES * QC, 1))
    conv_weight = bell_draw(seeds[4], (27, C, C), (27 * C) ** -0.5, 0.125)
    conv_gain = jnp.clip(1.0 + 0.15 * jax.random.normal(seeds[5], (C,), jnp.float32), 0.25, 1.75)
    conv_shift = bell_draw(seeds[6], (C,), 0.5, 2.5, jnp.float32)
    reduce_weight = bell_draw(seeds[7], (8, C2, C), (8 * C) ** -0.5, 0.21875)
    down_gain = jnp.clip(1.0 + 0.15 * jax.random.normal(seeds[8], (C2,), jnp.float32), 0.25, 1.75)
    down_shift = bell_draw(seeds[9], (C2,), 0.5, 2.5, jnp.float32)
    return {"features": features, "occupancy": occupancy, "brick_coords": brick_coords, "coarse_owner": coarse_owner, "conv_weight": conv_weight, "conv_gain": conv_gain, "conv_shift": conv_shift, "reduce_weight": reduce_weight, "down_gain": down_gain, "down_shift": down_shift}


epsilon = 1e-05

def place_bricks(values, coords_part):
    number, depth = (values.shape[0], values.shape[1])
    shaped = values.reshape(number, depth, BRICK, BRICK, BRICK)
    holder = jnp.zeros((GRID_X * TX, GRID_Y * TY, TZ, depth, BRICK, BRICK, BRICK), values.dtype)
    holder = holder.at[coords_part[0], coords_part[1], coords_part[2]].set(shaped)
    holder = holder.transpose(3, 0, 4, 1, 5, 2, 6)
    return holder.reshape(depth, GRID_X * TX * BRICK, GRID_Y * TY * BRICK, TZ * BRICK)

def convolve(active, conv_weight):
    depth, size_x, size_y, size_z = active.shape
    padded_grid = jnp.pad(active, ((0, 0), (1, 1), (1, 1), (1, 1)))
    total = jnp.zeros((conv_weight.shape[1], size_x * size_y * size_z), jnp.float32)
    for tap_index in range(27):
        shift_a, shift_b, shift_c = (tap_index // 9, tap_index // 3 % 3, tap_index % 3)
        window = padded_grid[:, shift_a:shift_a + size_x, shift_b:shift_b + size_y, shift_c:shift_c + size_z]
        total = total + jnp.dot(conv_weight[tap_index].astype(jnp.float32), window.reshape(depth, -1).astype(jnp.float32), preferred_element_type=jnp.float32)
    return total.reshape(-1, size_x, size_y, size_z)

def reduce_resolution(brick_section, reduce_weight):
    depth, size_x, size_y, size_z = brick_section.shape
    split_view = brick_section.reshape(depth, size_x // 2, 2, size_y // 2, 2, size_z // 2, 2)
    total = jnp.zeros((reduce_weight.shape[1], size_x // 2 * (size_y // 2) * (size_z // 2)), jnp.float32)
    for offset_index in range(8):
        off_a, off_b, off_c = (offset_index // 4, offset_index // 2 % 2, offset_index % 2)
        window = split_view[:, :, off_a, :, off_b, :, off_c]
        total = total + jnp.dot(reduce_weight[offset_index].astype(jnp.float32), window.reshape(depth, -1).astype(jnp.float32), preferred_element_type=jnp.float32)
    return total.reshape(-1, size_x // 2, size_y // 2, size_z // 2)

def coarse_pool(region_mask):
    size_x, size_y, size_z = region_mask.shape
    return region_mask.reshape(size_x // 2, 2, size_y // 2, 2, size_z // 2, 2).max(axis=(1, 3, 5))

def moments(value_collection, weights_list):
    total_count = sum([jnp.sum(weights) for weights in weights_list])
    first = sum([lax.optimization_barrier(jnp.sum(values * weights, axis=(1, 2, 3))) for values, weights in zip(value_collection, weights_list)])
    mean = first / total_count
    second = sum([lax.optimization_barrier(jnp.sum(weights * (values - mean[:, None, None, None]) ** 2, axis=(1, 2, 3))) for values, weights in zip(value_collection, weights_list)])
    return (mean, second / total_count)

def to_rows(coarse):
    depth = coarse.shape[0]
    shaped = coarse.reshape(depth, GRID_X, TX // 2, BRICK, GRID_Y, TY // 2, BRICK, TZ // 2, BRICK)
    return shaped.transpose(1, 4, 2, 5, 7, 0, 3, 6, 8).reshape(N_SPACE * QC, depth, CELLS)

def reference(features, occupancy, brick_coords, coarse_owner, conv_weight, conv_gain, conv_shift, reduce_weight, down_gain, down_shift):
    per_level = N_SPACE * BRICKS_DEV
    actives, masks, convs = ([], [], [])
    for level in range(N_LEVEL):
        first_row = level * per_level
        occupied = occupancy[first_row:first_row + per_level]
        coords_part = brick_coords[:, first_row:first_row + per_level]
        masked = features[first_row:first_row + per_level] * occupied.astype(jnp.bfloat16)[:, None, :]
        active = place_bricks(masked, coords_part)
        region_mask = place_bricks(occupied.astype(jnp.float32)[:, None, :], coords_part)[0]
        actives.append(active)
        masks.append(region_mask)
        convs.append(convolve(active, conv_weight) * region_mask)
    mean1, var1 = moments(convs, masks)
    first_scale = conv_gain / jnp.sqrt(var1 + epsilon)
    reduced_list, lowres_mask_list = ([], [])
    for level in range(N_LEVEL):
        normed = (convs[level] - mean1[:, None, None, None]) * first_scale[:, None, None, None] + conv_shift[:, None, None, None]
        brick_section = (actives[level].astype(jnp.float32) + masks[level] * jnp.maximum(normed, 0.0)).astype(jnp.bfloat16)
        reduced_list.append(reduce_resolution(brick_section, reduce_weight).astype(jnp.bfloat16))
        lowres_mask_list.append(coarse_pool(masks[level]))
    down_values = [down.astype(jnp.float32) for down in reduced_list]
    mean2, var2 = moments(down_values, lowres_mask_list)
    scale2 = down_gain / jnp.sqrt(var2 + epsilon)
    settled_rows = []
    for level in range(N_LEVEL):
        normed = (down_values[level] - mean2[:, None, None, None]) * scale2[:, None, None, None] + down_shift[:, None, None, None]
        settled = lowres_mask_list[level] * jnp.maximum(normed, 0.0)
        settled_rows.append(to_rows(settled).astype(jnp.bfloat16))
    values = jnp.concatenate(settled_rows, axis=0)
    owners = coarse_owner[:, 0].reshape(-1, QC)
    quarter = jnp.arange(QC, dtype=jnp.int32)
    earlier = (quarter[None, None, :] < quarter[None, :, None]) & (owners[:, None, :] == owners[:, :, None])
    ranks = lax.optimization_barrier(jnp.sum(earlier.astype(jnp.int32), axis=2))
    device_ids = jnp.arange(owners.shape[0], dtype=jnp.int32)[:, None]
    level_ids = device_ids // N_SPACE
    space_ids = device_ids % N_SPACE
    targets = ((owners * N_SPACE + space_ids) * N_LEVEL + level_ids) * CAPC + ranks
    coarse_map = jnp.zeros((COARSE, values.shape[1], CELLS), jnp.bfloat16)
    return coarse_map.at[targets.reshape(-1).astype(jnp.int32)].set(values)
```

```python
import jax
import jax.numpy as jnp
from jax import lax
from jax.sharding import PartitionSpec as P

BRICK = 8
TX = 2
TY = 4
TZ = 2
CAPC = 2


epsilon = 1e-05


def passed_along(block, axis, distance):
    devices = range(lax.axis_size(axis))
    route = [(i - distance, i) for i in devices if i - distance in devices]
    return lax.ppermute(block, axis, route)


def moments(values, weights):
    local_count = jnp.sum(weights)
    local_mean = jnp.sum(values * weights, axis=1) / jnp.maximum(local_count, 1.0)
    centered = values - local_mean[:, None]
    local_square = jnp.sum(weights * centered * centered, axis=1)
    width = local_mean.shape[0]
    padded = 128 * ((2 * width + 1 + 127) // 128)
    row = jnp.concatenate(
        [local_mean, local_square, local_count[None], jnp.zeros(padded - 2 * width - 1, jnp.float32)]
    )
    devices = lax.axis_size("level") * lax.axis_size("space")
    table = lax.all_to_all(
        jnp.broadcast_to(row, (devices, padded)), ("level", "space"), 0, 0, tiled=True
    )
    means = table[:, :width]
    counts = table[:, 2 * width][:, None]
    total_count = jnp.sum(counts)
    mean = jnp.sum(means * counts, axis=0) / total_count
    square = jnp.sum(table[:, width : 2 * width] + counts * (means - mean) ** 2, axis=0)
    return (mean, square / total_count)


def edge_range(step, length, width):
    if step == -1:
        return slice(length - width, length)
    if step == 1:
        return slice(0, width)
    return slice(0, length)


def rim_range(step, length):
    if step == -1:
        return slice(0, 1)
    if step == 1:
        return slice(length + 1, length + 2)
    return slice(1, length + 1)


def shards(
    features,
    occupancy,
    brick_coords,
    coarse_owner,
    conv_weight,
    conv_gain,
    conv_shift,
    reduce_weight,
    down_gain,
    down_shift,
):
    space_count = lax.axis_size("space")
    grid_y = min(4, space_count // 4)
    grid_x = space_count // grid_y
    space_place = lax.axis_index("space")
    tile_x = space_place // grid_y
    tile_y = space_place % grid_y
    bricks_here, depth, cells = features.shape
    size_x, size_y, size_z = (TX * BRICK, TY * BRICK, TZ * BRICK)
    position = (brick_coords[0] % TX * TY + brick_coords[1] % TY) * TZ + brick_coords[2]
    slots = jnp.arange(bricks_here, dtype=jnp.int32)
    chooser = (position[None, :] == slots[:, None]).astype(jnp.int32)
    slot_of = jnp.sum(chooser * slots[None, :], axis=1)
    gate = occupancy.astype(jnp.bfloat16)
    active_rows = (features * gate[:, None, :])[slot_of]
    gate_rows = occupancy.astype(jnp.float32)[slot_of]
    active = (
        active_rows.reshape(TX, TY, TZ, depth, BRICK, BRICK, BRICK)
        .transpose(3, 0, 4, 1, 5, 2, 6)
        .reshape(depth, size_x, size_y, size_z)
    )
    region_mask = (
        gate_rows.reshape(TX, TY, TZ, BRICK, BRICK, BRICK)
        .transpose(0, 3, 1, 4, 2, 5)
        .reshape(size_x, size_y, size_z)
    )
    padded_grid = jnp.pad(active, ((0, 0), (1, 1), (1, 1), (1, 1)))
    for step_x, step_y in ((-1, -1), (-1, 0), (-1, 1), (0, -1), (0, 1), (1, -1), (1, 0), (1, 1)):
        inside = (
            (tile_x + step_x >= 0)
            & (tile_x + step_x < grid_x)
            & (tile_y + step_y >= 0)
            & (tile_y + step_y < grid_y)
        )
        offset = -(step_x * grid_y + step_y)
        piece = active[:, edge_range(step_x, size_x, 1), edge_range(step_y, size_y, 1)]
        arrived = passed_along(piece, "space", offset)
        arrived = jnp.where(inside, arrived, jnp.zeros_like(arrived))
        padded_grid = padded_grid.at[
            :, rim_range(step_x, size_x), rim_range(step_y, size_y), 1 : size_z + 1
        ].set(arrived)
    total = jnp.zeros((depth, size_x * size_y * size_z), jnp.float32)
    for pair_index in range(9):
        shift_a, shift_b = (pair_index // 3, pair_index % 3)
        column = padded_grid[:, shift_a : shift_a + size_x, shift_b : shift_b + size_y, :]
        stacked = jnp.concatenate(
            [
                column[:, :, :, shift_c : shift_c + size_z].reshape(depth, -1)
                for shift_c in range(3)
            ],
            axis=0,
        )
        taps = conv_weight[3 * pair_index : 3 * pair_index + 3]
        joined = taps.transpose(1, 0, 2).reshape(taps.shape[1], -1)
        total = total + jnp.dot(joined, stacked, preferred_element_type=jnp.float32)
    flat_mask = region_mask.reshape(-1)
    conv_out = total * flat_mask
    mean1, var1 = moments(conv_out, flat_mask)
    first_scale = conv_gain / jnp.sqrt(var1 + epsilon)
    normed = (conv_out - mean1[:, None]) * first_scale[:, None] + conv_shift[:, None]
    brick_section = (
        active.reshape(depth, -1).astype(jnp.float32) + flat_mask * jnp.maximum(normed, 0.0)
    ).astype(jnp.bfloat16)
    split_view = brick_section.reshape(depth, size_x // 2, 2, size_y // 2, 2, size_z // 2, 2)
    wide = reduce_weight.shape[1]
    down_total = jnp.zeros((wide, size_x // 2 * (size_y // 2) * (size_z // 2)), jnp.float32)
    for offset_index in range(8):
        off_a, off_b, off_c = (offset_index // 4, offset_index // 2 % 2, offset_index % 2)
        window = split_view[:, :, off_a, :, off_b, :, off_c].reshape(depth, -1)
        down_total = down_total + jnp.dot(
            reduce_weight[offset_index], window, preferred_element_type=jnp.float32
        )
    down = down_total.astype(jnp.bfloat16)
    coarse_mask = region_mask.reshape(size_x // 2, 2, size_y // 2, 2, size_z // 2, 2).max(
        axis=(1, 3, 5)
    )
    blocks_x, blocks_y, blocks_z = (TX // 2, TY // 2, TZ // 2)
    coarse_rows = (
        down.reshape(wide, blocks_x, BRICK, blocks_y, BRICK, blocks_z, BRICK)
        .transpose(1, 3, 5, 0, 2, 4, 6)
        .reshape(-1, wide, cells)
    )
    mask_rows = (
        coarse_mask.reshape(blocks_x, BRICK, blocks_y, BRICK, blocks_z, BRICK)
        .transpose(0, 2, 4, 1, 3, 5)
        .reshape(-1, cells)
    )
    owners = coarse_owner[:, 0]
    quarter = jnp.arange(owners.shape[0], dtype=jnp.int32)
    earlier = (quarter[None, :] < quarter[:, None]) & (owners[None, :] == owners[:, None])
    ranks = jnp.sum(earlier.astype(jnp.int32), axis=1)
    groups = lax.axis_size("level")
    selector = (
        (owners[None, None, :] == jnp.arange(groups, dtype=jnp.int32)[:, None, None])
        & (ranks[None, None, :] == jnp.arange(CAPC, dtype=jnp.int32)[None, :, None])
    ).astype(jnp.bfloat16)
    sent = jnp.where(mask_rows[:, None, :] > 0, coarse_rows, -jnp.inf)
    gathered = lax.all_gather(sent, "level")
    choosers = lax.all_gather(selector, "level")
    mean2, var2 = moments(down.astype(jnp.float32), coarse_mask.reshape(-1))
    scale2 = down_gain / jnp.sqrt(var2 + epsilon)
    chooser = lax.dynamic_index_in_dim(choosers, lax.axis_index("level"), 1, keepdims=False)
    slot = jnp.argmax(chooser, axis=2)
    filled = jnp.max(chooser, axis=2) > 0
    rows = jnp.take_along_axis(gathered, slot[:, :, None, None], axis=1)
    normed2 = (rows.astype(jnp.float32) - mean2[None, None, :, None]) * scale2[
        None, None, :, None
    ] + down_shift[None, None, :, None]
    settled = jnp.where(filled[:, :, None, None], jnp.maximum(normed2, 0.0), 0.0)
    return settled.reshape(-1, wide, cells).astype(jnp.bfloat16)


def solution(mesh):
    in_specs = (
        P(("level", "space"), None, None),
        P(("level", "space"), None),
        P(None, ("level", "space")),
        P(("level", "space"), None),
        P(),
        P(),
        P(),
        P(),
        P(),
        P(),
    )
    out_specs = P(("level", "space"), None, None)
    return jax.shard_map(shards, mesh=mesh, in_specs=in_specs, out_specs=out_specs, check_vma=False)
```

```python
import jax
import jax.numpy as jnp
import numpy as np
from jax import lax
from jax.experimental import pallas as pl
from jax.experimental.pallas import tpu as pltpu
from jax.sharding import PartitionSpec as P

BRICK = 8
TX = 2
TY = 4
TZ = 2
CAPC = 2
C = 96
C2 = 192
LANES = 128
SX = TX * BRICK
SY = TY * BRICK
SZ = TZ * BRICK
PAIRS = SY // 2
GRID_Y = 4
EMPTY = -3e38
epsilon = 1e-05

bf16 = jnp.bfloat16
f32 = jnp.float32
VMEM = pl.BlockSpec(memory_space=pltpu.VMEM)
SMEM = pl.BlockSpec(memory_space=pltpu.SMEM)


def params(mib=56):
    return pltpu.CompilerParams(vmem_limit_bytes=mib << 20)


def cell_chooser():
    chosen = np.zeros((256, 256), np.float32)
    for row in range(256):
        i2, j, c, half = row >> 7, (row >> 4) & 7, (row >> 3) & 1, row & 7
        z = 2 * half + c
        chosen[row, (z // 8) * 128 + i2 * 64 + j * 8 + z % 8] = 1
    return jnp.asarray(chosen, bf16)


def rows_dot(left, right):
    return lax.dot_general(left, right, (((1,), (1,)), ((), ())), preferred_element_type=f32)


def plain_dot(left, right):
    return lax.dot_general(left, right, (((1,), (0,)), ((), ())), preferred_element_type=f32)


def pack_kernel(coords, features, occupancy, chooser, act, x_low, x_high, y_low, y_high, order):
    for n in range(16):
        place = ((coords[0, n] % TX) * TY + coords[1, n] % TY) * TZ + coords[2, n]
        order[place] = n
    zero_column = jnp.zeros((SX, SZ, LANES), bf16)
    act[:, 0, 0] = zero_column
    act[:, PAIRS, 1] = zero_column
    picks = chooser[...]
    for tx in range(TX):
        for ty in range(TY):
            halves = []
            for tz in range(TZ):
                n = order[(tx * TY + ty) * TZ + tz]
                gate = occupancy[pl.ds(n, 1), :].astype(f32)
                gate = jnp.broadcast_to(gate, (LANES, 512)).astype(bf16)
                halves.append(jnp.concatenate([features[n] * gate[:C], gate[C:]], axis=0))
            for h in range(4):
                lanes = slice(128 * h, 128 * h + 128)
                source = jnp.concatenate([half[:, lanes] for half in halves], axis=1)
                cells = rows_dot(picks, source).reshape(2, 4, 2, SZ, LANES).astype(bf16)
                x = 8 * tx + 2 * h
                act[x : x + 2, 4 * ty : 4 * ty + 4, 1] = cells[:, :, 0]
                act[x : x + 2, 4 * ty + 1 : 4 * ty + 5, 0] = cells[:, :, 1]
    x_low[...] = act[0]
    x_high[...] = act[SX - 1]
    y_low[...] = act[:, 0, 1]
    y_high[...] = act[:, PAIRS, 0]


def pack(coords, features, occupancy):
    face = jax.ShapeDtypeStruct((PAIRS + 1, 2, SZ, LANES), bf16)
    side = jax.ShapeDtypeStruct((SX, SZ, LANES), bf16)
    return pl.pallas_call(
        pack_kernel,
        out_shape=(
            jax.ShapeDtypeStruct((SX, PAIRS + 1, 2, SZ, LANES), bf16),
            face,
            face,
            side,
            side,
        ),
        in_specs=[SMEM, VMEM, VMEM, VMEM],
        out_specs=(VMEM,) * 5,
        scratch_shapes=[pltpu.SMEM((16,), jnp.int32)],
        compiler_params=params(),
        name="pack",
    )(coords, features, occupancy, cell_chooser())


def z_shifted(cells):
    shape = cells.shape[:-2]
    wide = cells.astype(f32).reshape(-1, 2, 8, LANES)
    even, odd = wide[:, 0], wide[:, 1]
    place = lax.broadcasted_iota(jnp.int32, odd.shape, 1)
    before = jnp.where(place == 0, 0.0, pltpu.roll(odd, 1, 1))
    after = jnp.where(place == 7, 0.0, pltpu.roll(even, 7, 1))
    low = jnp.stack([before, even], axis=1).reshape(*shape, SZ, LANES).astype(bf16)
    high = jnp.stack([odd, after], axis=1).reshape(*shape, SZ, LANES).astype(bf16)
    return low, high


def lane_spread():
    row = lax.broadcasted_iota(jnp.int32, (LANES, LANES), 0)
    return jnp.where(row == LANES - 1, 1.0, 0.0).astype(bf16)


def conv_kernel(act, x_low, x_high, y_low, y_high, weight, out, stats, grid, taps, masks):
    space = lax.axis_index("space")
    tile_x, tile_y = space // GRID_Y, space % GRID_Y
    last_x = lax.axis_size("space") // GRID_Y - 1

    def kept(value, inside):
        return value * jnp.where(inside, 1.0, 0.0).astype(bf16)

    def place(x, plane):
        low, high = z_shifted(plane)
        grid[0, x] = low
        grid[1, x] = plane
        grid[2, x] = high

    place(0, kept(x_low[...], tile_x > 0))
    place(SX + 1, kept(x_high[...], tile_x < last_x))

    def fill(x, carry):
        place(x + 1, act[x])
        return carry

    lax.fori_loop(0, SX, fill, 0)
    for c, side in zip((0, 1, 2), (z_shifted(y_low[...])[0], y_low[...], z_shifted(y_low[...])[1])):
        grid[c, 1 : SX + 1, 0, 0] = kept(side, tile_y > 0)
    for c, side in zip((0, 1, 2), (z_shifted(y_high[...])[0], y_high[...], z_shifted(y_high[...])[1])):
        grid[c, 1 : SX + 1, PAIRS, 1] = kept(side, tile_y < GRID_Y - 1)
    taps[...] = jnp.zeros(taps.shape, bf16)
    for a in range(3):
        for b in range(3):
            for c in range(3):
                for parity in range(2):
                    first = (a * 3 + c) * 512 + (b + parity) * LANES
                    taps[first : first + C, parity * LANES : parity * LANES + C] = weight[(a * 3 + b) * 3 + c].T

    def convolve(x, carry):
        total, count = carry
        pieces = []
        for a in range(3):
            for c in range(3):
                for d in range(4):
                    rows = grid[c, x + a, d // 2 : d // 2 + PAIRS, d % 2]
                    pieces.append(rows.reshape(PAIRS * SZ, LANES))
        value = plain_dot(jnp.concatenate(pieces, axis=1), taps[...])
        spread = lane_spread()
        even = grid[1, x + 1, 0:PAIRS, 1].reshape(PAIRS * SZ, LANES)
        odd = grid[1, x + 1, 1 : PAIRS + 1, 0].reshape(PAIRS * SZ, LANES)
        mask = jnp.concatenate([plain_dot(even, spread), plain_dot(odd, spread)], axis=1)
        masks[x] = mask.astype(bf16)
        out[x] = value
        total = total + jnp.sum(value * mask, axis=0, keepdims=True)
        return total, count + jnp.sum(mask, axis=0, keepdims=True)

    zero = jnp.zeros((1, 2 * LANES), f32)
    total, count = lax.fori_loop(0, SX, convolve, (zero, zero))
    total = total[:, :LANES] + total[:, LANES:]
    count = count[:, :LANES] + count[:, LANES:]
    mean = total / jnp.maximum(count, 1.0)
    both = jnp.concatenate([mean, mean], axis=1)

    def spread_out(x, carry):
        gap = (out[x] - both) * masks[x].astype(f32)
        return carry + jnp.sum(gap * gap, axis=0, keepdims=True)

    square = lax.fori_loop(0, SX, spread_out, zero)
    square = square[:, :LANES] + square[:, LANES:]
    lane = lax.broadcasted_iota(jnp.int32, (1, LANES), 1)
    row = jnp.concatenate([jnp.where(lane == LANES - 1, count, mean), square], axis=1)
    stats[...] = jnp.broadcast_to(row, stats.shape)


def convolution(act, x_low, x_high, y_low, y_high, weight, devices):
    return pl.pallas_call(
        conv_kernel,
        out_shape=(
            jax.ShapeDtypeStruct((SX, PAIRS * SZ, 2 * LANES), f32),
            jax.ShapeDtypeStruct((devices, 2 * LANES), f32),
        ),
        in_specs=[VMEM] * 6,
        out_specs=(VMEM, VMEM),
        scratch_shapes=[
            pltpu.VMEM((3, SX + 2, PAIRS + 1, 2, SZ, LANES), bf16),
            pltpu.VMEM((9 * 512, 2 * LANES), bf16),
            pltpu.VMEM((SX, PAIRS * SZ, 2 * LANES), bf16),
        ],
        compiler_params=params(),
        name="conv",
    )(act, x_low, x_high, y_low, y_high, weight)


def padded_row(values):
    return jnp.pad(values, (0, LANES - values.shape[0]))[None]


def section_kernel(conv, act, table, gain, shift, weight, owners, sent, stats, taps, down, cover):
    means, squares = table[:, :LANES], table[:, LANES:]
    counts = table[:, LANES - 1 : LANES]
    whole = jnp.sum(counts, axis=0, keepdims=True)
    mean = jnp.sum(means * counts, axis=0, keepdims=True) / whole
    var = jnp.sum(squares + counts * (means - mean) ** 2, axis=0, keepdims=True) / whole
    lane = lax.broadcasted_iota(jnp.int32, (1, LANES), 1)
    scale = jnp.where(lane < C, gain[...] / jnp.sqrt(var + epsilon), 0.0)
    mean = jnp.where(lane < C, mean, 0.0)
    mean = jnp.concatenate([mean, mean], axis=1)
    scale = jnp.concatenate([scale, scale], axis=1)
    moved = jnp.concatenate([shift[...], shift[...]], axis=1)
    taps[...] = jnp.zeros(taps.shape, bf16)
    for a in range(2):
        for b in range(2):
            for c in range(2):
                first = ((a * 2 + c) * 2 + b) * LANES
                taps[:C2, first : first + C] = weight[(a * 2 + b) * 2 + c]

    def reduce_plane(X, carry):
        total, count = carry
        pieces, covers = [], []
        spread = lane_spread()
        for a in range(2):
            x = 2 * X + a
            even = act[x, 0:PAIRS, 1].reshape(PAIRS * SZ, LANES)
            odd = act[x, 1 : PAIRS + 1, 0].reshape(PAIRS * SZ, LANES)
            even_mask, odd_mask = plain_dot(even, spread), plain_dot(odd, spread)
            mask = jnp.concatenate([even_mask, odd_mask], axis=1)
            active = jnp.concatenate([even, odd], axis=1).astype(f32)
            normed = (conv[x] - mean) * scale + moved
            section = active + mask * jnp.maximum(normed, 0.0)
            section = section.reshape(PAIRS, 2, 8, 2 * LANES)
            for c in range(2):
                pieces.append(section[:, c].reshape(PAIRS * 8, 2 * LANES).astype(bf16))
            both = jnp.maximum(even_mask, odd_mask).reshape(PAIRS, 2, 8, LANES)
            covers.append(jnp.maximum(both[:, 0], both[:, 1]).reshape(PAIRS * 8, LANES))
        value = rows_dot(jnp.concatenate(pieces, axis=1), taps[...])
        value = value.astype(bf16).astype(f32)
        covered = jnp.maximum(covers[0], covers[1])
        covered = jnp.concatenate([covered, covered], axis=1)
        down[X] = value
        cover[X] = covered
        total = total + jnp.sum(value * covered, axis=0, keepdims=True)
        return total, count + jnp.sum(covered, axis=0, keepdims=True)

    zero = jnp.zeros((1, 2 * LANES), f32)
    total, count = lax.fori_loop(0, SX // 2, reduce_plane, (zero, zero))
    mean2 = total / jnp.maximum(count, 1.0)

    def spread_out(X, carry):
        gap = (down[X] - mean2) * cover[X]
        return carry + jnp.sum(gap * gap, axis=0, keepdims=True)

    square = lax.fori_loop(0, SX // 2, spread_out, zero)
    wide_lane = lax.broadcasted_iota(jnp.int32, (1, 2 * LANES), 1)
    row = jnp.concatenate([jnp.where(wide_lane == 2 * LANES - 1, count, mean2), square], axis=1)
    stats[...] = jnp.broadcast_to(row, stats.shape)

    level = lax.axis_index("level")
    groups = lax.axis_size("level")
    unit = (
        lax.broadcasted_iota(jnp.int32, (C2, 2 * LANES), 0)
        == lax.broadcasted_iota(jnp.int32, (C2, 2 * LANES), 1)
    )
    unit = jnp.where(unit, 1.0, 0.0).astype(bf16)
    half = PAIRS // 2 * 8
    rows = []
    for q in range(2):
        value = down[:, q * half : (q + 1) * half].reshape(SX // 2 * half, 2 * LANES)
        covered = cover[:, q * half : (q + 1) * half].reshape(SX // 2 * half, 2 * LANES)
        coded = jnp.where(covered > 0, value, EMPTY).astype(bf16)
        rows.append(rows_dot(unit, coded).astype(bf16))
    first, second = owners[0, 0], owners[1, 0]
    for distance in range(4):
        target = (level + distance) % groups
        for k in range(CAPC):
            takes_first = (first == target) & (k == 0)
            takes_second = (second == target) & (jnp.where(first == second, 1, 0) == k)
            chosen = jnp.where(takes_first, rows[0], jnp.where(takes_second, rows[1], EMPTY))
            sent[distance, k] = chosen.astype(bf16)


def section(conv, act, table, gain, shift, weight, owners):
    return pl.pallas_call(
        section_kernel,
        out_shape=(
            jax.ShapeDtypeStruct((4, CAPC, C2, 512), bf16),
            jax.ShapeDtypeStruct((table.shape[0], 4 * LANES), f32),
        ),
        in_specs=[VMEM] * 6 + [SMEM],
        out_specs=(VMEM, VMEM),
        scratch_shapes=[
            pltpu.VMEM((2 * LANES, 8 * LANES), bf16),
            pltpu.VMEM((SX // 2, PAIRS * 8, 2 * LANES), f32),
            pltpu.VMEM((SX // 2, PAIRS * 8, 2 * LANES), f32),
        ],
        compiler_params=params(),
        name="section",
    )(conv, act, table, gain, shift, weight, owners)


def settle_kernel(own, near, far, back, table, gain, shift, out):
    turned = table[...].T
    means, squares = turned[:C2], turned[2 * LANES : 2 * LANES + C2]
    counts = turned[2 * LANES - 1 : 2 * LANES]
    whole = jnp.sum(counts, axis=1, keepdims=True)
    mean = jnp.sum(means * counts, axis=1, keepdims=True) / whole
    var = jnp.sum(squares + counts * (means - mean) ** 2, axis=1, keepdims=True) / whole
    scale = gain[...] / jnp.sqrt(var + epsilon)
    moved = shift[...]
    level = lax.axis_index("level")
    groups = lax.axis_size("level")
    for distance, source in enumerate((own, near, far, back)):
        origin = (level + groups - distance) % groups
        for k in range(CAPC):
            value = source[k].astype(f32)
            normed = (value - mean) * scale + moved
            out[origin * CAPC + k] = jnp.maximum(normed, 0.0).astype(bf16)


def settle(own, near, far, back, table, gain, shift):
    return pl.pallas_call(
        settle_kernel,
        out_shape=jax.ShapeDtypeStruct((8, C2, 512), bf16),
        in_specs=[VMEM] * 7,
        out_specs=VMEM,
        compiler_params=params(),
        name="settle",
    )(own, near, far, back, table, gain, shift)


def to_all(rows):
    return lax.all_to_all(rows, ("level", "space"), 0, 0, tiled=True)


def shards(
    features,
    occupancy,
    brick_coords,
    coarse_owner,
    conv_weight,
    conv_gain,
    conv_shift,
    reduce_weight,
    down_gain,
    down_shift,
):
    space_count = lax.axis_size("space")
    level_count = lax.axis_size("level")
    grid_x = space_count // GRID_Y

    def from_tile(block, step_x, step_y):
        route = []
        for s in range(space_count):
            x, y = s // GRID_Y, s % GRID_Y
            route.append(((x + step_x) % grid_x * GRID_Y + (y + step_y) % GRID_Y, s))
        return lax.ppermute(block, "space", route)

    act, x_low, x_high, y_low, y_high = pack(brick_coords, features, occupancy)
    y_before = from_tile(y_high, 0, -1)
    y_after = from_tile(y_low, 0, 1)
    tile_y = lax.axis_index("space") % GRID_Y
    for_low = (y_before * (tile_y > 0).astype(bf16), y_after * (tile_y < GRID_Y - 1).astype(bf16))

    def with_corners(face, x):
        face = face.at[0, 0].set(for_low[0][x])
        return face.at[PAIRS, 1].set(for_low[1][x])

    x_before = from_tile(with_corners(x_high, SX - 1), -1, 0)
    x_after = from_tile(with_corners(x_low, 0), 1, 0)
    conv, stats = convolution(
        act, x_before, x_after, y_before, y_after, conv_weight, space_count * level_count
    )
    sent, stats2 = section(
        conv,
        act,
        to_all(stats),
        padded_row(conv_gain),
        padded_row(conv_shift),
        reduce_weight,
        coarse_owner,
    )
    arrived = [
        lax.ppermute(sent[d], "level", [(g, (g + d) % level_count) for g in range(level_count)])
        for d in range(1, level_count)
    ]
    return settle(
        sent[0], *arrived, to_all(stats2), down_gain[:, None], down_shift[:, None]
    )


def solution(mesh):
    in_specs = (
        P(("level", "space"), None, None),
        P(("level", "space"), None),
        P(None, ("level", "space")),
        P(("level", "space"), None),
        P(),
        P(),
        P(),
        P(),
        P(),
        P(),
    )
    out_specs = P(("level", "space"), None, None)
    return jax.shard_map(shards, mesh=mesh, in_specs=in_specs, out_specs=out_specs, check_vma=False)
```

```python
import functools

import jax
import jax.numpy as jnp
import numpy as np
from jax import lax
from jax.experimental import pallas as pl
from jax.experimental.pallas import tpu as pltpu
from jax.sharding import PartitionSpec as P

BRICK = 8
TX = 2
TY = 4
TZ = 2
CAPC = 2
C = 96
C2 = 192
LANES = 128
SX = TX * BRICK
SY = TY * BRICK
SZ = TZ * BRICK
PAIRS = SY // 2
GRID_Y = 4
EMPTY = -3e38
epsilon = 1e-05

bf16 = jnp.bfloat16
f32 = jnp.float32
VMEM = pl.BlockSpec(memory_space=pltpu.VMEM)
SMEM = pl.BlockSpec(memory_space=pltpu.SMEM)


def params(mib=56):
    return pltpu.CompilerParams(vmem_limit_bytes=mib << 20)


def cell_chooser():
    chosen = np.zeros((256, 256), np.float32)
    for row in range(256):
        i2, j, c, half = row >> 7, (row >> 4) & 7, (row >> 3) & 1, row & 7
        z = 2 * half + c
        chosen[row, (z // 8) * 128 + i2 * 64 + j * 8 + z % 8] = 1
    return jnp.asarray(chosen, bf16)


def rows_dot(left, right):
    return lax.dot_general(left, right, (((1,), (1,)), ((), ())), preferred_element_type=f32)


def plain_dot(left, right):
    return lax.dot_general(left, right, (((1,), (0,)), ((), ())), preferred_element_type=f32)


def pack_kernel(parts, coords, features, occupancy, chooser, act, *rest):
    faces, order = rest[:-1], rest[-1]
    for n in range(16):
        place = ((coords[0, n] % TX) * TY + coords[1, n] % TY) * TZ + coords[2, n]
        order[place] = n
    picks = chooser[...]
    for tx in range(TX):
        for part, ty in enumerate(parts):
            halves = []
            for tz in range(TZ):
                n = order[(tx * TY + ty) * TZ + tz]
                gate = occupancy[pl.ds(n, 1), :].astype(f32)
                gate = jnp.broadcast_to(gate, (LANES, 512)).astype(bf16)
                halves.append(jnp.concatenate([features[n] * gate[:C], gate[C:]], axis=0))
            for h in range(4):
                lanes = slice(128 * h, 128 * h + 128)
                source = jnp.concatenate([half[:, lanes] for half in halves], axis=1)
                cells = rows_dot(picks, source).reshape(2, 4, 2, SZ, LANES).astype(bf16)
                x = 8 * tx + 2 * h
                act[x : x + 2, part] = cells
                if faces and ty == 0:
                    faces[0][x : x + 2] = cells[:, 0, 0]
                if faces and ty == TY - 1:
                    faces[1][x : x + 2] = cells[:, 3, 1]


def pack(coords, features, occupancy, chooser, parts, with_faces):
    side = jax.ShapeDtypeStruct((SX, SZ, LANES), bf16)
    faces = (side, side) if with_faces else ()
    return pl.pallas_call(
        functools.partial(pack_kernel, parts),
        out_shape=(jax.ShapeDtypeStruct((SX, len(parts), 4, 2, SZ, LANES), bf16),) + faces,
        in_specs=[SMEM, VMEM, VMEM, VMEM],
        out_specs=(VMEM,) * (1 + len(faces)),
        scratch_shapes=[pltpu.SMEM((16,), jnp.int32)],
        compiler_params=params(12),
        name="pack",
    )(coords, features, occupancy, chooser)


def z_shifted(cells):
    shape = cells.shape[:-2]
    wide = cells.astype(f32).reshape(-1, 2, 8, LANES)
    even, odd = wide[:, 0], wide[:, 1]
    place = lax.broadcasted_iota(jnp.int32, odd.shape, 1)
    before = jnp.where(place == 0, 0.0, pltpu.roll(odd, 1, 1))
    after = jnp.where(place == 7, 0.0, pltpu.roll(even, 7, 1))
    low = jnp.stack([before, even], axis=1).reshape(*shape, SZ, LANES).astype(bf16)
    high = jnp.stack([odd, after], axis=1).reshape(*shape, SZ, LANES).astype(bf16)
    return low, high


def lane_spread():
    row = lax.broadcasted_iota(jnp.int32, (LANES, LANES), 0)
    return jnp.where(row == LANES - 1, 1.0, 0.0).astype(bf16)


def plane_of(outer, inner, x):
    return jnp.concatenate([outer[x, 0], inner[x, 0], inner[x, 1], outer[x, 1]], axis=0)


def put_columns(grid, slot, before, plane, after):
    for c, (first, middle, last) in enumerate(
        zip(z_triple(before), z_triple(plane), z_triple(after))
    ):
        grid[c, slot, 0, 0] = first
        grid[c, slot, 0:PAIRS, 1] = middle[:, 0]
        grid[c, slot, 1 : PAIRS + 1, 0] = middle[:, 1]
        grid[c, slot, PAIRS, 1] = last


def z_triple(cells):
    low, high = z_shifted(cells)
    return low, cells, high


def kept(value, inside):
    return value * jnp.where(inside, 1.0, 0.0).astype(bf16)


def planes_dot(grid, slot, count, taps):
    rows = count * PAIRS * SZ
    pieces = []
    for a in range(3):
        for c in range(3):
            for d in range(4):
                block = grid[c, pl.ds(slot + a, count), d // 2 : d // 2 + PAIRS, d % 2]
                pieces.append(block.reshape(rows, LANES))
    return plain_dot(jnp.concatenate(pieces, axis=1), taps[...])


def planes_mask(grid, slot, count):
    rows = count * PAIRS * SZ
    spread = lane_spread()
    even = grid[1, pl.ds(slot + 1, count), 0:PAIRS, 1].reshape(rows, LANES)
    odd = grid[1, pl.ds(slot + 1, count), 1 : PAIRS + 1, 0].reshape(rows, LANES)
    return jnp.concatenate([plain_dot(even, spread), plain_dot(odd, spread)], axis=1)


def folded(row):
    return row[:, :LANES] + row[:, LANES:]


MID = SX - 2
STEP = 2


def middle_kernel(outer, inner, y_before, y_after, weight, out, stats, taps, grid, masks):
    tile_y = lax.axis_index("space") % GRID_Y

    def fill(x, carry):
        before = kept(y_before[x], tile_y > 0)
        after = kept(y_after[x], tile_y < GRID_Y - 1)
        put_columns(grid, x, before, plane_of(outer, inner, x), after)
        return carry

    lax.fori_loop(0, SX, fill, 0)
    taps[...] = jnp.zeros(taps.shape, bf16)
    for a in range(3):
        for b in range(3):
            for c in range(3):
                for parity in range(2):
                    first = (a * 3 + c) * 512 + (b + parity) * LANES
                    taps[first : first + C, parity * LANES : parity * LANES + C] = weight[(a * 3 + b) * 3 + c].T

    def convolve(step, carry):
        total, count = carry
        x = step * STEP
        value = planes_dot(grid, x, STEP, taps)
        mask = planes_mask(grid, x, STEP)
        out[pl.ds(x, STEP)] = value.reshape(STEP, PAIRS * SZ, 2 * LANES)
        masks[pl.ds(x, STEP)] = mask.astype(bf16).reshape(STEP, PAIRS * SZ, 2 * LANES)
        total = total + jnp.sum(value * mask, axis=0, keepdims=True)
        return total, count + jnp.sum(mask, axis=0, keepdims=True)

    zero = jnp.zeros((1, 2 * LANES), f32)
    total, count = lax.fori_loop(0, MID // STEP, convolve, (zero, zero))
    count = folded(count)
    mean = folded(total) / jnp.maximum(count, 1.0)
    both = jnp.concatenate([mean, mean], axis=1)

    def spread_out(x, carry):
        gap = (out[x] - both) * masks[x].astype(f32)
        return carry + jnp.sum(gap * gap, axis=0, keepdims=True)

    square = folded(lax.fori_loop(0, MID, spread_out, zero))
    stats[...] = jnp.concatenate([mean, square, count, jnp.zeros((5, LANES), f32)], axis=0)


def middle(outer, inner, y_before, y_after, weight):
    return pl.pallas_call(
        middle_kernel,
        out_shape=(
            jax.ShapeDtypeStruct((MID, PAIRS * SZ, 2 * LANES), f32),
            jax.ShapeDtypeStruct((8, LANES), f32),
            jax.ShapeDtypeStruct((9 * 512, 2 * LANES), bf16),
        ),
        in_specs=[VMEM] * 5,
        out_specs=(VMEM,) * 3,
        scratch_shapes=[
            pltpu.VMEM((3, SX, PAIRS + 1, 2, SZ, LANES), bf16),
            pltpu.VMEM((MID, PAIRS * SZ, 2 * LANES), bf16),
        ],
        compiler_params=params(26),
        name="middle",
    )(outer, inner, y_before, y_after, weight)


def edge_kernel(outer, inner, y_before, y_after, x_before, x_after, taps, part, out, stats, grid):
    space = lax.axis_index("space")
    tile_x, tile_y = space // GRID_Y, space % GRID_Y
    last_x = lax.axis_size("space") // GRID_Y - 1
    for slot, x in zip((1, 2, 3, 4), (0, 1, SX - 2, SX - 1)):
        before = kept(y_before[x], tile_y > 0)
        after = kept(y_after[x], tile_y < GRID_Y - 1)
        put_columns(grid, slot, before, plane_of(outer, inner, x), after)
    for slot, halo, inside in ((0, x_before, tile_x > 0), (5, x_after, tile_x < last_x)):
        for c, cells in enumerate(z_triple(kept(halo[...], inside))):
            grid[c, slot] = cells.reshape(PAIRS + 1, 2, SZ, LANES)
    values, masks = [], []
    for index, slot in enumerate((0, 3)):
        value = planes_dot(grid, slot, 1, taps)
        out[index] = value
        values.append(value)
        masks.append(planes_mask(grid, slot, 1))
    value, mask = jnp.concatenate(values, axis=0), jnp.concatenate(masks, axis=0)
    count = folded(jnp.sum(mask, axis=0, keepdims=True))
    mean = folded(jnp.sum(value * mask, axis=0, keepdims=True)) / jnp.maximum(count, 1.0)
    gap = (value - jnp.concatenate([mean, mean], axis=1)) * mask
    square = folded(jnp.sum(gap * gap, axis=0, keepdims=True))
    mean0, square0, count0 = part[0:1], part[1:2], part[2:3]
    both = count + count0
    joint = (mean * count + mean0 * count0) / jnp.maximum(both, 1.0)
    square = square + square0 + count * (mean - joint) ** 2 + count0 * (mean0 - joint) ** 2
    lane = lax.broadcasted_iota(jnp.int32, (1, LANES), 1)
    row = jnp.concatenate([jnp.where(lane == LANES - 1, both, joint), square], axis=1)
    stats[...] = jnp.broadcast_to(row[None], stats.shape)


def edges(outer, inner, y_before, y_after, x_before, x_after, taps, part, devices):
    return pl.pallas_call(
        edge_kernel,
        out_shape=(
            jax.ShapeDtypeStruct((2, PAIRS * SZ, 2 * LANES), f32),
            jax.ShapeDtypeStruct((devices, 1, 2 * LANES), f32),
        ),
        in_specs=[VMEM] * 8,
        out_specs=(VMEM, VMEM),
        scratch_shapes=[pltpu.VMEM((3, 6, PAIRS + 1, 2, SZ, LANES), bf16)],
        compiler_params=params(20),
        name="edges",
    )(outer, inner, y_before, y_after, x_before, x_after, taps, part)


def joined(table, width):
    means, squares = table[:, :, :width], table[:, :, width:]
    counts = table[:, :, width - 1 : width]
    whole = jnp.sum(counts, axis=0)
    mean = jnp.sum(means * counts, axis=0) / whole
    gap = means - mean[None]
    return mean, jnp.sum(squares + counts * gap * gap, axis=0) / whole


def section_kernel(mid, edge, outer, inner, table, gain, shift, weight, owners, *rest):
    sent, (stats, taps, down, cover, lines) = rest[:4], rest[4:]
    mean, var = joined(table, LANES)
    lines[...] = jnp.zeros(lines.shape, f32)
    lines[0:1, :C] = gain[...]
    lines[1:2, :C] = shift[...]
    real = lax.broadcasted_iota(jnp.int32, (1, LANES), 1) < C
    scale = jnp.where(real, lines[0:1] / jnp.sqrt(var + epsilon), 0.0)
    mean = jnp.where(real, mean, 0.0)
    moved = lines[1:2]
    mean = jnp.concatenate([mean, mean], axis=1)
    scale = jnp.concatenate([scale, scale], axis=1)
    moved = jnp.concatenate([moved, moved], axis=1)
    taps[...] = jnp.zeros(taps.shape, bf16)
    for a in range(2):
        for b in range(2):
            for c in range(2):
                first = ((a * 2 + c) * 2 + b) * LANES
                taps[:C2, first : first + C] = weight[(a * 2 + b) * 2 + c]

    spread = lane_spread()
    total = count = jnp.zeros((1, 2 * LANES), f32)
    for X in range(SX // 2):
        pieces, covers = [], []
        for a in range(2):
            x = 2 * X + a
            conv = edge[0] if x == 0 else edge[1] if x == SX - 1 else mid[x - 1]
            plane = plane_of(outer, inner, x)
            even = plane[:, 0].reshape(PAIRS * SZ, LANES)
            odd = plane[:, 1].reshape(PAIRS * SZ, LANES)
            even_mask, odd_mask = plain_dot(even, spread), plain_dot(odd, spread)
            mask = jnp.concatenate([even_mask, odd_mask], axis=1)
            active = jnp.concatenate([even, odd], axis=1).astype(f32)
            normed = (conv - mean) * scale + moved
            section = active + mask * jnp.maximum(normed, 0.0)
            section = section.reshape(PAIRS, 2, 8, 2 * LANES)
            for c in range(2):
                pieces.append(section[:, c].reshape(PAIRS * 8, 2 * LANES).astype(bf16))
            both = jnp.maximum(even_mask, odd_mask).reshape(PAIRS, 2, 8, LANES)
            covers.append(jnp.maximum(both[:, 0], both[:, 1]).reshape(PAIRS * 8, LANES))
        value = rows_dot(jnp.concatenate(pieces, axis=1), taps[...])
        value = value.astype(bf16).astype(f32)
        covered = jnp.maximum(covers[0], covers[1])
        covered = jnp.concatenate([covered, covered], axis=1)
        down[X] = value
        cover[X] = covered
        total = total + jnp.sum(value * covered, axis=0, keepdims=True)
        count = count + jnp.sum(covered, axis=0, keepdims=True)

    zero = jnp.zeros((1, 2 * LANES), f32)
    mean2 = total / jnp.maximum(count, 1.0)

    def spread_out(X, carry):
        gap = (down[X] - mean2) * cover[X]
        return carry + jnp.sum(gap * gap, axis=0, keepdims=True)

    square = lax.fori_loop(0, SX // 2, spread_out, zero)
    wide_lane = lax.broadcasted_iota(jnp.int32, (1, 2 * LANES), 1)
    row = jnp.concatenate([jnp.where(wide_lane == 2 * LANES - 1, count, mean2), square], axis=1)
    stats[...] = jnp.broadcast_to(row[None], stats.shape)

    level = lax.axis_index("level")
    groups = lax.axis_size("level")
    unit = (
        lax.broadcasted_iota(jnp.int32, (C2, 2 * LANES), 0)
        == lax.broadcasted_iota(jnp.int32, (C2, 2 * LANES), 1)
    )
    unit = jnp.where(unit, 1.0, 0.0).astype(bf16)
    half = PAIRS // 2 * 8
    rows = []
    for q in range(2):
        value = down[:, q * half : (q + 1) * half].reshape(SX // 2 * half, 2 * LANES)
        covered = cover[:, q * half : (q + 1) * half].reshape(SX // 2 * half, 2 * LANES)
        coded = jnp.where(covered > 0, value, EMPTY).astype(bf16)
        rows.append(rows_dot(unit, coded).astype(bf16))
    first, second = owners[0, 0], owners[1, 0]
    for distance in range(4):
        target = (level + distance) % groups
        for k in range(CAPC):
            takes_first = (first == target) & (k == 0)
            takes_second = (second == target) & (jnp.where(first == second, 1, 0) == k)
            chosen = jnp.where(takes_first, rows[0], jnp.where(takes_second, rows[1], EMPTY))
            sent[distance][k] = chosen.astype(bf16)


def section(mid, edge, outer, inner, table, gain, shift, weight, owners):
    return pl.pallas_call(
        section_kernel,
        out_shape=(jax.ShapeDtypeStruct((CAPC, C2, 512), bf16),) * 4
        + (jax.ShapeDtypeStruct((table.shape[0], 1, 4 * LANES), f32),),
        in_specs=[VMEM] * 8 + [SMEM],
        out_specs=(VMEM,) * 5,
        scratch_shapes=[
            pltpu.VMEM((2 * LANES, 8 * LANES), bf16),
            pltpu.VMEM((SX // 2, PAIRS * 8, 2 * LANES), f32),
            pltpu.VMEM((SX // 2, PAIRS * 8, 2 * LANES), f32),
            pltpu.VMEM((8, LANES), f32),
        ],
        compiler_params=params(20),
        name="section",
    )(mid, edge, outer, inner, table, gain, shift, weight, owners)


def settle_kernel(own, near, far, back, table, gain, shift, out, lines):
    lines[...] = jnp.zeros(lines.shape, f32)
    mean, var = joined(table, 2 * LANES)
    lines[0:1] = mean
    lines[1:2] = var
    lines[2:3, :C2] = gain[...]
    lines[3:4, :C2] = shift[...]
    turned = lines[...].T[:C2]
    mean, moved = turned[:, 0:1], turned[:, 3:4]
    scale = turned[:, 2:3] / jnp.sqrt(turned[:, 1:2] + epsilon)
    level = lax.axis_index("level")
    groups = lax.axis_size("level")
    for distance, source in enumerate((own, near, far, back)):
        origin = (level + groups - distance) % groups
        for k in range(CAPC):
            value = source[k].astype(f32)
            normed = (value - mean) * scale + moved
            out[origin * CAPC + k] = jnp.maximum(normed, 0.0).astype(bf16)


def settle(own, near, far, back, table, gain, shift):
    return pl.pallas_call(
        settle_kernel,
        out_shape=jax.ShapeDtypeStruct((8, C2, 512), bf16),
        in_specs=[VMEM] * 7,
        out_specs=VMEM,
        scratch_shapes=[pltpu.VMEM((8, 2 * LANES), f32)],
        compiler_params=params(12),
        name="settle",
    )(own, near, far, back, table, gain, shift)


def to_all(rows):
    return lax.all_to_all(rows, ("level", "space"), 0, 0, tiled=True)


def shards(
    features,
    occupancy,
    brick_coords,
    coarse_owner,
    conv_weight,
    conv_gain,
    conv_shift,
    reduce_weight,
    down_gain,
    down_shift,
):
    space_count = lax.axis_size("space")
    level_count = lax.axis_size("level")
    grid_x = space_count // GRID_Y

    def from_tile(block, step_x, step_y):
        route = []
        for s in range(space_count):
            x, y = s // GRID_Y, s % GRID_Y
            route.append(((x + step_x) % grid_x * GRID_Y + (y + step_y) % GRID_Y, s))
        return lax.ppermute(block, "space", route)

    chooser = cell_chooser()
    outer, y_low, y_high = pack(brick_coords, features, occupancy, chooser, (0, TY - 1), True)
    y_before = from_tile(y_high, 0, -1)
    y_after = from_tile(y_low, 0, 1)
    (inner,) = pack(brick_coords, features, occupancy, chooser, (1, 2), False)
    tile_y = lax.axis_index("space") % GRID_Y
    from_below = (tile_y > 0).astype(bf16)
    from_above = (tile_y < GRID_Y - 1).astype(bf16)

    def face(x):
        return jnp.concatenate(
            [
                (y_before[x] * from_below)[None],
                outer[x, 0].reshape(8, SZ, LANES),
                inner[x].reshape(16, SZ, LANES),
                outer[x, 1].reshape(8, SZ, LANES),
                (y_after[x] * from_above)[None],
            ]
        )

    x_before = from_tile(face(SX - 1), -1, 0)
    x_after = from_tile(face(0), 1, 0)
    mid, part, taps = middle(outer, inner, y_before, y_after, conv_weight)
    edge, stats = edges(
        outer,
        inner,
        y_before,
        y_after,
        x_before,
        x_after,
        taps,
        part,
        space_count * level_count,
    )
    *sent, stats2 = section(
        mid,
        edge,
        outer,
        inner,
        to_all(stats),
        conv_gain[None],
        conv_shift[None],
        reduce_weight,
        coarse_owner,
    )
    arrived = [
        lax.ppermute(sent[d], "level", [(g, (g + d) % level_count) for g in range(level_count)])
        for d in range(1, level_count)
    ]
    return settle(sent[0], *arrived, to_all(stats2), down_gain[None], down_shift[None])


def solution(mesh):
    in_specs = (
        P(("level", "space"), None, None),
        P(("level", "space"), None),
        P(None, ("level", "space")),
        P(("level", "space"), None),
        P(),
        P(),
        P(),
        P(),
        P(),
        P(),
    )
    out_specs = P(("level", "space"), None, None)
    return jax.shard_map(shards, mesh=mesh, in_specs=in_specs, out_specs=out_specs, check_vma=False)
```

```python
import functools

import jax
import jax.numpy as jnp
from jax import lax
from jax.experimental import pallas as pl
from jax.experimental.pallas import tpu as pltpu
from jax.sharding import PartitionSpec as P

BRICK = 8
TX = 2
TY = 4
TZ = 2
CAPC = 2
C = 96
C2 = 192
LANES = 128
SX = TX * BRICK
SY = TY * BRICK
SZ = TZ * BRICK
PAIRS = SY // 2
GRID_Y = 4
EMPTY = -3e38
epsilon = 1e-05

bf16 = jnp.bfloat16
f32 = jnp.float32
VMEM = pl.BlockSpec(memory_space=pltpu.VMEM)
SMEM = pl.BlockSpec(memory_space=pltpu.SMEM)
HBM = pl.BlockSpec(memory_space=pltpu.HBM)


def params(mib=56):
    return pltpu.CompilerParams(vmem_limit_bytes=mib << 20)


def cell_chooser():
    row = lax.broadcasted_iota(jnp.int32, (256, 256), 0)
    lane = lax.broadcasted_iota(jnp.int32, (256, 256), 1)
    z = 2 * (row & 7) + ((row >> 3) & 1)
    source = ((z >> 3) << 7) + ((row >> 4) << 3) + (z & 7)
    return jnp.where(source == lane, 1.0, 0.0).astype(bf16)


def rows_dot(left, right):
    return lax.dot_general(left, right, (((1,), (1,)), ((), ())), preferred_element_type=f32)


def plain_dot(left, right):
    return lax.dot_general(left, right, (((1,), (0,)), ((), ())), preferred_element_type=f32)


def pack_bricks(parts, coords, features, occupancy, act, faces, order):
    for n in range(16):
        place = ((coords[0, n] % TX) * TY + coords[1, n] % TY) * TZ + coords[2, n]
        order[place] = n
    picks = cell_chooser()
    for tx in range(TX):
        for part, ty in enumerate(parts):
            halves = []
            for tz in range(TZ):
                n = order[(tx * TY + ty) * TZ + tz]
                gate = occupancy[pl.ds(n, 1), :].astype(f32)
                gate = jnp.broadcast_to(gate, (LANES, 512)).astype(bf16)
                halves.append(jnp.concatenate([features[n] * gate[:C], gate[C:]], axis=0))
            for h in range(4):
                lanes = slice(128 * h, 128 * h + 128)
                source = jnp.concatenate([half[:, lanes] for half in halves], axis=1)
                cells = rows_dot(picks, source).reshape(2, 4, 2, SZ, LANES).astype(bf16)
                x = 8 * tx + 2 * h
                act[x : x + 2, part] = cells
                if faces and ty == 0:
                    faces[0][x : x + 2] = cells[:, 0, 0]
                if faces and ty == TY - 1:
                    faces[1][x : x + 2] = cells[:, 3, 1]


def outer_kernel(coords, features, occupancy, act, y_low, y_high, order, places, bricks, gates, sems):
    copies = [
        pltpu.make_async_copy(coords, places, sems.at[0]),
        pltpu.make_async_copy(occupancy, gates, sems.at[1]),
        pltpu.make_async_copy(features, bricks, sems.at[2]),
    ]
    for copy in copies:
        copy.start()
    for copy in copies:
        copy.wait()
    pack_bricks((0, TY - 1), places, bricks, gates, act, (y_low, y_high), order)


def inner_kernel(coords, features, occupancy, act, order):
    pack_bricks((1, 2), coords, features, occupancy, act, (), order)


ACT = jax.ShapeDtypeStruct((SX, 2, 4, 2, SZ, LANES), bf16)


def pack_outer(coords, features, occupancy):
    side = jax.ShapeDtypeStruct((SX, SZ, LANES), bf16)
    arrays = [pltpu.with_memory_space_constraint(a, pltpu.HBM) for a in (coords, features, occupancy)]
    return pl.pallas_call(
        outer_kernel,
        out_shape=(ACT, side, side),
        in_specs=[HBM] * 3,
        out_specs=(VMEM,) * 3,
        scratch_shapes=[
            pltpu.SMEM((16,), jnp.int32),
            pltpu.SMEM((3, 16), jnp.int32),
            pltpu.VMEM((16, C, 512), bf16),
            pltpu.VMEM((16, 512), jnp.int32),
            pltpu.SemaphoreType.DMA((3,)),
        ],
        compiler_params=params(12),
        name="pack_outer",
    )(*arrays)


def pack_inner(coords, features, occupancy):
    return pl.pallas_call(
        inner_kernel,
        out_shape=ACT,
        in_specs=[SMEM, VMEM, VMEM],
        out_specs=VMEM,
        scratch_shapes=[pltpu.SMEM((16,), jnp.int32)],
        compiler_params=params(12),
        name="pack_inner",
    )(coords, features, occupancy)


def face_kernel(outer, inner, y_before, y_after, low, high):
    tile_y = lax.axis_index("space") % GRID_Y
    for face, x in ((low, 0), (high, SX - 1)):
        face[0] = kept(y_before[x], tile_y > 0)
        face[1 : SY + 1] = plane_of(outer, inner, x).reshape(SY, SZ, LANES)
        face[SY + 1] = kept(y_after[x], tile_y < GRID_Y - 1)


def faces(outer, inner, y_before, y_after):
    face = jax.ShapeDtypeStruct((SY + 2, SZ, LANES), bf16)
    return pl.pallas_call(
        face_kernel,
        out_shape=(face, face),
        in_specs=[VMEM] * 4,
        out_specs=(VMEM, VMEM),
        compiler_params=params(8),
        name="faces",
    )(outer, inner, y_before, y_after)


def z_shifted(cells):
    shape = cells.shape[:-2]
    wide = cells.astype(f32).reshape(-1, 2, 8, LANES)
    even, odd = wide[:, 0], wide[:, 1]
    place = lax.broadcasted_iota(jnp.int32, odd.shape, 1)
    before = jnp.where(place == 0, 0.0, pltpu.roll(odd, 1, 1))
    after = jnp.where(place == 7, 0.0, pltpu.roll(even, 7, 1))
    low = jnp.stack([before, even], axis=1).reshape(*shape, SZ, LANES).astype(bf16)
    high = jnp.stack([odd, after], axis=1).reshape(*shape, SZ, LANES).astype(bf16)
    return low, high


def lane_spread():
    row = lax.broadcasted_iota(jnp.int32, (LANES, LANES), 0)
    return jnp.where(row == LANES - 1, 1.0, 0.0).astype(bf16)


def plane_of(outer, inner, x):
    return jnp.concatenate([outer[x, 0], inner[x, 0], inner[x, 1], outer[x, 1]], axis=0)


def put_columns(grid, slot, before, plane, after):
    for c, (first, middle, last) in enumerate(
        zip(z_triple(before), z_triple(plane), z_triple(after))
    ):
        grid[c, slot, 0, 0] = first
        grid[c, slot, 0:PAIRS, 1] = middle[:, 0]
        grid[c, slot, 1 : PAIRS + 1, 0] = middle[:, 1]
        grid[c, slot, PAIRS, 1] = last


def z_triple(cells):
    low, high = z_shifted(cells)
    return low, cells, high


def kept(value, inside):
    return value * jnp.where(inside, 1.0, 0.0).astype(bf16)


def planes_dot(grid, slot, count, taps):
    rows = count * PAIRS * SZ
    pieces = []
    for a in range(3):
        for c in range(3):
            for d in range(4):
                block = grid[c, pl.ds(slot + a, count), d // 2 : d // 2 + PAIRS, d % 2]
                pieces.append(block.reshape(rows, LANES))
    return plain_dot(jnp.concatenate(pieces, axis=1), taps[...])


def planes_mask(grid, slot, count):
    rows = count * PAIRS * SZ
    spread = lane_spread()
    even = grid[1, pl.ds(slot + 1, count), 0:PAIRS, 1].reshape(rows, LANES)
    odd = grid[1, pl.ds(slot + 1, count), 1 : PAIRS + 1, 0].reshape(rows, LANES)
    return jnp.concatenate([plain_dot(even, spread), plain_dot(odd, spread)], axis=1)


def folded(row):
    return row[:, :LANES] + row[:, LANES:]


MID = SX - 2
STEP = 2


def merged(first, second):
    (mean0, square0, count0), (mean1, square1, count1) = first, second
    count = count0 + count1
    mean = (mean0 * count0 + mean1 * count1) / jnp.maximum(count, 1.0)
    square = square0 + square1 + count0 * (mean0 - mean) ** 2 + count1 * (mean1 - mean) ** 2
    return mean, square, count


def moments_of(value, mask):
    count = folded(jnp.sum(mask, axis=0, keepdims=True))
    mean = folded(jnp.sum(value * mask, axis=0, keepdims=True)) / jnp.maximum(count, 1.0)
    gap = (value - jnp.concatenate([mean, mean], axis=1)) * mask
    return mean, folded(jnp.sum(gap * gap, axis=0, keepdims=True)), count


def middle_kernel(outer, inner, y_before, y_after, weight, out, stats, taps, grid):
    tile_y = lax.axis_index("space") % GRID_Y

    def fill(x):
        before = kept(y_before[x], tile_y > 0)
        after = kept(y_after[x], tile_y < GRID_Y - 1)
        put_columns(grid, x, before, plane_of(outer, inner, x), after)

    taps[...] = jnp.zeros(taps.shape, bf16)
    for a in range(3):
        for b in range(3):
            for c in range(3):
                for parity in range(2):
                    first = (a * 3 + c) * 512 + (b + parity) * LANES
                    taps[first : first + C, parity * LANES : parity * LANES + C] = weight[(a * 3 + b) * 3 + c].T
    for x in range(STEP + 2):
        fill(x)
    zero = jnp.zeros((1, LANES), f32)
    carry = (zero, zero, zero)
    for x in range(0, MID, STEP):
        for later in range(x + STEP + 2, min(x + 2 * STEP + 2, SX)):
            fill(later)
        value = planes_dot(grid, x, STEP, taps)
        out[x : x + STEP] = value.reshape(STEP, PAIRS * SZ, 2 * LANES)
        carry = merged(carry, moments_of(value, planes_mask(grid, x, STEP)))
    stats[...] = jnp.concatenate(list(carry) + [jnp.zeros((5, LANES), f32)], axis=0)


def middle(outer, inner, y_before, y_after, weight):
    return pl.pallas_call(
        middle_kernel,
        out_shape=(
            pltpu.VMEM((MID, PAIRS * SZ, 2 * LANES), f32),
            jax.ShapeDtypeStruct((8, LANES), f32),
            jax.ShapeDtypeStruct((9 * 512, 2 * LANES), bf16),
        ),
        in_specs=[VMEM] * 5,
        out_specs=(VMEM,) * 3,
        scratch_shapes=[pltpu.VMEM((3, SX, PAIRS + 1, 2, SZ, LANES), bf16)],
        compiler_params=params(24),
        name="middle",
    )(outer, inner, y_before, y_after, weight)


def edge_kernel(outer, inner, y_before, y_after, x_before, x_after, taps, part, owners, out, stats, grid):
    space = lax.axis_index("space")
    tile_x, tile_y = space // GRID_Y, space % GRID_Y
    last_x = lax.axis_size("space") // GRID_Y - 1
    for slot, x in zip((1, 2, 3, 4), (0, 1, SX - 2, SX - 1)):
        before = kept(y_before[x], tile_y > 0)
        after = kept(y_after[x], tile_y < GRID_Y - 1)
        put_columns(grid, slot, before, plane_of(outer, inner, x), after)
    for slot, halo, inside in ((0, x_before, tile_x > 0), (5, x_after, tile_x < last_x)):
        for c, cells in enumerate(z_triple(kept(halo[...], inside))):
            grid[c, slot] = cells.reshape(PAIRS + 1, 2, SZ, LANES)
    carry = (part[0:1], part[1:2], part[2:3])
    for index, slot in enumerate((0, 3)):
        value = planes_dot(grid, slot, 1, taps)
        out[index] = value
        carry = merged(carry, moments_of(value, planes_mask(grid, slot, 1)))
    joint, square, both = carry
    lane = lax.broadcasted_iota(jnp.int32, (1, LANES), 1)
    joint = jnp.where(lane == LANES - 1, both, joint)
    for q in range(2):
        joint = jnp.where(lane == C + q, owners[q, 0].astype(f32), joint)
    row = jnp.concatenate([joint, square], axis=1)
    stats[...] = jnp.broadcast_to(row[None], stats.shape)


def edges(outer, inner, y_before, y_after, x_before, x_after, taps, part, owners, devices):
    return pl.pallas_call(
        edge_kernel,
        out_shape=(
            jax.ShapeDtypeStruct((2, PAIRS * SZ, 2 * LANES), f32),
            jax.ShapeDtypeStruct((devices, 1, 2 * LANES), f32),
        ),
        in_specs=[VMEM] * 8 + [SMEM],
        out_specs=(VMEM, VMEM),
        scratch_shapes=[pltpu.VMEM((3, 6, PAIRS + 1, 2, SZ, LANES), bf16)],
        compiler_params=params(20),
        name="edges",
    )(outer, inner, y_before, y_after, x_before, x_after, taps, part, owners)


def joined(table, width):
    means, squares = table[:, :, :width], table[:, :, width:]
    counts = table[:, :, width - 1 : width]
    whole = jnp.sum(counts, axis=0)
    mean = jnp.sum(means * counts, axis=0) / whole
    gap = means - mean[None]
    return mean, jnp.sum(squares + counts * gap * gap, axis=0) / whole


def section_kernel(
    mid, edge, outer, inner, table, gain, shift, weight, sent, names, stats, taps, down, cover, lines
):
    level, groups = lax.axis_index("level"), lax.axis_size("level")
    for distance in range(4):
        origin = (level + groups - distance) % groups
        device = origin * lax.axis_size("space") + lax.axis_index("space")
        names[distance] = table[device][:, :LANES]
    mean, var = joined(table, LANES)
    lines[...] = jnp.zeros(lines.shape, f32)
    lines[0:1, :C] = gain[...]
    lines[1:2, :C] = shift[...]
    real = lax.broadcasted_iota(jnp.int32, (1, LANES), 1) < C
    scale = jnp.where(real, lines[0:1] / jnp.sqrt(var + epsilon), 0.0)
    mean = jnp.where(real, mean, 0.0)
    moved = lines[1:2]
    mean = jnp.concatenate([mean, mean], axis=1)
    scale = jnp.concatenate([scale, scale], axis=1)
    moved = jnp.concatenate([moved, moved], axis=1)
    taps[...] = jnp.zeros(taps.shape, bf16)
    for a in range(2):
        for b in range(2):
            for c in range(2):
                first = ((a * 2 + c) * 2 + b) * LANES
                taps[:C2, first : first + C] = weight[(a * 2 + b) * 2 + c]

    spread = lane_spread()
    total = count = jnp.zeros((1, 2 * LANES), f32)
    for X in range(SX // 2):
        pieces, covers = [], []
        for a in range(2):
            x = 2 * X + a
            conv = edge[0] if x == 0 else edge[1] if x == SX - 1 else mid[x - 1]
            plane = plane_of(outer, inner, x)
            even = plane[:, 0].reshape(PAIRS * SZ, LANES)
            odd = plane[:, 1].reshape(PAIRS * SZ, LANES)
            even_mask, odd_mask = plain_dot(even, spread), plain_dot(odd, spread)
            mask = jnp.concatenate([even_mask, odd_mask], axis=1)
            active = jnp.concatenate([even, odd], axis=1).astype(f32)
            normed = (conv - mean) * scale + moved
            section = active + mask * jnp.maximum(normed, 0.0)
            section = section.reshape(PAIRS, 2, 8, 2 * LANES)
            for c in range(2):
                pieces.append(section[:, c].reshape(PAIRS * 8, 2 * LANES).astype(bf16))
            both = jnp.maximum(even_mask, odd_mask).reshape(PAIRS, 2, 8, LANES)
            covers.append(jnp.maximum(both[:, 0], both[:, 1]).reshape(PAIRS * 8, LANES))
        value = rows_dot(jnp.concatenate(pieces, axis=1), taps[...])
        value = value.astype(bf16).astype(f32)
        covered = jnp.maximum(covers[0], covers[1])
        covered = jnp.concatenate([covered, covered], axis=1)
        down[X] = value
        cover[X] = covered
        total = total + jnp.sum(value * covered, axis=0, keepdims=True)
        count = count + jnp.sum(covered, axis=0, keepdims=True)

    zero = jnp.zeros((1, 2 * LANES), f32)
    mean2 = total / jnp.maximum(count, 1.0)

    def spread_out(X, carry):
        gap = (down[X] - mean2) * cover[X]
        return carry + jnp.sum(gap * gap, axis=0, keepdims=True)

    square = lax.fori_loop(0, SX // 2, spread_out, zero)
    wide_lane = lax.broadcasted_iota(jnp.int32, (1, 2 * LANES), 1)
    row = jnp.concatenate([jnp.where(wide_lane == 2 * LANES - 1, count, mean2), square], axis=1)
    stats[...] = jnp.broadcast_to(row[None], stats.shape)

    unit = (
        lax.broadcasted_iota(jnp.int32, (C2, 2 * LANES), 0)
        == lax.broadcasted_iota(jnp.int32, (C2, 2 * LANES), 1)
    )
    unit = jnp.where(unit, 1.0, 0.0).astype(bf16)
    half = PAIRS // 2 * 8
    for q in range(2):
        value = down[:, q * half : (q + 1) * half].reshape(SX // 2 * half, 2 * LANES)
        covered = cover[:, q * half : (q + 1) * half].reshape(SX // 2 * half, 2 * LANES)
        coded = jnp.where(covered > 0, value, EMPTY).astype(bf16)
        sent[q] = rows_dot(unit, coded).astype(bf16)


def section(mid, edge, outer, inner, table, gain, shift, weight, devices):
    return pl.pallas_call(
        section_kernel,
        out_shape=(
            jax.ShapeDtypeStruct((2, C2, 512), bf16),
            jax.ShapeDtypeStruct((4, 1, LANES), f32),
            jax.ShapeDtypeStruct((devices, 1, 4 * LANES), f32),
        ),
        in_specs=[VMEM] * 8,
        out_specs=(VMEM,) * 3,
        scratch_shapes=[
            pltpu.VMEM((2 * LANES, 8 * LANES), bf16),
            pltpu.VMEM((SX // 2, PAIRS * 8, 2 * LANES), f32),
            pltpu.VMEM((SX // 2, PAIRS * 8, 2 * LANES), f32),
            pltpu.VMEM((8, LANES), f32),
        ],
        compiler_params=params(20),
        name="section",
    )(mid, edge, outer, inner, table, gain, shift, weight)


def merge_kernel(table, out):
    width = 2 * LANES
    means, squares = table[:, :, :width], table[:, :, width:]
    counts = table[:, :, width - 1 : width]
    whole = jnp.sum(counts, axis=0)
    mean = jnp.sum(means * counts, axis=0) / jnp.maximum(whole, 1.0)
    gap = means - mean[None]
    square = jnp.sum(squares + counts * gap * gap, axis=0)
    lane = lax.broadcasted_iota(jnp.int32, (1, width), 1)
    out[:, :, :width] = jnp.where(lane == width - 1, whole, mean)[None]
    out[:, :, width:] = square[None]


def merge(table):
    return pl.pallas_call(
        merge_kernel,
        out_shape=jax.ShapeDtypeStruct((1, 1, 4 * LANES), f32),
        in_specs=[VMEM],
        out_specs=VMEM,
        compiler_params=params(4),
        name="merge",
    )(table)


def settle_kernel(
    own, near, far0, far1, back, names, row0, row1, row2, row3, gain, shift, out, lines, ready, sems
):
    lines[...] = jnp.zeros(lines.shape, f32)
    table = jnp.concatenate([row0[...], row1[...], row2[...], row3[...]], axis=0)
    mean, var = joined(table, 2 * LANES)
    lines[0:1] = mean
    lines[1:2] = var
    lines[2:3, :C2] = gain[...]
    lines[3:4, :C2] = shift[...]
    turned = lines[...].T[:C2]
    mean, moved = turned[:, 0:1], turned[:, 3:4]
    scale = turned[:, 2:3] / jnp.sqrt(turned[:, 1:2] + epsilon)
    level = lax.axis_index("level")
    groups = lax.axis_size("level")
    copies = []
    sources = ((own, 0, own, 1), (near, 0, near, 1), (far0, 0, far1, 0), (back, 0, back, 1))
    for distance, (first, first_at, second, second_at) in enumerate(sources):
        origin = (level + groups - distance) % groups
        named = jnp.where(names[distance] == level.astype(f32), 1.0, 0.0)
        takes0, takes1 = named[:, C : C + 1], named[:, C + 1 : C + 2]
        value0 = jnp.maximum((first[first_at].astype(f32) - mean) * scale + moved, 0.0)
        value1 = jnp.maximum((second[second_at].astype(f32) - mean) * scale + moved, 0.0)
        chosen = (
            jnp.where(takes0 > 0, value0, jnp.where(takes1 > 0, value1, 0.0)),
            jnp.where(takes0 * takes1 > 0, value1, 0.0),
        )
        for k in range(CAPC):
            slot = distance * CAPC + k
            ready[slot] = chosen[k].astype(bf16)
            copies.append(
                pltpu.make_async_copy(ready.at[slot], out.at[origin * CAPC + k], sems.at[slot])
            )
            copies[-1].start()
    for copy in copies:
        copy.wait()


def settle(rows, names, tables, gain, shift):
    return pl.pallas_call(
        settle_kernel,
        out_shape=jax.ShapeDtypeStruct((8, C2, 512), bf16),
        in_specs=[VMEM] * 12,
        out_specs=HBM,
        scratch_shapes=[
            pltpu.VMEM((8, 2 * LANES), f32),
            pltpu.VMEM((8, C2, 512), bf16),
            pltpu.SemaphoreType.DMA((8,)),
        ],
        compiler_params=params(12),
        name="settle",
    )(*rows, names, *tables, gain, shift)


def to_all(rows, axes):
    return lax.all_to_all(rows, axes, 0, 0, tiled=True)


def shards(
    features,
    occupancy,
    brick_coords,
    coarse_owner,
    conv_weight,
    conv_gain,
    conv_shift,
    reduce_weight,
    down_gain,
    down_shift,
):
    space_count = lax.axis_size("space")
    level_count = lax.axis_size("level")
    grid_x = space_count // GRID_Y

    def from_tile(block, step_x, step_y):
        route = []
        for s in range(space_count):
            x, y = s // GRID_Y, s % GRID_Y
            route.append(((x + step_x) % grid_x * GRID_Y + (y + step_y) % GRID_Y, s))
        return lax.ppermute(block, "space", route)

    outer, y_low, y_high = pack_outer(brick_coords, features, occupancy)
    y_before = from_tile(y_high, 0, -1)
    y_after = from_tile(y_low, 0, 1)
    inner = pack_inner(brick_coords, features, occupancy)
    x_low, x_high = faces(outer, inner, y_before, y_after)
    x_before = from_tile(x_high, -1, 0)
    x_after = from_tile(x_low, 1, 0)
    mid, part, taps = middle(outer, inner, y_before, y_after, conv_weight)
    edge, stats = edges(
        outer,
        inner,
        y_before,
        y_after,
        x_before,
        x_after,
        taps,
        part,
        coarse_owner,
        space_count * level_count,
    )
    sent, names, stats2 = section(
        mid,
        edge,
        outer,
        inner,
        to_all(stats, ("level", "space")),
        conv_gain[None],
        conv_shift[None],
        reduce_weight,
        space_count,
    )
    def up_level(block, distance):
        route = [(g, (g + distance) % level_count) for g in range(level_count)]
        return lax.ppermute(block, "level", route)

    near = up_level(sent, 1)
    back = up_level(sent, -1)
    table = to_all(stats2, "space")
    near, back, table = lax.optimization_barrier((near, back, table))
    here = merge(table)
    far0 = up_level(near[:1], 1)
    far1 = up_level(back[1:], -1)
    tables = [here] + [up_level(here, d) for d in range(1, level_count)]
    return settle(
        (sent, near, far0, far1, back), names, tables, down_gain[None], down_shift[None]
    )


def solution(mesh):
    in_specs = (
        P(("level", "space"), None, None),
        P(("level", "space"), None),
        P(None, ("level", "space")),
        P(("level", "space"), None),
        P(),
        P(),
        P(),
        P(),
        P(),
        P(),
    )
    out_specs = P(("level", "space"), None, None)
    return jax.shard_map(shards, mesh=mesh, in_specs=in_specs, out_specs=out_specs, check_vma=False)
```

```python
import functools

import jax
import jax.numpy as jnp
from jax import lax
from jax.experimental import pallas as pl
from jax.experimental.pallas import tpu as pltpu
from jax.sharding import PartitionSpec as P

BRICK = 8
TX = 2
TY = 4
TZ = 2
CAPC = 2
C = 96
C2 = 192
LANES = 128
SX = TX * BRICK
SY = TY * BRICK
SZ = TZ * BRICK
PAIRS = SY // 2
WIDE = 4 * C
GRID_Y = 4
EMPTY = -3e38
epsilon = 1e-05

bf16 = jnp.bfloat16
f32 = jnp.float32
VMEM = pl.BlockSpec(memory_space=pltpu.VMEM)
SMEM = pl.BlockSpec(memory_space=pltpu.SMEM)
HBM = pl.BlockSpec(memory_space=pltpu.HBM)


def params(mib=56):
    return pltpu.CompilerParams(vmem_limit_bytes=mib << 20)


def cell_chooser():
    row = lax.broadcasted_iota(jnp.int32, (256, 256), 0)
    lane = lax.broadcasted_iota(jnp.int32, (256, 256), 1)
    z = 2 * (row & 7) + ((row >> 3) & 1)
    source = ((z >> 3) << 7) + ((row >> 4) << 3) + (z & 7)
    return jnp.where(source == lane, 1.0, 0.0).astype(bf16)


def rows_dot(left, right):
    return lax.dot_general(left, right, (((1,), (1,)), ((), ())), preferred_element_type=f32)


def plain_dot(left, right):
    return lax.dot_general(left, right, (((1,), (0,)), ((), ())), preferred_element_type=f32)


def pack_bricks(parts, coords, features, occupancy, act, faces, order):
    for n in range(16):
        place = ((coords[0, n] % TX) * TY + coords[1, n] % TY) * TZ + coords[2, n]
        order[place] = n
    picks = cell_chooser()
    for tx in range(TX):
        for part, ty in enumerate(parts):
            halves = []
            for tz in range(TZ):
                n = order[(tx * TY + ty) * TZ + tz]
                gate = occupancy[pl.ds(n, 1), :].astype(f32)
                gate = jnp.broadcast_to(gate, (LANES, 512)).astype(bf16)
                halves.append(jnp.concatenate([features[n] * gate[:C], gate[C:]], axis=0))
            for h in range(4):
                lanes = slice(128 * h, 128 * h + 128)
                source = jnp.concatenate([half[:, lanes] for half in halves], axis=1)
                cells = rows_dot(picks, source).reshape(2, 4, 2, SZ, LANES).astype(bf16)
                x = 8 * tx + 2 * h
                act[x : x + 2, part] = cells
                if faces and ty == 0:
                    faces[0][x : x + 2] = cells[:, 0, 0]
                if faces and ty == TY - 1:
                    faces[1][x : x + 2] = cells[:, 3, 1]


def outer_kernel(
    coords, features, occupancy, act, y_low, y_high, coords_out, gates, order, places, bricks, sems
):
    copies = [
        pltpu.make_async_copy(coords, places, sems.at[0]),
        pltpu.make_async_copy(occupancy, gates, sems.at[1]),
        pltpu.make_async_copy(features, bricks, sems.at[2]),
        pltpu.make_async_copy(coords, coords_out, sems.at[3]),
    ]
    for copy in copies:
        copy.start()
    for copy in copies:
        copy.wait()
    pack_bricks((0, TY - 1), places, bricks, gates, act, (y_low, y_high), order)


def inner_kernel(coords, features, occupancy, act, order):
    pack_bricks((1, 2), coords, features, occupancy, act, (), order)


ACT = jax.ShapeDtypeStruct((SX, 2, 4, 2, SZ, LANES), bf16)


def pack_outer(coords, features, occupancy):
    side = jax.ShapeDtypeStruct((SX, SZ, LANES), bf16)
    arrays = [pltpu.with_memory_space_constraint(a, pltpu.HBM) for a in (coords, features, occupancy)]
    return pl.pallas_call(
        outer_kernel,
        out_shape=(
            ACT,
            side,
            side,
            jax.ShapeDtypeStruct(coords.shape, jnp.int32),
            jax.ShapeDtypeStruct(occupancy.shape, jnp.int32),
        ),
        in_specs=[HBM] * 3,
        out_specs=(VMEM,) * 5,
        scratch_shapes=[
            pltpu.SMEM((16,), jnp.int32),
            pltpu.SMEM((3, 16), jnp.int32),
            pltpu.VMEM((16, C, 512), bf16),
            pltpu.SemaphoreType.DMA((4,)),
        ],
        compiler_params=params(12),
        name="pack_outer",
    )(*arrays)


def pack_inner(coords, features, occupancy):
    return pl.pallas_call(
        inner_kernel,
        out_shape=ACT,
        in_specs=[SMEM, VMEM, VMEM],
        out_specs=VMEM,
        scratch_shapes=[pltpu.SMEM((16,), jnp.int32)],
        compiler_params=params(12),
        name="pack_inner",
    )(coords, features, occupancy)


def face_kernel(outer, inner, y_before, y_after, low, high):
    tile_y = lax.axis_index("space") % GRID_Y
    for face, x in ((low, 0), (high, SX - 1)):
        face[0] = kept(y_before[x], tile_y > 0)
        face[1 : SY + 1] = plane_of(outer, inner, x).reshape(SY, SZ, LANES)
        face[SY + 1] = kept(y_after[x], tile_y < GRID_Y - 1)


def faces(outer, inner, y_before, y_after):
    face = jax.ShapeDtypeStruct((SY + 2, SZ, LANES), bf16)
    return pl.pallas_call(
        face_kernel,
        out_shape=(face, face),
        in_specs=[VMEM] * 4,
        out_specs=(VMEM, VMEM),
        compiler_params=params(8),
        name="faces",
    )(outer, inner, y_before, y_after)


def window_forms(a, b, c, d):
    a, b, c, d = (cells.astype(f32) for cells in (a, b, c, d))
    lane = lax.broadcasted_iota(jnp.int32, a.shape, 2)
    b, c, d = pltpu.roll(b, 96, 2), pltpu.roll(c, 64, 2), pltpu.roll(d, 32, 2)
    wide = jnp.concatenate(
        [jnp.where(lane < 96, a, b), jnp.where(lane < 64, b, c), jnp.where(lane < 32, c, d)], axis=2
    ).reshape(PAIRS, 2, 8, WIDE)
    even, odd = wide[:, 0], wide[:, 1]
    place = lax.broadcasted_iota(jnp.int32, odd.shape, 1)
    before = jnp.where(place == 0, 0.0, pltpu.roll(odd, 1, 1))
    after = jnp.where(place == 7, 0.0, pltpu.roll(even, 7, 1))
    pairs = ((before, even), (even, odd), (odd, after))
    return [jnp.stack(pair, axis=1).reshape(PAIRS, SZ, WIDE).astype(bf16) for pair in pairs]


def lane_spread():
    row = lax.broadcasted_iota(jnp.int32, (LANES, LANES), 0)
    return jnp.where(row == LANES - 1, 1.0, 0.0).astype(bf16)


def plane_of(outer, inner, x):
    return jnp.concatenate([outer[x, 0], inner[x, 0], inner[x, 1], outer[x, 1]], axis=0)


def kept(value, inside):
    return value * jnp.where(inside, 1.0, 0.0).astype(bf16)


def planes_dot(pieces, taps):
    rows = [piece.reshape(-1, WIDE) for piece in pieces]
    return plain_dot(jnp.concatenate(rows, axis=1), taps)


def planes_mask(planes):
    spread = lane_spread()
    even = jnp.concatenate([plane[:, 0].reshape(PAIRS * SZ, LANES) for plane in planes], axis=0)
    odd = jnp.concatenate([plane[:, 1].reshape(PAIRS * SZ, LANES) for plane in planes], axis=0)
    return jnp.concatenate([plain_dot(even, spread), plain_dot(odd, spread)], axis=1)


def folded(row):
    return row[:, :LANES] + row[:, LANES:]


MID = SX - 2
STEP = 2


def merged(first, second):
    (mean0, square0, count0), (mean1, square1, count1) = first, second
    count = count0 + count1
    mean = (mean0 * count0 + mean1 * count1) / jnp.maximum(count, 1.0)
    square = square0 + square1 + count0 * (mean0 - mean) ** 2 + count1 * (mean1 - mean) ** 2
    return mean, square, count


def moments_of(value, mask):
    count = folded(jnp.sum(mask, axis=0, keepdims=True))
    mean = folded(jnp.sum(value * mask, axis=0, keepdims=True)) / jnp.maximum(count, 1.0)
    gap = (value - jnp.concatenate([mean, mean], axis=1)) * mask
    return mean, folded(jnp.sum(gap * gap, axis=0, keepdims=True)), count


def middle_kernel(outer, inner, y_before, y_after, weight, out, partial, stats, taps, grid):
    tile_y = lax.axis_index("space") % GRID_Y

    def fill(x):
        before = kept(y_before[x], tile_y > 0)[None]
        after = kept(y_after[x], tile_y < GRID_Y - 1)[None]
        plane = plane_of(outer, inner, x)
        even, odd = plane[:, 0], plane[:, 1]
        forms = window_forms(
            jnp.concatenate([before, odd[:-1]], axis=0),
            even,
            odd,
            jnp.concatenate([even[1:], after], axis=0),
        )
        for c in range(3):
            grid[c, x] = forms[c]

    taps[...] = jnp.zeros(taps.shape, bf16)
    for a in range(3):
        for b in range(3):
            for c in range(3):
                for parity in range(2):
                    first = (a * 3 + c) * WIDE + (b + parity) * C
                    taps[first : first + C, parity * LANES : parity * LANES + C] = weight[(a * 3 + b) * 3 + c].T
    for x in range(STEP + 2):
        fill(x)
    pieces = [grid[c, a] for a in range(2) for c in range(3)]
    partial[0] = planes_dot(pieces, taps[3 * WIDE :])
    zero = jnp.zeros((1, LANES), f32)
    carry = (zero, zero, zero)
    for x in range(0, MID, STEP):
        for later in range(x + STEP + 2, min(x + 2 * STEP + 2, SX)):
            fill(later)
        pieces = [grid[c, x + a : x + a + STEP] for a in range(3) for c in range(3)]
        value = planes_dot(pieces, taps[...])
        out[x : x + STEP] = value.reshape(STEP, PAIRS * SZ, 2 * LANES)
        mask = planes_mask([plane_of(outer, inner, x + 1 + step) for step in range(STEP)])
        carry = merged(carry, moments_of(value, mask))
    pieces = [grid[c, SX - 2 + a] for a in range(2) for c in range(3)]
    partial[1] = planes_dot(pieces, taps[: 6 * WIDE])
    stats[...] = jnp.concatenate(list(carry) + [jnp.zeros((5, LANES), f32)], axis=0)


def middle(outer, inner, y_before, y_after, weight):
    return pl.pallas_call(
        middle_kernel,
        out_shape=(
            pltpu.VMEM((MID, PAIRS * SZ, 2 * LANES), f32),
            jax.ShapeDtypeStruct((2, PAIRS * SZ, 2 * LANES), f32),
            jax.ShapeDtypeStruct((8, LANES), f32),
            jax.ShapeDtypeStruct((9 * WIDE, 2 * LANES), bf16),
        ),
        in_specs=[VMEM] * 5,
        out_specs=(VMEM,) * 4,
        scratch_shapes=[pltpu.VMEM((3, SX, PAIRS, SZ, WIDE), bf16)],
        compiler_params=params(26),
        name="middle",
    )(outer, inner, y_before, y_after, weight)


def edge_kernel(outer, inner, x_before, x_after, partial, taps, part, owners, out, stats):
    tile_x = lax.axis_index("space") // GRID_Y
    last_x = lax.axis_size("space") // GRID_Y - 1
    carry = (part[0:1], part[1:2], part[2:3])
    sides = ((x_before, tile_x > 0, 0, 0), (x_after, tile_x < last_x, 6 * WIDE, SX - 1))
    for index, (halo, inside, first, x) in enumerate(sides):
        cells = kept(halo[...], inside).reshape(PAIRS + 1, 2, SZ, LANES)
        forms = window_forms(cells[:-1, 0], cells[:-1, 1], cells[1:, 0], cells[1:, 1])
        value = partial[index] + planes_dot(forms, taps[first : first + 3 * WIDE])
        out[index] = value
        carry = merged(carry, moments_of(value, planes_mask([plane_of(outer, inner, x)])))
    joint, square, both = carry
    lane = lax.broadcasted_iota(jnp.int32, (1, LANES), 1)
    joint = jnp.where(lane == LANES - 1, both, joint)
    for q in range(2):
        joint = jnp.where(lane == C + q, owners[q, 0].astype(f32), joint)
    row = jnp.concatenate([joint, square], axis=1)
    stats[...] = jnp.broadcast_to(row[None], stats.shape)


def edges(outer, inner, x_before, x_after, partial, taps, part, owners, devices):
    return pl.pallas_call(
        edge_kernel,
        out_shape=(
            jax.ShapeDtypeStruct((2, PAIRS * SZ, 2 * LANES), f32),
            jax.ShapeDtypeStruct((devices, 1, 2 * LANES), f32),
        ),
        in_specs=[VMEM] * 7 + [SMEM],
        out_specs=(VMEM, VMEM),
        compiler_params=params(16),
        name="edges",
    )(outer, inner, x_before, x_after, partial, taps, part, owners)


def joined(table, width):
    means, squares = table[:, :, :width], table[:, :, width:]
    counts = table[:, :, width - 1 : width]
    whole = jnp.sum(counts, axis=0)
    mean = jnp.sum(means * counts, axis=0) / whole
    gap = means - mean[None]
    return mean, jnp.sum(squares + counts * gap * gap, axis=0) / whole


def section_kernel(
    mid, edge, outer, inner, table, gain, shift, weight, sent, names, stats, taps, down, cover, lines
):
    level, groups = lax.axis_index("level"), lax.axis_size("level")
    for distance in range(4):
        origin = (level + groups - distance) % groups
        device = origin * lax.axis_size("space") + lax.axis_index("space")
        names[distance] = table[device][:, :LANES]
    mean, var = joined(table, LANES)
    lines[...] = jnp.zeros(lines.shape, f32)
    lines[0:1, :C] = gain[...]
    lines[1:2, :C] = shift[...]
    real = lax.broadcasted_iota(jnp.int32, (1, LANES), 1) < C
    scale = jnp.where(real, lines[0:1] / jnp.sqrt(var + epsilon), 0.0)
    mean = jnp.where(real, mean, 0.0)
    moved = lines[1:2]
    mean = jnp.concatenate([mean, mean], axis=1)
    scale = jnp.concatenate([scale, scale], axis=1)
    moved = jnp.concatenate([moved, moved], axis=1)
    taps[...] = jnp.zeros(taps.shape, bf16)
    for a in range(2):
        for b in range(2):
            for c in range(2):
                first = ((a * 2 + c) * 2 + b) * LANES
                taps[:C2, first : first + C] = weight[(a * 2 + b) * 2 + c]

    spread = lane_spread()
    total = count = jnp.zeros((1, 2 * LANES), f32)
    for X in range(SX // 2):
        pieces, covers = [], []
        for a in range(2):
            x = 2 * X + a
            conv = edge[0] if x == 0 else edge[1] if x == SX - 1 else mid[x - 1]
            plane = plane_of(outer, inner, x)
            even = plane[:, 0].reshape(PAIRS * SZ, LANES)
            odd = plane[:, 1].reshape(PAIRS * SZ, LANES)
            even_mask, odd_mask = plain_dot(even, spread), plain_dot(odd, spread)
            mask = jnp.concatenate([even_mask, odd_mask], axis=1)
            active = jnp.concatenate([even, odd], axis=1).astype(f32)
            normed = (conv - mean) * scale + moved
            section = active + mask * jnp.maximum(normed, 0.0)
            section = section.reshape(PAIRS, 2, 8, 2 * LANES)
            for c in range(2):
                pieces.append(section[:, c].reshape(PAIRS * 8, 2 * LANES).astype(bf16))
            both = jnp.maximum(even_mask, odd_mask).reshape(PAIRS, 2, 8, LANES)
            covers.append(jnp.maximum(both[:, 0], both[:, 1]).reshape(PAIRS * 8, LANES))
        value = rows_dot(jnp.concatenate(pieces, axis=1), taps[...])
        value = value.astype(bf16).astype(f32)
        covered = jnp.maximum(covers[0], covers[1])
        covered = jnp.concatenate([covered, covered], axis=1)
        down[X] = value
        cover[X] = covered
        total = total + jnp.sum(value * covered, axis=0, keepdims=True)
        count = count + jnp.sum(covered, axis=0, keepdims=True)

    zero = jnp.zeros((1, 2 * LANES), f32)
    mean2 = total / jnp.maximum(count, 1.0)

    def spread_out(X, carry):
        gap = (down[X] - mean2) * cover[X]
        return carry + jnp.sum(gap * gap, axis=0, keepdims=True)

    square = lax.fori_loop(0, SX // 2, spread_out, zero)
    wide_lane = lax.broadcasted_iota(jnp.int32, (1, 2 * LANES), 1)
    row = jnp.concatenate([jnp.where(wide_lane == 2 * LANES - 1, count, mean2), square], axis=1)
    stats[...] = jnp.broadcast_to(row[None], stats.shape)

    unit = (
        lax.broadcasted_iota(jnp.int32, (C2, 2 * LANES), 0)
        == lax.broadcasted_iota(jnp.int32, (C2, 2 * LANES), 1)
    )
    unit = jnp.where(unit, 1.0, 0.0).astype(bf16)
    half = PAIRS // 2 * 8
    for q in range(2):
        value = down[:, q * half : (q + 1) * half].reshape(SX // 2 * half, 2 * LANES)
        covered = cover[:, q * half : (q + 1) * half].reshape(SX // 2 * half, 2 * LANES)
        coded = jnp.where(covered > 0, value, EMPTY).astype(bf16)
        sent[q] = rows_dot(unit, coded).astype(bf16)


def section(mid, edge, outer, inner, table, gain, shift, weight, devices):
    return pl.pallas_call(
        section_kernel,
        out_shape=(
            jax.ShapeDtypeStruct((2, C2, 512), bf16),
            jax.ShapeDtypeStruct((4, 1, LANES), f32),
            jax.ShapeDtypeStruct((devices, 1, 4 * LANES), f32),
        ),
        in_specs=[VMEM] * 8,
        out_specs=(VMEM,) * 3,
        scratch_shapes=[
            pltpu.VMEM((2 * LANES, 8 * LANES), bf16),
            pltpu.VMEM((SX // 2, PAIRS * 8, 2 * LANES), f32),
            pltpu.VMEM((SX // 2, PAIRS * 8, 2 * LANES), f32),
            pltpu.VMEM((8, LANES), f32),
        ],
        compiler_params=params(20),
        name="section",
    )(mid, edge, outer, inner, table, gain, shift, weight)


def merge_kernel(table, near, back, out, up, down):
    width = 2 * LANES
    means, squares = table[:, :, :width], table[:, :, width:]
    counts = table[:, :, width - 1 : width]
    whole = jnp.sum(counts, axis=0)
    mean = jnp.sum(means * counts, axis=0) / jnp.maximum(whole, 1.0)
    gap = means - mean[None]
    square = jnp.sum(squares + counts * gap * gap, axis=0)
    lane = lax.broadcasted_iota(jnp.int32, (1, width), 1)
    row = jnp.concatenate([jnp.where(lane == width - 1, whole, mean), square], axis=1)
    out[...] = row[None]
    high = row.astype(bf16).astype(f32)
    middle = (row - high).astype(bf16).astype(f32)
    low = row - high - middle
    rows = jnp.concatenate([high, middle, low, jnp.zeros((13, 2 * width), f32)], axis=0).astype(bf16)
    for block, brick in ((up, near[0]), (down, back[1])):
        block[:C2] = brick
        block[C2:] = rows


def merge(table, near, back):
    block = jax.ShapeDtypeStruct((C2 + 16, 512), bf16)
    return pl.pallas_call(
        merge_kernel,
        out_shape=(jax.ShapeDtypeStruct((1, 1, 4 * LANES), f32), block, block),
        in_specs=[VMEM] * 3,
        out_specs=(VMEM,) * 3,
        compiler_params=params(8),
        name="merge",
    )(table, near, back)


def row_of(block):
    rows = block[C2:].astype(f32)
    return rows[0:1] + rows[1:2] + rows[2:3]


def settle_kernel(
    own, near, far0, far1, back, names, row_here, row_far, gain, shift, out, lines, ready, sems
):
    lines[...] = jnp.zeros(lines.shape, f32)
    rows = (row_here[0], row_of(far0), row_far[0], row_of(far1))
    table = jnp.concatenate([row[None] for row in rows], axis=0)
    mean, var = joined(table, 2 * LANES)
    lines[0:1] = mean
    lines[1:2] = var
    lines[2:3, :C2] = gain[...]
    lines[3:4, :C2] = shift[...]
    turned = lines[...].T[:C2]
    mean, moved = turned[:, 0:1], turned[:, 3:4]
    scale = turned[:, 2:3] / jnp.sqrt(turned[:, 1:2] + epsilon)
    level = lax.axis_index("level")
    groups = lax.axis_size("level")
    copies = []
    sources = ((own[0], own[1]), (near[0], near[1]), (far0[:C2], far1[:C2]), (back[0], back[1]))
    for distance, (first, second) in enumerate(sources):
        origin = (level + groups - distance) % groups
        named = jnp.where(names[distance] == level.astype(f32), 1.0, 0.0)
        takes0, takes1 = named[:, C : C + 1], named[:, C + 1 : C + 2]
        value0 = jnp.maximum((first.astype(f32) - mean) * scale + moved, 0.0)
        value1 = jnp.maximum((second.astype(f32) - mean) * scale + moved, 0.0)
        chosen = (
            jnp.where(takes0 > 0, value0, jnp.where(takes1 > 0, value1, 0.0)),
            jnp.where(takes0 * takes1 > 0, value1, 0.0),
        )
        for k in range(CAPC):
            slot = distance * CAPC + k
            ready[slot] = chosen[k].astype(bf16)
            copies.append(
                pltpu.make_async_copy(ready.at[slot], out.at[origin * CAPC + k], sems.at[slot])
            )
            copies[-1].start()
    for copy in copies:
        copy.wait()


def settle(rows, names, tables, gain, shift):
    return pl.pallas_call(
        settle_kernel,
        out_shape=jax.ShapeDtypeStruct((8, C2, 512), bf16),
        in_specs=[VMEM] * 10,
        out_specs=HBM,
        scratch_shapes=[
            pltpu.VMEM((8, 2 * LANES), f32),
            pltpu.VMEM((8, C2, 512), bf16),
            pltpu.SemaphoreType.DMA((8,)),
        ],
        compiler_params=params(12),
        name="settle",
    )(*rows, names, *tables, gain, shift)


def to_all(rows, axes):
    return lax.all_to_all(rows, axes, 0, 0, tiled=True)


def shards(
    features,
    occupancy,
    brick_coords,
    coarse_owner,
    conv_weight,
    conv_gain,
    conv_shift,
    reduce_weight,
    down_gain,
    down_shift,
):
    space_count = lax.axis_size("space")
    level_count = lax.axis_size("level")
    grid_x = space_count // GRID_Y

    def from_tile(block, step_x, step_y):
        route = []
        for s in range(space_count):
            x, y = s // GRID_Y, s % GRID_Y
            route.append(((x + step_x) % grid_x * GRID_Y + (y + step_y) % GRID_Y, s))
        return lax.ppermute(block, "space", route)

    outer, y_low, y_high, coords, gates = pack_outer(brick_coords, features, occupancy)
    y_before = from_tile(y_high, 0, -1)
    y_after = from_tile(y_low, 0, 1)
    inner = pack_inner(coords, features, gates)
    x_low, x_high = faces(outer, inner, y_before, y_after)
    x_before = from_tile(x_high, -1, 0)
    x_after = from_tile(x_low, 1, 0)
    mid, partial, part, taps = middle(outer, inner, y_before, y_after, conv_weight)
    edge, stats = edges(
        outer,
        inner,
        x_before,
        x_after,
        partial,
        taps,
        part,
        coarse_owner,
        space_count * level_count,
    )
    sent, names, stats2 = section(
        mid,
        edge,
        outer,
        inner,
        to_all(stats, ("level", "space")),
        conv_gain[None],
        conv_shift[None],
        reduce_weight,
        space_count,
    )
    def up_level(block, distance):
        route = [(g, (g + distance) % level_count) for g in range(level_count)]
        return lax.ppermute(block, "level", route)

    near = up_level(sent, 1)
    back = up_level(sent, -1)
    here, up, down = merge(to_all(stats2, "space"), near, back)
    tables = [here, up_level(here, 2)]
    far0 = up_level(up, 1)
    far1 = up_level(down, -1)
    return settle(
        (sent, near, far0, far1, back), names, tables, down_gain[None], down_shift[None]
    )


def solution(mesh):
    in_specs = (
        P(("level", "space"), None, None),
        P(("level", "space"), None),
        P(None, ("level", "space")),
        P(("level", "space"), None),
        P(),
        P(),
        P(),
        P(),
        P(),
        P(),
    )
    out_specs = P(("level", "space"), None, None)
    return jax.shard_map(shards, mesh=mesh, in_specs=in_specs, out_specs=out_specs, check_vma=False)
```

```python
import functools

import jax
import jax.numpy as jnp
from jax import lax
from jax.experimental import pallas as pl
from jax.experimental.pallas import tpu as pltpu
from jax.sharding import PartitionSpec as P

BRICK = 8
TX = 2
TY = 4
TZ = 2
CAPC = 2
C = 96
C2 = 192
LANES = 128
SX = TX * BRICK
SY = TY * BRICK
SZ = TZ * BRICK
PAIRS = SY // 2
WIDE = 4 * C
GRID_Y = 4
EMPTY = -3e38
epsilon = 1e-05

bf16 = jnp.bfloat16
f32 = jnp.float32
VMEM = pl.BlockSpec(memory_space=pltpu.VMEM)
SMEM = pl.BlockSpec(memory_space=pltpu.SMEM)
HBM = pl.BlockSpec(memory_space=pltpu.HBM)


def params(mib=56):
    return pltpu.CompilerParams(vmem_limit_bytes=mib << 20)


def cell_chooser():
    row = lax.broadcasted_iota(jnp.int32, (256, 256), 0)
    lane = lax.broadcasted_iota(jnp.int32, (256, 256), 1)
    z = 2 * (row & 7) + ((row >> 3) & 1)
    source = ((z >> 3) << 7) + ((row >> 4) << 3) + (z & 7)
    return jnp.where(source == lane, 1.0, 0.0).astype(bf16)


def rows_dot(left, right):
    return lax.dot_general(left, right, (((1,), (1,)), ((), ())), preferred_element_type=f32)


def plain_dot(left, right):
    return lax.dot_general(left, right, (((1,), (0,)), ((), ())), preferred_element_type=f32)


def pack_bricks(parts, coords, features, occupancy, act, faces, order):
    for n in range(16):
        place = ((coords[0, n] % TX) * TY + coords[1, n] % TY) * TZ + coords[2, n]
        order[place] = n
    picks = cell_chooser()
    for tx in range(TX):
        for part, ty in enumerate(parts):
            halves = []
            for tz in range(TZ):
                n = order[(tx * TY + ty) * TZ + tz]
                gate = occupancy[pl.ds(n, 1), :].astype(f32)
                gate = jnp.broadcast_to(gate, (LANES, 512)).astype(bf16)
                halves.append(jnp.concatenate([features[n] * gate[:C], gate[C:]], axis=0))
            for h in range(4):
                lanes = slice(128 * h, 128 * h + 128)
                source = jnp.concatenate([half[:, lanes] for half in halves], axis=1)
                cells = rows_dot(picks, source).reshape(2, 4, 2, SZ, LANES).astype(bf16)
                x = 8 * tx + 2 * h
                act[x : x + 2, part] = cells
                if faces and ty == 0:
                    faces[0][x : x + 2] = cells[:, 0, 0]
                if faces and ty == TY - 1:
                    faces[1][x : x + 2] = cells[:, 3, 1]


def outer_kernel(
    coords, features, occupancy, act, y_low, y_high, coords_out, gates, order, places, bricks, sems
):
    copies = [
        pltpu.make_async_copy(coords, places, sems.at[0]),
        pltpu.make_async_copy(occupancy, gates, sems.at[1]),
        pltpu.make_async_copy(features, bricks, sems.at[2]),
        pltpu.make_async_copy(coords, coords_out, sems.at[3]),
    ]
    for copy in copies:
        copy.start()
    for copy in copies:
        copy.wait()
    pack_bricks((0, TY - 1), places, bricks, gates, act, (y_low, y_high), order)


def inner_kernel(coords, features, occupancy, act, order):
    pack_bricks((1, 2), coords, features, occupancy, act, (), order)


ACT = jax.ShapeDtypeStruct((SX, 2, 4, 2, SZ, LANES), bf16)


def pack_outer(coords, features, occupancy):
    side = jax.ShapeDtypeStruct((SX, SZ, LANES), bf16)
    arrays = [pltpu.with_memory_space_constraint(a, pltpu.HBM) for a in (coords, features, occupancy)]
    return pl.pallas_call(
        outer_kernel,
        out_shape=(
            ACT,
            side,
            side,
            jax.ShapeDtypeStruct(coords.shape, jnp.int32),
            jax.ShapeDtypeStruct(occupancy.shape, jnp.int32),
        ),
        in_specs=[HBM] * 3,
        out_specs=(VMEM,) * 5,
        scratch_shapes=[
            pltpu.SMEM((16,), jnp.int32),
            pltpu.SMEM((3, 16), jnp.int32),
            pltpu.VMEM((16, C, 512), bf16),
            pltpu.SemaphoreType.DMA((4,)),
        ],
        compiler_params=params(12),
        name="pack_outer",
    )(*arrays)


def pack_inner(coords, features, occupancy):
    return pl.pallas_call(
        inner_kernel,
        out_shape=ACT,
        in_specs=[SMEM, VMEM, VMEM],
        out_specs=VMEM,
        scratch_shapes=[pltpu.SMEM((16,), jnp.int32)],
        compiler_params=params(12),
        name="pack_inner",
    )(coords, features, occupancy)


def face_kernel(outer, inner, y_before, y_after, low, high):
    tile_y = lax.axis_index("space") % GRID_Y
    for face, x in ((low, 0), (high, SX - 1)):
        face[0] = kept(y_before[x], tile_y > 0)
        face[1 : SY + 1] = plane_of(outer, inner, x).reshape(SY, SZ, LANES)
        face[SY + 1] = kept(y_after[x], tile_y < GRID_Y - 1)


def faces(outer, inner, y_before, y_after):
    face = jax.ShapeDtypeStruct((SY + 2, SZ, LANES), bf16)
    return pl.pallas_call(
        face_kernel,
        out_shape=(face, face),
        in_specs=[VMEM] * 4,
        out_specs=(VMEM, VMEM),
        compiler_params=params(8),
        name="faces",
    )(outer, inner, y_before, y_after)


def window_forms(a, b, c, d):
    a, b, c, d = (cells.astype(f32) for cells in (a, b, c, d))
    lane = lax.broadcasted_iota(jnp.int32, a.shape, 2)
    b, c, d = pltpu.roll(b, 96, 2), pltpu.roll(c, 64, 2), pltpu.roll(d, 32, 2)
    wide = jnp.concatenate(
        [jnp.where(lane < 96, a, b), jnp.where(lane < 64, b, c), jnp.where(lane < 32, c, d)], axis=2
    ).reshape(PAIRS, 2, 8, WIDE)
    even, odd = wide[:, 0], wide[:, 1]
    place = lax.broadcasted_iota(jnp.int32, odd.shape, 1)
    before = jnp.where(place == 0, 0.0, pltpu.roll(odd, 1, 1))
    after = jnp.where(place == 7, 0.0, pltpu.roll(even, 7, 1))
    pairs = ((before, even), (even, odd), (odd, after))
    return [jnp.stack(pair, axis=1).reshape(PAIRS, SZ, WIDE).astype(bf16) for pair in pairs]


def plane_of(outer, inner, x):
    return jnp.concatenate([outer[x, 0], inner[x, 0], inner[x, 1], outer[x, 1]], axis=0)


def kept(value, inside):
    return value * jnp.where(inside, 1.0, 0.0).astype(bf16)


def planes_dot(pieces, taps):
    rows = [piece.reshape(-1, WIDE) for piece in pieces]
    return plain_dot(jnp.concatenate(rows, axis=1), taps)


def mask_of(cells):
    return jnp.broadcast_to(cells[:, LANES - 1 :], cells.shape)


def rows_of(planes, parity):
    return jnp.concatenate(
        [plane[:, parity].reshape(PAIRS * SZ, LANES) for plane in planes], axis=0
    ).astype(f32)


def planes_mask(planes):
    return jnp.concatenate([mask_of(rows_of(planes, 0)), mask_of(rows_of(planes, 1))], axis=1)


def folded(row):
    return row[:, :LANES] + row[:, LANES:]


MID = SX - 2
STEP = 2
GROUP = 2


def merged(first, second):
    (mean0, square0, count0), (mean1, square1, count1) = first, second
    count = count0 + count1
    mean = (mean0 * count0 + mean1 * count1) / jnp.maximum(count, 1.0)
    square = square0 + square1 + count0 * (mean0 - mean) ** 2 + count1 * (mean1 - mean) ** 2
    return mean, square, count


def moments_of(value, mask):
    count = folded(jnp.sum(mask, axis=0, keepdims=True))
    mean = folded(jnp.sum(value * mask, axis=0, keepdims=True)) / jnp.maximum(count, 1.0)
    gap = (value - jnp.concatenate([mean, mean], axis=1)) * mask
    return mean, folded(jnp.sum(gap * gap, axis=0, keepdims=True)), count


def middle_kernel(outer, inner, y_before, y_after, weight, out, partial, stats, taps, grid):
    tile_y = lax.axis_index("space") % GRID_Y

    def fill(x):
        before = kept(y_before[x], tile_y > 0)[None]
        after = kept(y_after[x], tile_y < GRID_Y - 1)[None]
        plane = plane_of(outer, inner, x)
        even, odd = plane[:, 0], plane[:, 1]
        forms = window_forms(
            jnp.concatenate([before, odd[:-1]], axis=0),
            even,
            odd,
            jnp.concatenate([even[1:], after], axis=0),
        )
        for c in range(3):
            grid[c, x] = forms[c]

    taps[...] = jnp.zeros(taps.shape, bf16)
    for a in range(3):
        for b in range(3):
            for c in range(3):
                for parity in range(2):
                    first = (a * 3 + c) * WIDE + (b + parity) * C
                    taps[first : first + C, parity * LANES : parity * LANES + C] = weight[(a * 3 + b) * 3 + c].T
    for x in range(STEP + 2):
        fill(x)
    pieces = [grid[c, a] for a in range(2) for c in range(3)]
    partial[0] = planes_dot(pieces, taps[3 * WIDE :])
    zero = jnp.zeros((1, LANES), f32)
    carry = (zero, zero, zero)
    for x in range(0, MID, STEP):
        for later in range(x + STEP + 2, min(x + 2 * STEP + 2, SX)):
            fill(later)
        pieces = [grid[c, x + a : x + a + STEP] for a in range(3) for c in range(3)]
        value = planes_dot(pieces, taps[...])
        out[x : x + STEP] = value.reshape(STEP, PAIRS * SZ, 2 * LANES)
        mask = planes_mask([plane_of(outer, inner, x + 1 + step) for step in range(STEP)])
        carry = merged(carry, moments_of(value, mask))
    pieces = [grid[c, SX - 2 + a] for a in range(2) for c in range(3)]
    partial[1] = planes_dot(pieces, taps[: 6 * WIDE])
    stats[...] = jnp.concatenate(list(carry) + [jnp.zeros((5, LANES), f32)], axis=0)


def middle(outer, inner, y_before, y_after, weight):
    return pl.pallas_call(
        middle_kernel,
        out_shape=(
            pltpu.VMEM((MID, PAIRS * SZ, 2 * LANES), f32),
            jax.ShapeDtypeStruct((2, PAIRS * SZ, 2 * LANES), f32),
            jax.ShapeDtypeStruct((8, LANES), f32),
            jax.ShapeDtypeStruct((9 * WIDE, 2 * LANES), bf16),
        ),
        in_specs=[VMEM] * 5,
        out_specs=(VMEM,) * 4,
        scratch_shapes=[pltpu.VMEM((3, SX, PAIRS, SZ, WIDE), bf16)],
        compiler_params=params(26),
        name="middle",
    )(outer, inner, y_before, y_after, weight)


def edge_kernel(outer, inner, x_before, x_after, partial, taps, part, owners, out, stats):
    tile_x = lax.axis_index("space") // GRID_Y
    last_x = lax.axis_size("space") // GRID_Y - 1
    carry = (part[0:1], part[1:2], part[2:3])
    sides = ((x_before, tile_x > 0, 0, 0), (x_after, tile_x < last_x, 6 * WIDE, SX - 1))
    for index, (halo, inside, first, x) in enumerate(sides):
        cells = kept(halo[...], inside).reshape(PAIRS + 1, 2, SZ, LANES)
        forms = window_forms(cells[:-1, 0], cells[:-1, 1], cells[1:, 0], cells[1:, 1])
        value = partial[index] + planes_dot(forms, taps[first : first + 3 * WIDE])
        out[index] = value
        carry = merged(carry, moments_of(value, planes_mask([plane_of(outer, inner, x)])))
    joint, square, both = carry
    lane = lax.broadcasted_iota(jnp.int32, (1, LANES), 1)
    joint = jnp.where(lane == LANES - 1, both, joint)
    for q in range(2):
        joint = jnp.where(lane == C + q, owners[q, 0].astype(f32), joint)
    row = jnp.concatenate([joint, square], axis=1)
    stats[...] = jnp.broadcast_to(row[None], stats.shape)


def edges(outer, inner, x_before, x_after, partial, taps, part, owners, devices):
    return pl.pallas_call(
        edge_kernel,
        out_shape=(
            jax.ShapeDtypeStruct((2, PAIRS * SZ, 2 * LANES), f32),
            jax.ShapeDtypeStruct((devices, 1, 2 * LANES), f32),
        ),
        in_specs=[VMEM] * 7 + [SMEM],
        out_specs=(VMEM, VMEM),
        compiler_params=params(16),
        name="edges",
    )(outer, inner, x_before, x_after, partial, taps, part, owners)


def joined(table, width):
    means, squares = table[:, :, :width], table[:, :, width:]
    counts = table[:, :, width - 1 : width]
    whole = jnp.sum(counts, axis=0)
    mean = jnp.sum(means * counts, axis=0) / whole
    gap = means - mean[None]
    return mean, jnp.sum(squares + counts * gap * gap, axis=0) / whole


def section_kernel(
    mid, edge, outer, inner, table, gain, shift, weight, sent, names, stats, taps, down, cover, lines
):
    level, groups = lax.axis_index("level"), lax.axis_size("level")
    for distance in range(4):
        origin = (level + groups - distance) % groups
        device = origin * lax.axis_size("space") + lax.axis_index("space")
        names[distance] = table[device][:, :LANES]
    mean, var = joined(table, LANES)
    lines[...] = jnp.zeros(lines.shape, f32)
    lines[0:1, :C] = gain[...]
    lines[1:2, :C] = shift[...]
    real = lax.broadcasted_iota(jnp.int32, (1, LANES), 1) < C
    scale = jnp.where(real, lines[0:1] / jnp.sqrt(var + epsilon), 0.0)
    mean = jnp.where(real, mean, 0.0)
    moved = lines[1:2] - mean * scale
    scale = jnp.concatenate([scale, scale], axis=1)
    moved = jnp.concatenate([moved, moved], axis=1)
    taps[...] = jnp.zeros(taps.shape, bf16)
    for a in range(2):
        for b in range(2):
            for c in range(2):
                first = ((a * 2 + c) * 2 + b) * LANES
                taps[first : first + C, :C2] = weight[(a * 2 + b) * 2 + c].T

    total = count = jnp.zeros((1, 2 * LANES), f32)
    for group in range(0, SX // 2, GROUP):
        blocks, coverings = [], []
        for X in range(group, group + GROUP):
            pieces, covers = [], []
            for a in range(2):
                x = 2 * X + a
                conv = edge[0] if x == 0 else edge[1] if x == SX - 1 else mid[x - 1]
                plane = plane_of(outer, inner, x)
                even, odd = rows_of([plane], 0), rows_of([plane], 1)
                even_mask, odd_mask = mask_of(even), mask_of(odd)
                mask = jnp.concatenate([even_mask, odd_mask], axis=1)
                active = jnp.concatenate([even, odd], axis=1)
                section = active + mask * jnp.maximum(conv * scale + moved, 0.0)
                section = section.reshape(PAIRS, 2, 8, 2 * LANES)
                for c in range(2):
                    pieces.append(section[:, c].reshape(PAIRS * 8, 2 * LANES).astype(bf16))
                both = jnp.maximum(even_mask, odd_mask).reshape(PAIRS, 2, 8, LANES)
                covers.append(jnp.maximum(both[:, 0], both[:, 1]).reshape(PAIRS * 8, LANES))
            blocks.append(jnp.concatenate(pieces, axis=1))
            coverings.append(jnp.maximum(covers[0], covers[1]))
        value = plain_dot(jnp.concatenate(blocks, axis=0), taps[...])
        value = value.astype(bf16).astype(f32)
        covered = jnp.concatenate(coverings, axis=0)
        covered = jnp.concatenate([covered, covered], axis=1)
        down[group : group + GROUP] = value.reshape(GROUP, PAIRS * 8, 2 * LANES)
        cover[group : group + GROUP] = covered.reshape(GROUP, PAIRS * 8, 2 * LANES)
        total = total + jnp.sum(value * covered, axis=0, keepdims=True)
        count = count + jnp.sum(covered, axis=0, keepdims=True)

    zero = jnp.zeros((1, 2 * LANES), f32)
    mean2 = total / jnp.maximum(count, 1.0)

    def spread_out(X, carry):
        gap = (down[X] - mean2) * cover[X]
        return carry + jnp.sum(gap * gap, axis=0, keepdims=True)

    square = lax.fori_loop(0, SX // 2, spread_out, zero)
    wide_lane = lax.broadcasted_iota(jnp.int32, (1, 2 * LANES), 1)
    row = jnp.concatenate([jnp.where(wide_lane == 2 * LANES - 1, count, mean2), square], axis=1)
    stats[...] = jnp.broadcast_to(row[None], stats.shape)

    unit = (
        lax.broadcasted_iota(jnp.int32, (C2, 2 * LANES), 0)
        == lax.broadcasted_iota(jnp.int32, (C2, 2 * LANES), 1)
    )
    unit = jnp.where(unit, 1.0, 0.0).astype(bf16)
    half = PAIRS // 2 * 8
    for q in range(2):
        value = down[:, q * half : (q + 1) * half].reshape(SX // 2 * half, 2 * LANES)
        covered = cover[:, q * half : (q + 1) * half].reshape(SX // 2 * half, 2 * LANES)
        coded = jnp.where(covered > 0, value, EMPTY).astype(bf16)
        sent[q] = rows_dot(unit, coded).astype(bf16)


def section(mid, edge, outer, inner, table, gain, shift, weight, devices):
    return pl.pallas_call(
        section_kernel,
        out_shape=(
            jax.ShapeDtypeStruct((2, C2, 512), bf16),
            jax.ShapeDtypeStruct((4, 1, LANES), f32),
            jax.ShapeDtypeStruct((devices, 1, 4 * LANES), f32),
        ),
        in_specs=[VMEM] * 8,
        out_specs=(VMEM,) * 3,
        scratch_shapes=[
            pltpu.VMEM((8 * LANES, 2 * LANES), bf16),
            pltpu.VMEM((SX // 2, PAIRS * 8, 2 * LANES), f32),
            pltpu.VMEM((SX // 2, PAIRS * 8, 2 * LANES), f32),
            pltpu.VMEM((8, LANES), f32),
        ],
        compiler_params=params(20),
        name="section",
    )(mid, edge, outer, inner, table, gain, shift, weight)


def merge_kernel(table, near, back, out, up, down):
    width = 2 * LANES
    means, squares = table[:, :, :width], table[:, :, width:]
    counts = table[:, :, width - 1 : width]
    whole = jnp.sum(counts, axis=0)
    mean = jnp.sum(means * counts, axis=0) / jnp.maximum(whole, 1.0)
    gap = means - mean[None]
    square = jnp.sum(squares + counts * gap * gap, axis=0)
    lane = lax.broadcasted_iota(jnp.int32, (1, width), 1)
    row = jnp.concatenate([jnp.where(lane == width - 1, whole, mean), square], axis=1)
    out[...] = row[None]
    high = row.astype(bf16).astype(f32)
    middle = (row - high).astype(bf16).astype(f32)
    low = row - high - middle
    rows = jnp.concatenate([high, middle, low, jnp.zeros((13, 2 * width), f32)], axis=0).astype(bf16)
    for block, brick in ((up, near[0]), (down, back[1])):
        block[:C2] = brick
        block[C2:] = rows


def merge(table, near, back):
    block = jax.ShapeDtypeStruct((C2 + 16, 512), bf16)
    return pl.pallas_call(
        merge_kernel,
        out_shape=(jax.ShapeDtypeStruct((1, 1, 4 * LANES), f32), block, block),
        in_specs=[VMEM] * 3,
        out_specs=(VMEM,) * 3,
        compiler_params=params(8),
        name="merge",
    )(table, near, back)


def row_of(block):
    rows = block[C2:].astype(f32)
    return rows[0:1] + rows[1:2] + rows[2:3]


def settle_kernel(
    own, near, far0, far1, back, names, row_here, row_far, gain, shift, out, lines, ready, sems
):
    lines[...] = jnp.zeros(lines.shape, f32)
    rows = (row_here[0], row_of(far0), row_far[0], row_of(far1))
    table = jnp.concatenate([row[None] for row in rows], axis=0)
    mean, var = joined(table, 2 * LANES)
    lines[0:1] = mean
    lines[1:2] = var
    lines[2:3, :C2] = gain[...]
    lines[3:4, :C2] = shift[...]
    turned = lines[...].T[:C2]
    scale = turned[:, 2:3] / jnp.sqrt(turned[:, 1:2] + epsilon)
    moved = turned[:, 3:4] - turned[:, 0:1] * scale
    level = lax.axis_index("level")
    groups = lax.axis_size("level")
    copies = []
    sources = ((own[0], own[1]), (near[0], near[1]), (far0[:C2], far1[:C2]), (back[0], back[1]))
    for distance, (first, second) in enumerate(sources):
        origin = (level + groups - distance) % groups
        named = jnp.where(names[distance] == level.astype(f32), 1.0, 0.0)
        takes0, takes1 = named[:, C : C + 1], named[:, C + 1 : C + 2]
        value0 = jnp.maximum(first.astype(f32) * scale + moved, 0.0)
        value1 = jnp.maximum(second.astype(f32) * scale + moved, 0.0)
        chosen = (
            jnp.where(takes0 > 0, value0, jnp.where(takes1 > 0, value1, 0.0)),
            jnp.where(takes0 * takes1 > 0, value1, 0.0),
        )
        for k in range(CAPC):
            slot = distance * CAPC + k
            ready[slot] = chosen[k].astype(bf16)
            copies.append(
                pltpu.make_async_copy(ready.at[slot], out.at[origin * CAPC + k], sems.at[slot])
            )
            copies[-1].start()
    for copy in copies:
        copy.wait()


def settle(rows, names, tables, gain, shift):
    return pl.pallas_call(
        settle_kernel,
        out_shape=jax.ShapeDtypeStruct((8, C2, 512), bf16),
        in_specs=[VMEM] * 10,
        out_specs=HBM,
        scratch_shapes=[
            pltpu.VMEM((8, 2 * LANES), f32),
            pltpu.VMEM((8, C2, 512), bf16),
            pltpu.SemaphoreType.DMA((8,)),
        ],
        compiler_params=params(12),
        name="settle",
    )(*rows, names, *tables, gain, shift)


def to_all(rows, axes):
    return lax.all_to_all(rows, axes, 0, 0, tiled=True)


def shards(
    features,
    occupancy,
    brick_coords,
    coarse_owner,
    conv_weight,
    conv_gain,
    conv_shift,
    reduce_weight,
    down_gain,
    down_shift,
):
    space_count = lax.axis_size("space")
    level_count = lax.axis_size("level")
    grid_x = space_count // GRID_Y

    def from_tile(block, step_x, step_y):
        route = []
        for s in range(space_count):
            x, y = s // GRID_Y, s % GRID_Y
            route.append(((x + step_x) % grid_x * GRID_Y + (y + step_y) % GRID_Y, s))
        return lax.ppermute(block, "space", route)

    outer, y_low, y_high, coords, gates = pack_outer(brick_coords, features, occupancy)
    y_before = from_tile(y_high, 0, -1)
    y_after = from_tile(y_low, 0, 1)
    inner = pack_inner(coords, features, gates)
    x_low, x_high = faces(outer, inner, y_before, y_after)
    x_before = from_tile(x_high, -1, 0)
    x_after = from_tile(x_low, 1, 0)
    mid, partial, part, taps = middle(outer, inner, y_before, y_after, conv_weight)
    edge, stats = edges(
        outer,
        inner,
        x_before,
        x_after,
        partial,
        taps,
        part,
        coarse_owner,
        space_count * level_count,
    )
    sent, names, stats2 = section(
        mid,
        edge,
        outer,
        inner,
        to_all(stats, ("level", "space")),
        conv_gain[None],
        conv_shift[None],
        reduce_weight,
        space_count,
    )
    def up_level(block, distance):
        route = [(g, (g + distance) % level_count) for g in range(level_count)]
        return lax.ppermute(block, "level", route)

    near = up_level(sent, 1)
    back = up_level(sent, -1)
    here, up, down = merge(to_all(stats2, "space"), near, back)
    tables = [here, up_level(here, 2)]
    far0 = up_level(up, 1)
    far1 = up_level(down, -1)
    return settle(
        (sent, near, far0, far1, back), names, tables, down_gain[None], down_shift[None]
    )


def solution(mesh):
    in_specs = (
        P(("level", "space"), None, None),
        P(("level", "space"), None),
        P(None, ("level", "space")),
        P(("level", "space"), None),
        P(),
        P(),
        P(),
        P(),
        P(),
        P(),
    )
    out_specs = P(("level", "space"), None, None)
    return jax.shard_map(shards, mesh=mesh, in_specs=in_specs, out_specs=out_specs, check_vma=False)
```

```python
import functools

import jax
import jax.numpy as jnp
from jax import lax
from jax.experimental import pallas as pl
from jax.experimental.pallas import tpu as pltpu
from jax.sharding import PartitionSpec as P

BRICK = 8
TX = 2
TY = 4
TZ = 2
CAPC = 2
C = 96
C2 = 192
LANES = 128
SX = TX * BRICK
SY = TY * BRICK
SZ = TZ * BRICK
PAIRS = SY // 2
WIDE = 4 * C
GRID_Y = 4
EMPTY = -3e38
epsilon = 1e-05

bf16 = jnp.bfloat16
f32 = jnp.float32
VMEM = pl.BlockSpec(memory_space=pltpu.VMEM)
SMEM = pl.BlockSpec(memory_space=pltpu.SMEM)
HBM = pl.BlockSpec(memory_space=pltpu.HBM)


def params(mib=56):
    return pltpu.CompilerParams(vmem_limit_bytes=mib << 20)


def cell_chooser():
    row = lax.broadcasted_iota(jnp.int32, (256, 256), 0)
    lane = lax.broadcasted_iota(jnp.int32, (256, 256), 1)
    z = 2 * (row & 7) + ((row >> 3) & 1)
    source = ((z >> 3) << 7) + ((row >> 4) << 3) + (z & 7)
    return jnp.where(source == lane, 1.0, 0.0).astype(bf16)


def rows_dot(left, right):
    return lax.dot_general(left, right, (((1,), (1,)), ((), ())), preferred_element_type=f32)


def plain_dot(left, right):
    return lax.dot_general(left, right, (((1,), (0,)), ((), ())), preferred_element_type=f32)


def brick_order(coords, order):
    for n in range(16):
        place = ((coords[0, n] % TX) * TY + coords[1, n] % TY) * TZ + coords[2, n]
        order[place] = n


def gated_brick(n, features, occupancy):
    gate = occupancy[pl.ds(n, 1), :].astype(f32)
    gate = jnp.broadcast_to(gate, (LANES, 512)).astype(bf16)
    return jnp.concatenate([features[n] * gate[:C], gate[C:]], axis=0)


def side_chooser(j):
    row = lax.broadcasted_iota(jnp.int32, (128, 1024), 0)
    lane = lax.broadcasted_iota(jnp.int32, (128, 1024), 1)
    z = 2 * (row & 7) + ((row >> 3) & 1)
    source = ((z >> 3) << 9) + ((row >> 4) << 6) + 8 * j + (z & 7)
    return jnp.where(source == lane, 1.0, 0.0).astype(bf16)


def sides_kernel(
    coords, features, occupancy, y_low, y_high, coords_out, gates, order, places, bricks, sems
):
    copies = [
        pltpu.make_async_copy(coords, places, sems.at[0]),
        pltpu.make_async_copy(occupancy, gates, sems.at[1]),
        pltpu.make_async_copy(features, bricks, sems.at[2]),
        pltpu.make_async_copy(coords, coords_out, sems.at[3]),
    ]
    for copy in copies:
        copy.start()
    choosers = [side_chooser(j) for j in (0, BRICK - 1)]
    for copy in copies:
        copy.wait()
    brick_order(places, order)
    for side, ty, picks in ((y_low, 0, choosers[0]), (y_high, TY - 1, choosers[1])):
        for tx in range(TX):
            first = (tx * TY + ty) * TZ
            source = [gated_brick(order[first + tz], bricks, gates) for tz in range(TZ)]
            cells = rows_dot(picks, jnp.concatenate(source, axis=1))
            side[8 * tx : 8 * tx + 8] = cells.reshape(8, SZ, LANES).astype(bf16)


def pack_sides(coords, features, occupancy):
    side = jax.ShapeDtypeStruct((SX, SZ, LANES), bf16)
    arrays = [pltpu.with_memory_space_constraint(a, pltpu.HBM) for a in (coords, features, occupancy)]
    return pl.pallas_call(
        sides_kernel,
        out_shape=(
            side,
            side,
            jax.ShapeDtypeStruct(coords.shape, jnp.int32),
            jax.ShapeDtypeStruct(occupancy.shape, jnp.int32),
        ),
        in_specs=[HBM] * 3,
        out_specs=(VMEM,) * 4,
        scratch_shapes=[
            pltpu.SMEM((16,), jnp.int32),
            pltpu.SMEM((3, 16), jnp.int32),
            pltpu.VMEM((16, C, 512), bf16),
            pltpu.SemaphoreType.DMA((4,)),
        ],
        compiler_params=params(12),
        name="pack_sides",
    )(*arrays)


def pack_kernel(coords, features, occupancy, act, order):
    brick_order(coords, order)
    picks = cell_chooser()
    for tx in range(TX):
        for ty in range(TY):
            first = (tx * TY + ty) * TZ
            halves = [gated_brick(order[first + tz], features, occupancy) for tz in range(TZ)]
            for h in range(4):
                lanes = slice(128 * h, 128 * h + 128)
                source = jnp.concatenate([half[:, lanes] for half in halves], axis=1)
                cells = rows_dot(picks, source).reshape(2, 4, 2, SZ, LANES)
                x = 8 * tx + 2 * h
                act[x : x + 2, 4 * ty : 4 * ty + 4] = cells.astype(bf16)


def pack(coords, features, occupancy):
    return pl.pallas_call(
        pack_kernel,
        out_shape=jax.ShapeDtypeStruct((SX, PAIRS, 2, SZ, LANES), bf16),
        in_specs=[SMEM, VMEM, VMEM],
        out_specs=VMEM,
        scratch_shapes=[pltpu.SMEM((16,), jnp.int32)],
        compiler_params=params(12),
        name="pack",
    )(coords, features, occupancy)


def face_kernel(act, y_before, y_after, low, high):
    tile_y = lax.axis_index("space") % GRID_Y
    for face, x in ((low, 0), (high, SX - 1)):
        face[0] = kept(y_before[x], tile_y > 0)
        face[1 : SY + 1] = act[x].reshape(SY, SZ, LANES)
        face[SY + 1] = kept(y_after[x], tile_y < GRID_Y - 1)


def faces(act, y_before, y_after):
    face = jax.ShapeDtypeStruct((SY + 2, SZ, LANES), bf16)
    return pl.pallas_call(
        face_kernel,
        out_shape=(face, face),
        in_specs=[VMEM] * 3,
        out_specs=(VMEM, VMEM),
        compiler_params=params(8),
        name="faces",
    )(act, y_before, y_after)


def window_forms(a, b, c, d):
    a, b, c, d = (cells.astype(f32) for cells in (a, b, c, d))
    lane = lax.broadcasted_iota(jnp.int32, a.shape, 2)
    b, c, d = pltpu.roll(b, 96, 2), pltpu.roll(c, 64, 2), pltpu.roll(d, 32, 2)
    wide = jnp.concatenate(
        [jnp.where(lane < 96, a, b), jnp.where(lane < 64, b, c), jnp.where(lane < 32, c, d)], axis=2
    ).reshape(PAIRS, 2, 8, WIDE)
    even, odd = wide[:, 0], wide[:, 1]
    place = lax.broadcasted_iota(jnp.int32, odd.shape, 1)
    before = jnp.where(place == 0, 0.0, pltpu.roll(odd, 1, 1))
    after = jnp.where(place == 7, 0.0, pltpu.roll(even, 7, 1))
    pairs = ((before, even), (even, odd), (odd, after))
    return [jnp.stack(pair, axis=1).reshape(PAIRS, SZ, WIDE).astype(bf16) for pair in pairs]


def kept(value, inside):
    return value * jnp.where(inside, 1.0, 0.0).astype(bf16)


def planes_dot(pieces, taps):
    rows = [piece.reshape(-1, WIDE) for piece in pieces]
    return plain_dot(jnp.concatenate(rows, axis=1), taps)


def mask_of(cells):
    return jnp.broadcast_to(cells[:, LANES - 1 :], cells.shape)


def rows_of(planes, parity):
    return jnp.concatenate(
        [plane[:, parity].reshape(PAIRS * SZ, LANES) for plane in planes], axis=0
    ).astype(f32)


def planes_mask(planes):
    return jnp.concatenate([mask_of(rows_of(planes, 0)), mask_of(rows_of(planes, 1))], axis=1)


def folded(row):
    return row[:, :LANES] + row[:, LANES:]


MID = SX - 2
STEP = 2
GROUP = 2


def merged(first, second):
    (mean0, square0, count0), (mean1, square1, count1) = first, second
    count = count0 + count1
    mean = (mean0 * count0 + mean1 * count1) / jnp.maximum(count, 1.0)
    square = square0 + square1 + count0 * (mean0 - mean) ** 2 + count1 * (mean1 - mean) ** 2
    return mean, square, count


def moments_of(value, mask):
    count = folded(jnp.sum(mask, axis=0, keepdims=True))
    mean = folded(jnp.sum(value * mask, axis=0, keepdims=True)) / jnp.maximum(count, 1.0)
    gap = (value - jnp.concatenate([mean, mean], axis=1)) * mask
    return mean, folded(jnp.sum(gap * gap, axis=0, keepdims=True)), count


def middle_kernel(act, y_before, y_after, weight, out, partial, stats, taps, grid):
    tile_y = lax.axis_index("space") % GRID_Y

    def fill(x):
        before = kept(y_before[x], tile_y > 0)[None]
        after = kept(y_after[x], tile_y < GRID_Y - 1)[None]
        plane = act[x]
        even, odd = plane[:, 0], plane[:, 1]
        forms = window_forms(
            jnp.concatenate([before, odd[:-1]], axis=0),
            even,
            odd,
            jnp.concatenate([even[1:], after], axis=0),
        )
        for c in range(3):
            grid[c, x] = forms[c]

    taps[...] = jnp.zeros(taps.shape, bf16)
    for a in range(3):
        for b in range(3):
            for c in range(3):
                for parity in range(2):
                    first = (a * 3 + c) * WIDE + (b + parity) * C
                    taps[first : first + C, parity * LANES : parity * LANES + C] = weight[(a * 3 + b) * 3 + c].T
    for x in range(STEP + 2):
        fill(x)
    pieces = [grid[c, a] for a in range(2) for c in range(3)]
    partial[0] = planes_dot(pieces, taps[3 * WIDE :])
    zero = jnp.zeros((1, LANES), f32)
    carry = (zero, zero, zero)
    for x in range(0, MID, STEP):
        for later in range(x + STEP + 2, min(x + 2 * STEP + 2, SX)):
            fill(later)
        pieces = [grid[c, x + a : x + a + STEP] for a in range(3) for c in range(3)]
        value = planes_dot(pieces, taps[...])
        out[x : x + STEP] = value.reshape(STEP, PAIRS * SZ, 2 * LANES)
        mask = planes_mask([act[x + 1 + step] for step in range(STEP)])
        carry = merged(carry, moments_of(value, mask))
    pieces = [grid[c, SX - 2 + a] for a in range(2) for c in range(3)]
    partial[1] = planes_dot(pieces, taps[: 6 * WIDE])
    stats[...] = jnp.concatenate(list(carry) + [jnp.zeros((5, LANES), f32)], axis=0)


def middle(act, y_before, y_after, weight):
    return pl.pallas_call(
        middle_kernel,
        out_shape=(
            pltpu.VMEM((MID, PAIRS * SZ, 2 * LANES), f32),
            jax.ShapeDtypeStruct((2, PAIRS * SZ, 2 * LANES), f32),
            jax.ShapeDtypeStruct((8, LANES), f32),
            jax.ShapeDtypeStruct((9 * WIDE, 2 * LANES), bf16),
        ),
        in_specs=[VMEM] * 4,
        out_specs=(VMEM,) * 4,
        scratch_shapes=[pltpu.VMEM((3, SX, PAIRS, SZ, WIDE), bf16)],
        compiler_params=params(26),
        name="middle",
    )(act, y_before, y_after, weight)


def edge_kernel(act, x_before, x_after, partial, taps, part, owners, out, stats):
    tile_x = lax.axis_index("space") // GRID_Y
    last_x = lax.axis_size("space") // GRID_Y - 1
    carry = (part[0:1], part[1:2], part[2:3])
    sides = ((x_before, tile_x > 0, 0, 0), (x_after, tile_x < last_x, 6 * WIDE, SX - 1))
    for index, (halo, inside, first, x) in enumerate(sides):
        cells = kept(halo[...], inside).reshape(PAIRS + 1, 2, SZ, LANES)
        forms = window_forms(cells[:-1, 0], cells[:-1, 1], cells[1:, 0], cells[1:, 1])
        value = partial[index] + planes_dot(forms, taps[first : first + 3 * WIDE])
        out[index] = value
        carry = merged(carry, moments_of(value, planes_mask([act[x]])))
    joint, square, both = carry
    lane = lax.broadcasted_iota(jnp.int32, (1, LANES), 1)
    joint = jnp.where(lane == LANES - 1, both, joint)
    for q in range(2):
        joint = jnp.where(lane == C + q, owners[q, 0].astype(f32), joint)
    row = jnp.concatenate([joint, square], axis=1)
    stats[...] = jnp.broadcast_to(row[None], stats.shape)


def edges(act, x_before, x_after, partial, taps, part, owners, devices):
    return pl.pallas_call(
        edge_kernel,
        out_shape=(
            jax.ShapeDtypeStruct((2, PAIRS * SZ, 2 * LANES), f32),
            jax.ShapeDtypeStruct((devices, 1, 2 * LANES), f32),
        ),
        in_specs=[VMEM] * 6 + [SMEM],
        out_specs=(VMEM, VMEM),
        compiler_params=params(16),
        name="edges",
    )(act, x_before, x_after, partial, taps, part, owners)


def joined(table, width):
    means, squares = table[:, :, :width], table[:, :, width:]
    counts = table[:, :, width - 1 : width]
    whole = jnp.sum(counts, axis=0)
    mean = jnp.sum(means * counts, axis=0) / whole
    gap = means - mean[None]
    return mean, jnp.sum(squares + counts * gap * gap, axis=0) / whole


def section_kernel(
    mid, edge, act, table, gain, shift, weight, sent, names, stats, taps, down, cover, lines
):
    level, groups = lax.axis_index("level"), lax.axis_size("level")
    for distance in range(4):
        origin = (level + groups - distance) % groups
        device = origin * lax.axis_size("space") + lax.axis_index("space")
        names[distance] = table[device][:, :LANES]
    mean, var = joined(table, LANES)
    lines[...] = jnp.zeros(lines.shape, f32)
    lines[0:1, :C] = gain[...]
    lines[1:2, :C] = shift[...]
    real = lax.broadcasted_iota(jnp.int32, (1, LANES), 1) < C
    scale = jnp.where(real, lines[0:1] / jnp.sqrt(var + epsilon), 0.0)
    mean = jnp.where(real, mean, 0.0)
    moved = lines[1:2] - mean * scale
    scale = jnp.concatenate([scale, scale], axis=1)
    moved = jnp.concatenate([moved, moved], axis=1)
    taps[...] = jnp.zeros(taps.shape, bf16)
    for a in range(2):
        for b in range(2):
            for c in range(2):
                first = ((a * 2 + c) * 2 + b) * LANES
                taps[first : first + C, :C2] = weight[(a * 2 + b) * 2 + c].T

    total = count = jnp.zeros((1, 2 * LANES), f32)
    for group in range(0, SX // 2, GROUP):
        blocks, coverings = [], []
        for X in range(group, group + GROUP):
            pieces, covers = [], []
            for a in range(2):
                x = 2 * X + a
                conv = edge[0] if x == 0 else edge[1] if x == SX - 1 else mid[x - 1]
                plane = act[x]
                even, odd = rows_of([plane], 0), rows_of([plane], 1)
                even_mask, odd_mask = mask_of(even), mask_of(odd)
                mask = jnp.concatenate([even_mask, odd_mask], axis=1)
                active = jnp.concatenate([even, odd], axis=1)
                section = active + mask * jnp.maximum(conv * scale + moved, 0.0)
                section = section.reshape(PAIRS, 2, 8, 2 * LANES)
                for c in range(2):
                    pieces.append(section[:, c].reshape(PAIRS * 8, 2 * LANES).astype(bf16))
                both = jnp.maximum(even_mask, odd_mask).reshape(PAIRS, 2, 8, LANES)
                covers.append(jnp.maximum(both[:, 0], both[:, 1]).reshape(PAIRS * 8, LANES))
            blocks.append(jnp.concatenate(pieces, axis=1))
            coverings.append(jnp.maximum(covers[0], covers[1]))
        value = plain_dot(jnp.concatenate(blocks, axis=0), taps[...])
        value = value.astype(bf16).astype(f32)
        covered = jnp.concatenate(coverings, axis=0)
        covered = jnp.concatenate([covered, covered], axis=1)
        down[group : group + GROUP] = value.reshape(GROUP, PAIRS * 8, 2 * LANES)
        cover[group : group + GROUP] = covered.reshape(GROUP, PAIRS * 8, 2 * LANES)
        total = total + jnp.sum(value * covered, axis=0, keepdims=True)
        count = count + jnp.sum(covered, axis=0, keepdims=True)

    zero = jnp.zeros((1, 2 * LANES), f32)
    mean2 = total / jnp.maximum(count, 1.0)

    def spread_out(X, carry):
        gap = (down[X] - mean2) * cover[X]
        return carry + jnp.sum(gap * gap, axis=0, keepdims=True)

    square = zero
    for X in range(SX // 2):
        square = spread_out(X, square)
    wide_lane = lax.broadcasted_iota(jnp.int32, (1, 2 * LANES), 1)
    row = jnp.concatenate([jnp.where(wide_lane == 2 * LANES - 1, count, mean2), square], axis=1)
    stats[...] = jnp.broadcast_to(row[None], stats.shape)

    half = PAIRS // 2 * 8
    for q in range(2):
        value = down[:, q * half : (q + 1) * half].reshape(SX // 2 * half, 2 * LANES)
        covered = cover[:, q * half : (q + 1) * half].reshape(SX // 2 * half, 2 * LANES)
        coded = jnp.where(covered > 0, value, EMPTY).astype(bf16)
        sent[q] = coded.T[:C2]


def section(mid, edge, act, table, gain, shift, weight, devices):
    return pl.pallas_call(
        section_kernel,
        out_shape=(
            jax.ShapeDtypeStruct((2, C2, 512), bf16),
            jax.ShapeDtypeStruct((4, 1, LANES), f32),
            jax.ShapeDtypeStruct((devices, 1, 4 * LANES), f32),
        ),
        in_specs=[VMEM] * 7,
        out_specs=(VMEM,) * 3,
        scratch_shapes=[
            pltpu.VMEM((8 * LANES, 2 * LANES), bf16),
            pltpu.VMEM((SX // 2, PAIRS * 8, 2 * LANES), f32),
            pltpu.VMEM((SX // 2, PAIRS * 8, 2 * LANES), f32),
            pltpu.VMEM((8, LANES), f32),
        ],
        compiler_params=params(20),
        name="section",
    )(mid, edge, act, table, gain, shift, weight)


def merge_kernel(table, near, back, out, up, down):
    width = 2 * LANES
    means, squares = table[:, :, :width], table[:, :, width:]
    counts = table[:, :, width - 1 : width]
    whole = jnp.sum(counts, axis=0)
    mean = jnp.sum(means * counts, axis=0) / jnp.maximum(whole, 1.0)
    gap = means - mean[None]
    square = jnp.sum(squares + counts * gap * gap, axis=0)
    lane = lax.broadcasted_iota(jnp.int32, (1, width), 1)
    row = jnp.concatenate([jnp.where(lane == width - 1, whole, mean), square], axis=1)
    out[...] = row[None]
    high = row.astype(bf16).astype(f32)
    middle = (row - high).astype(bf16).astype(f32)
    low = row - high - middle
    rows = jnp.concatenate([high, middle, low, jnp.zeros((13, 2 * width), f32)], axis=0).astype(bf16)
    for block, brick in ((up, near[0]), (down, back[1])):
        block[:C2] = brick
        block[C2:] = rows


def merge(table, near, back):
    block = jax.ShapeDtypeStruct((C2 + 16, 512), bf16)
    return pl.pallas_call(
        merge_kernel,
        out_shape=(jax.ShapeDtypeStruct((1, 1, 4 * LANES), f32), block, block),
        in_specs=[VMEM] * 3,
        out_specs=(VMEM,) * 3,
        compiler_params=params(8),
        name="merge",
    )(table, near, back)


def row_of(block):
    rows = block[C2:].astype(f32)
    return rows[0:1] + rows[1:2] + rows[2:3]


def settle_kernel(
    own, near, far0, far1, back, names, row_here, row_far, gain, shift, out, lines, ready, sems
):
    lines[...] = jnp.zeros(lines.shape, f32)
    rows = (row_here[0], row_of(far0), row_far[0], row_of(far1))
    table = jnp.concatenate([row[None] for row in rows], axis=0)
    mean, var = joined(table, 2 * LANES)
    lines[0:1] = mean
    lines[1:2] = var
    lines[2:3, :C2] = gain[...]
    lines[3:4, :C2] = shift[...]
    turned = lines[...].T[:C2]
    scale = turned[:, 2:3] / jnp.sqrt(turned[:, 1:2] + epsilon)
    moved = turned[:, 3:4] - turned[:, 0:1] * scale
    level = lax.axis_index("level")
    groups = lax.axis_size("level")
    copies = []
    sources = ((own[0], own[1]), (near[0], near[1]), (far0[:C2], far1[:C2]), (back[0], back[1]))
    for distance, (first, second) in enumerate(sources):
        origin = (level + groups - distance) % groups
        named = jnp.where(names[distance] == level.astype(f32), 1.0, 0.0)
        takes0, takes1 = named[:, C : C + 1], named[:, C + 1 : C + 2]
        value0 = jnp.maximum(first.astype(f32) * scale + moved, 0.0)
        value1 = jnp.maximum(second.astype(f32) * scale + moved, 0.0)
        chosen = (
            jnp.where(takes0 > 0, value0, jnp.where(takes1 > 0, value1, 0.0)),
            jnp.where(takes0 * takes1 > 0, value1, 0.0),
        )
        for k in range(CAPC):
            slot = distance * CAPC + k
            ready[slot] = chosen[k].astype(bf16)
            copies.append(
                pltpu.make_async_copy(ready.at[slot], out.at[origin * CAPC + k], sems.at[slot])
            )
            copies[-1].start()
    for copy in copies:
        copy.wait()


def settle(rows, names, tables, gain, shift):
    return pl.pallas_call(
        settle_kernel,
        out_shape=jax.ShapeDtypeStruct((8, C2, 512), bf16),
        in_specs=[VMEM] * 10,
        out_specs=HBM,
        scratch_shapes=[
            pltpu.VMEM((8, 2 * LANES), f32),
            pltpu.VMEM((8, C2, 512), bf16),
            pltpu.SemaphoreType.DMA((8,)),
        ],
        compiler_params=params(12),
        name="settle",
    )(*rows, names, *tables, gain, shift)


def to_all(rows, axes):
    return lax.all_to_all(rows, axes, 0, 0, tiled=True)


def shards(
    features,
    occupancy,
    brick_coords,
    coarse_owner,
    conv_weight,
    conv_gain,
    conv_shift,
    reduce_weight,
    down_gain,
    down_shift,
):
    space_count = lax.axis_size("space")
    level_count = lax.axis_size("level")
    grid_x = space_count // GRID_Y

    def from_tile(block, step_x, step_y):
        route = []
        for s in range(space_count):
            x, y = s // GRID_Y, s % GRID_Y
            route.append(((x + step_x) % grid_x * GRID_Y + (y + step_y) % GRID_Y, s))
        return lax.ppermute(block, "space", route)

    y_low, y_high, coords, gates = pack_sides(brick_coords, features, occupancy)
    y_before = from_tile(y_high, 0, -1)
    y_after = from_tile(y_low, 0, 1)
    act = pack(coords, features, gates)
    x_low, x_high = faces(act, y_before, y_after)
    x_before = from_tile(x_high, -1, 0)
    x_after = from_tile(x_low, 1, 0)
    mid, partial, part, taps = middle(act, y_before, y_after, conv_weight)
    edge, stats = edges(
        act,
        x_before,
        x_after,
        partial,
        taps,
        part,
        coarse_owner,
        space_count * level_count,
    )
    sent, names, stats2 = section(
        mid,
        edge,
        act,
        to_all(stats, ("level", "space")),
        conv_gain[None],
        conv_shift[None],
        reduce_weight,
        space_count,
    )
    def up_level(block, distance):
        route = [(g, (g + distance) % level_count) for g in range(level_count)]
        return lax.ppermute(block, "level", route)

    near = up_level(sent, 1)
    back = up_level(sent, -1)
    here, up, down = merge(to_all(stats2, "space"), near, back)
    tables = [here, up_level(here, 2)]
    far0 = up_level(up, 1)
    far1 = up_level(down, -1)
    return settle(
        (sent, near, far0, far1, back), names, tables, down_gain[None], down_shift[None]
    )


def solution(mesh):
    in_specs = (
        P(("level", "space"), None, None),
        P(("level", "space"), None),
        P(None, ("level", "space")),
        P(("level", "space"), None),
        P(),
        P(),
        P(),
        P(),
        P(),
        P(),
    )
    out_specs = P(("level", "space"), None, None)
    return jax.shard_map(shards, mesh=mesh, in_specs=in_specs, out_specs=out_specs, check_vma=False)
```

```python
import functools

import jax
import jax.numpy as jnp
from jax import lax
from jax.experimental import pallas as pl
from jax.experimental.pallas import tpu as pltpu
from jax.sharding import PartitionSpec as P

BRICK = 8
TX = 2
TY = 4
TZ = 2
CAPC = 2
C = 96
C2 = 192
LANES = 128
SX = TX * BRICK
SY = TY * BRICK
SZ = TZ * BRICK
PAIRS = SY // 2
WIDE = 4 * C
GRID_Y = 4
EMPTY = -3e38
epsilon = 1e-05

bf16 = jnp.bfloat16
f32 = jnp.float32
VMEM = pl.BlockSpec(memory_space=pltpu.VMEM)
SMEM = pl.BlockSpec(memory_space=pltpu.SMEM)
HBM = pl.BlockSpec(memory_space=pltpu.HBM)


def params(mib=56):
    return pltpu.CompilerParams(vmem_limit_bytes=mib << 20)


def cell_chooser():
    row = lax.broadcasted_iota(jnp.int32, (256, 256), 0)
    lane = lax.broadcasted_iota(jnp.int32, (256, 256), 1)
    z = 2 * (row & 7) + ((row >> 3) & 1)
    source = ((z >> 3) << 7) + ((row >> 4) << 3) + (z & 7)
    return jnp.where(source == lane, 1.0, 0.0).astype(bf16)


def rows_dot(left, right):
    return lax.dot_general(left, right, (((1,), (1,)), ((), ())), preferred_element_type=f32)


def plain_dot(left, right):
    return lax.dot_general(left, right, (((1,), (0,)), ((), ())), preferred_element_type=f32)


def brick_order(coords, order):
    for n in range(16):
        place = ((coords[0, n] % TX) * TY + coords[1, n] % TY) * TZ + coords[2, n]
        order[place] = n


def gated_brick(n, features, occupancy):
    gate = occupancy[pl.ds(n, 1), :].astype(f32)
    gate = jnp.broadcast_to(gate, (LANES, 512)).astype(bf16)
    return jnp.concatenate([features[n] * gate[:C], gate[C:]], axis=0)


def side_chooser(j):
    row = lax.broadcasted_iota(jnp.int32, (128, 1024), 0)
    lane = lax.broadcasted_iota(jnp.int32, (128, 1024), 1)
    z = 2 * (row & 7) + ((row >> 3) & 1)
    source = ((z >> 3) << 9) + ((row >> 4) << 6) + 8 * j + (z & 7)
    return jnp.where(source == lane, 1.0, 0.0).astype(bf16)


def sides_kernel(
    coords, features, occupancy, y_low, y_high, coords_out, gates, order, places, bricks, sems
):
    copies = [
        pltpu.make_async_copy(coords, places, sems.at[0]),
        pltpu.make_async_copy(occupancy, gates, sems.at[1]),
        pltpu.make_async_copy(features, bricks, sems.at[2]),
        pltpu.make_async_copy(coords, coords_out, sems.at[3]),
    ]
    for copy in copies:
        copy.start()
    choosers = [side_chooser(j) for j in (0, BRICK - 1)]
    for copy in copies:
        copy.wait()
    brick_order(places, order)
    for side, ty, picks in ((y_low, 0, choosers[0]), (y_high, TY - 1, choosers[1])):
        for tx in range(TX):
            first = (tx * TY + ty) * TZ
            source = [gated_brick(order[first + tz], bricks, gates) for tz in range(TZ)]
            cells = rows_dot(picks, jnp.concatenate(source, axis=1))
            side[8 * tx : 8 * tx + 8] = cells.reshape(8, SZ, LANES).astype(bf16)


def pack_sides(coords, features, occupancy):
    side = jax.ShapeDtypeStruct((SX, SZ, LANES), bf16)
    arrays = [pltpu.with_memory_space_constraint(a, pltpu.HBM) for a in (coords, features, occupancy)]
    return pl.pallas_call(
        sides_kernel,
        out_shape=(
            side,
            side,
            jax.ShapeDtypeStruct(coords.shape, jnp.int32),
            jax.ShapeDtypeStruct(occupancy.shape, jnp.int32),
        ),
        in_specs=[HBM] * 3,
        out_specs=(VMEM,) * 4,
        scratch_shapes=[
            pltpu.SMEM((16,), jnp.int32),
            pltpu.SMEM((3, 16), jnp.int32),
            pltpu.VMEM((16, C, 512), bf16),
            pltpu.SemaphoreType.DMA((4,)),
        ],
        compiler_params=params(12),
        name="pack_sides",
    )(*arrays)


def pack_kernel(coords, features, occupancy, act, masks, cover, order):
    brick_order(coords, order)
    picks = cell_chooser()
    for tx in range(TX):
        for ty in range(TY):
            first = (tx * TY + ty) * TZ
            halves = [gated_brick(order[first + tz], features, occupancy) for tz in range(TZ)]
            for h in range(4):
                lanes = slice(128 * h, 128 * h + 128)
                source = jnp.concatenate([half[:, lanes] for half in halves], axis=1)
                cells = rows_dot(picks, source).reshape(2, 4, 2, SZ, LANES)
                x = 8 * tx + 2 * h
                act[x : x + 2, 4 * ty : 4 * ty + 4] = cells.astype(bf16)
    for X in range(SX // 2):
        covers = []
        for x in (2 * X, 2 * X + 1):
            even, odd = mask_of(rows_of([act[x]], 0)), mask_of(rows_of([act[x]], 1))
            masks[x] = jnp.concatenate([even, odd], axis=1).astype(bf16)
            both = jnp.maximum(even, odd).reshape(PAIRS, 2, 8, LANES)
            covers.append(jnp.maximum(both[:, 0], both[:, 1]).reshape(PAIRS * 8, LANES))
        covered = jnp.maximum(covers[0], covers[1])
        cover[X] = jnp.concatenate([covered, covered], axis=1)


def pack(coords, features, occupancy):
    return pl.pallas_call(
        pack_kernel,
        out_shape=(
            jax.ShapeDtypeStruct((SX, PAIRS, 2, SZ, LANES), bf16),
            jax.ShapeDtypeStruct((SX, PAIRS * SZ, 2 * LANES), bf16),
            jax.ShapeDtypeStruct((SX // 2, PAIRS * 8, 2 * LANES), f32),
        ),
        in_specs=[SMEM, VMEM, VMEM],
        out_specs=(VMEM,) * 3,
        scratch_shapes=[pltpu.SMEM((16,), jnp.int32)],
        compiler_params=params(12),
        name="pack",
    )(coords, features, occupancy)


def face_kernel(act, y_before, y_after, low, high):
    tile_y = lax.axis_index("space") % GRID_Y
    for face, x in ((low, 0), (high, SX - 1)):
        face[0] = kept(y_before[x], tile_y > 0)
        face[1 : SY + 1] = act[x].reshape(SY, SZ, LANES)
        face[SY + 1] = kept(y_after[x], tile_y < GRID_Y - 1)


def faces(act, y_before, y_after):
    face = jax.ShapeDtypeStruct((SY + 2, SZ, LANES), bf16)
    return pl.pallas_call(
        face_kernel,
        out_shape=(face, face),
        in_specs=[VMEM] * 3,
        out_specs=(VMEM, VMEM),
        compiler_params=params(8),
        name="faces",
    )(act, y_before, y_after)


def window_forms(a, b, c, d):
    a, b, c, d = (cells.astype(f32) for cells in (a, b, c, d))
    lane = lax.broadcasted_iota(jnp.int32, a.shape, 2)
    b, c, d = pltpu.roll(b, 96, 2), pltpu.roll(c, 64, 2), pltpu.roll(d, 32, 2)
    wide = jnp.concatenate(
        [jnp.where(lane < 96, a, b), jnp.where(lane < 64, b, c), jnp.where(lane < 32, c, d)], axis=2
    ).reshape(PAIRS, 2, 8, WIDE)
    even, odd = wide[:, 0], wide[:, 1]
    place = lax.broadcasted_iota(jnp.int32, odd.shape, 1)
    before = jnp.where(place == 0, 0.0, pltpu.roll(odd, 1, 1))
    after = jnp.where(place == 7, 0.0, pltpu.roll(even, 7, 1))
    pairs = ((before, even), (even, odd), (odd, after))
    return [jnp.stack(pair, axis=1).reshape(PAIRS, SZ, WIDE).astype(bf16) for pair in pairs]


def kept(value, inside):
    return value * jnp.where(inside, 1.0, 0.0).astype(bf16)


def planes_dot(pieces, taps):
    rows = [piece.reshape(-1, WIDE) for piece in pieces]
    return plain_dot(jnp.concatenate(rows, axis=1), taps)


def mask_of(cells):
    return jnp.broadcast_to(cells[:, LANES - 1 :], cells.shape)


def rows_of(planes, parity):
    return jnp.concatenate(
        [plane[:, parity].reshape(PAIRS * SZ, LANES) for plane in planes], axis=0
    ).astype(f32)


def folded(row):
    return row[:, :LANES] + row[:, LANES:]


MID = SX - 2
STEP = 2
GROUP = 2


def merged(first, second):
    (mean0, square0, count0), (mean1, square1, count1) = first, second
    count = count0 + count1
    mean = (mean0 * count0 + mean1 * count1) / jnp.maximum(count, 1.0)
    square = square0 + square1 + count0 * (mean0 - mean) ** 2 + count1 * (mean1 - mean) ** 2
    return mean, square, count


def moments_of(value, mask):
    count = folded(jnp.sum(mask, axis=0, keepdims=True))
    mean = folded(jnp.sum(value * mask, axis=0, keepdims=True)) / jnp.maximum(count, 1.0)
    gap = (value - jnp.concatenate([mean, mean], axis=1)) * mask
    return mean, folded(jnp.sum(gap * gap, axis=0, keepdims=True)), count


def middle_kernel(act, masks, y_before, y_after, weight, out, partial, stats, taps, grid):
    tile_y = lax.axis_index("space") % GRID_Y

    def fill(x):
        before = kept(y_before[x], tile_y > 0)[None]
        after = kept(y_after[x], tile_y < GRID_Y - 1)[None]
        plane = act[x]
        even, odd = plane[:, 0], plane[:, 1]
        forms = window_forms(
            jnp.concatenate([before, odd[:-1]], axis=0),
            even,
            odd,
            jnp.concatenate([even[1:], after], axis=0),
        )
        for c in range(3):
            grid[c, x] = forms[c]

    taps[...] = jnp.zeros(taps.shape, bf16)
    for a in range(3):
        for b in range(3):
            for c in range(3):
                for parity in range(2):
                    first = (a * 3 + c) * WIDE + (b + parity) * C
                    taps[first : first + C, parity * LANES : parity * LANES + C] = weight[(a * 3 + b) * 3 + c].T
    for x in range(STEP + 2):
        fill(x)
    pieces = [grid[c, a] for a in range(2) for c in range(3)]
    partial[0] = planes_dot(pieces, taps[3 * WIDE :])
    zero = jnp.zeros((1, LANES), f32)
    carry = (zero, zero, zero)
    for x in range(0, MID, STEP):
        for later in range(x + STEP + 2, min(x + 2 * STEP + 2, SX)):
            fill(later)
        pieces = [grid[c, x + a : x + a + STEP] for a in range(3) for c in range(3)]
        value = planes_dot(pieces, taps[...])
        out[x : x + STEP] = value.reshape(STEP, PAIRS * SZ, 2 * LANES)
        mask = masks[x + 1 : x + 1 + STEP].reshape(STEP * PAIRS * SZ, 2 * LANES).astype(f32)
        carry = merged(carry, moments_of(value, mask))
    pieces = [grid[c, SX - 2 + a] for a in range(2) for c in range(3)]
    partial[1] = planes_dot(pieces, taps[: 6 * WIDE])
    stats[...] = jnp.concatenate(list(carry) + [jnp.zeros((5, LANES), f32)], axis=0)


def middle(act, masks, y_before, y_after, weight):
    return pl.pallas_call(
        middle_kernel,
        out_shape=(
            pltpu.VMEM((MID, PAIRS * SZ, 2 * LANES), f32),
            jax.ShapeDtypeStruct((2, PAIRS * SZ, 2 * LANES), f32),
            jax.ShapeDtypeStruct((8, LANES), f32),
            jax.ShapeDtypeStruct((9 * WIDE, 2 * LANES), bf16),
        ),
        in_specs=[VMEM] * 5,
        out_specs=(VMEM,) * 4,
        scratch_shapes=[pltpu.VMEM((3, SX, PAIRS, SZ, WIDE), bf16)],
        compiler_params=params(26),
        name="middle",
    )(act, masks, y_before, y_after, weight)


def edge_kernel(masks, x_before, x_after, partial, taps, part, owners, out, stats):
    tile_x = lax.axis_index("space") // GRID_Y
    last_x = lax.axis_size("space") // GRID_Y - 1
    carry = (part[0:1], part[1:2], part[2:3])
    sides = ((x_before, tile_x > 0, 0, 0), (x_after, tile_x < last_x, 6 * WIDE, SX - 1))
    for index, (halo, inside, first, x) in enumerate(sides):
        cells = kept(halo[...], inside).reshape(PAIRS + 1, 2, SZ, LANES)
        forms = window_forms(cells[:-1, 0], cells[:-1, 1], cells[1:, 0], cells[1:, 1])
        value = partial[index] + planes_dot(forms, taps[first : first + 3 * WIDE])
        out[index] = value
        carry = merged(carry, moments_of(value, masks[x].astype(f32)))
    joint, square, both = carry
    lane = lax.broadcasted_iota(jnp.int32, (1, LANES), 1)
    joint = jnp.where(lane == LANES - 1, both, joint)
    for q in range(2):
        joint = jnp.where(lane == C + q, owners[0, q].astype(f32), joint)
    row = jnp.concatenate([joint, square], axis=1)
    stats[...] = jnp.broadcast_to(row[None], stats.shape)


def edges(masks, x_before, x_after, partial, taps, part, owners, devices):
    return pl.pallas_call(
        edge_kernel,
        out_shape=(
            jax.ShapeDtypeStruct((2, PAIRS * SZ, 2 * LANES), f32),
            jax.ShapeDtypeStruct((devices, 1, 2 * LANES), f32),
        ),
        in_specs=[VMEM] * 6 + [SMEM],
        out_specs=(VMEM, VMEM),
        compiler_params=params(16),
        name="edges",
    )(masks, x_before, x_after, partial, taps, part, owners)


def joined(table, width):
    means, squares = table[:, :, :width], table[:, :, width:]
    counts = table[:, :, width - 1 : width]
    whole = jnp.sum(counts, axis=0)
    mean = jnp.sum(means * counts, axis=0) / whole
    gap = means - mean[None]
    return mean, jnp.sum(squares + counts * gap * gap, axis=0) / whole


def section_kernel(
    mid, edge, act, table, gain, shift, weight, masks, cover, sent, names, stats, taps, down, lines
):
    level, groups = lax.axis_index("level"), lax.axis_size("level")
    for distance in range(4):
        origin = (level + groups - distance) % groups
        device = origin * lax.axis_size("space") + lax.axis_index("space")
        names[distance] = table[device][:, :LANES]
    mean, var = joined(table, LANES)
    lines[...] = jnp.zeros(lines.shape, f32)
    lines[0:1, :C] = gain[...]
    lines[1:2, :C] = shift[...]
    real = lax.broadcasted_iota(jnp.int32, (1, LANES), 1) < C
    scale = jnp.where(real, lines[0:1] / jnp.sqrt(var + epsilon), 0.0)
    mean = jnp.where(real, mean, 0.0)
    moved = lines[1:2] - mean * scale
    scale = jnp.concatenate([scale, scale], axis=1)
    moved = jnp.concatenate([moved, moved], axis=1)
    taps[...] = jnp.zeros(taps.shape, bf16)
    for a in range(2):
        for b in range(2):
            for c in range(2):
                first = ((a * 2 + c) * 2 + b) * LANES
                taps[first : first + C, :C2] = weight[(a * 2 + b) * 2 + c].T

    total = count = jnp.zeros((1, 2 * LANES), f32)
    for group in range(0, SX // 2, GROUP):
        blocks = []
        for X in range(group, group + GROUP):
            pieces = []
            for x in (2 * X, 2 * X + 1):
                conv = edge[0] if x == 0 else edge[1] if x == SX - 1 else mid[x - 1]
                active = jnp.concatenate([rows_of([act[x]], 0), rows_of([act[x]], 1)], axis=1)
                gained = masks[x].astype(f32) * jnp.maximum(conv * scale + moved, 0.0)
                section = (active + gained).reshape(PAIRS, 2, 8, 2 * LANES)
                for c in range(2):
                    pieces.append(section[:, c].reshape(PAIRS * 8, 2 * LANES).astype(bf16))
            blocks.append(jnp.concatenate(pieces, axis=1))
        value = plain_dot(jnp.concatenate(blocks, axis=0), taps[...])
        value = value.astype(bf16).astype(f32)
        covered = cover[group : group + GROUP].reshape(GROUP * PAIRS * 8, 2 * LANES)
        down[group : group + GROUP] = value.reshape(GROUP, PAIRS * 8, 2 * LANES)
        total = total + jnp.sum(value * covered, axis=0, keepdims=True)
        count = count + jnp.sum(covered, axis=0, keepdims=True)

    zero = jnp.zeros((1, 2 * LANES), f32)
    mean2 = total / jnp.maximum(count, 1.0)

    def spread_out(X, carry):
        gap = (down[X] - mean2) * cover[X]
        return carry + jnp.sum(gap * gap, axis=0, keepdims=True)

    square = zero
    for X in range(SX // 2):
        square = spread_out(X, square)
    wide_lane = lax.broadcasted_iota(jnp.int32, (1, 2 * LANES), 1)
    row = jnp.concatenate([jnp.where(wide_lane == 2 * LANES - 1, count, mean2), square], axis=1)
    stats[...] = jnp.broadcast_to(row[None], stats.shape)

    half = PAIRS // 2 * 8
    for q in range(2):
        value = down[:, q * half : (q + 1) * half].reshape(SX // 2 * half, 2 * LANES)
        covered = cover[:, q * half : (q + 1) * half].reshape(SX // 2 * half, 2 * LANES)
        coded = jnp.where(covered > 0, value, EMPTY).astype(bf16)
        sent[q] = coded.T[:C2]


def section(mid, edge, act, table, gain, shift, weight, masks, cover, devices):
    return pl.pallas_call(
        section_kernel,
        out_shape=(
            jax.ShapeDtypeStruct((2, C2, 512), bf16),
            jax.ShapeDtypeStruct((4, 1, LANES), f32),
            jax.ShapeDtypeStruct((devices, 1, 4 * LANES), f32),
        ),
        in_specs=[VMEM] * 9,
        out_specs=(VMEM,) * 3,
        scratch_shapes=[
            pltpu.VMEM((8 * LANES, 2 * LANES), bf16),
            pltpu.VMEM((SX // 2, PAIRS * 8, 2 * LANES), f32),
            pltpu.VMEM((8, LANES), f32),
        ],
        compiler_params=params(20),
        name="section",
    )(mid, edge, act, table, gain, shift, weight, masks, cover)


def merge_kernel(table, near, back, out, up, down):
    width = 2 * LANES
    means, squares = table[:, :, :width], table[:, :, width:]
    counts = table[:, :, width - 1 : width]
    whole = jnp.sum(counts, axis=0)
    mean = jnp.sum(means * counts, axis=0) / jnp.maximum(whole, 1.0)
    gap = means - mean[None]
    square = jnp.sum(squares + counts * gap * gap, axis=0)
    lane = lax.broadcasted_iota(jnp.int32, (1, width), 1)
    row = jnp.concatenate([jnp.where(lane == width - 1, whole, mean), square], axis=1)
    out[...] = row[None]
    high = row.astype(bf16).astype(f32)
    middle = (row - high).astype(bf16).astype(f32)
    low = row - high - middle
    rows = jnp.concatenate([high, middle, low, jnp.zeros((13, 2 * width), f32)], axis=0).astype(bf16)
    for block, brick in ((up, near[0]), (down, back[1])):
        block[:C2] = brick
        block[C2:] = rows


def merge(table, near, back):
    block = jax.ShapeDtypeStruct((C2 + 16, 512), bf16)
    return pl.pallas_call(
        merge_kernel,
        out_shape=(jax.ShapeDtypeStruct((1, 1, 4 * LANES), f32), block, block),
        in_specs=[VMEM] * 3,
        out_specs=(VMEM,) * 3,
        compiler_params=params(8),
        name="merge",
    )(table, near, back)


def row_of(block):
    rows = block[C2:].astype(f32)
    return rows[0:1] + rows[1:2] + rows[2:3]


def settle_kernel(
    own, near, far0, far1, back, names, row_here, row_far, gain, shift, out, lines, ready, sems
):
    lines[...] = jnp.zeros(lines.shape, f32)
    rows = (row_here[0], row_of(far0), row_far[0], row_of(far1))
    table = jnp.concatenate([row[None] for row in rows], axis=0)
    mean, var = joined(table, 2 * LANES)
    lines[0:1] = mean
    lines[1:2] = var
    lines[2:3, :C2] = gain[...]
    lines[3:4, :C2] = shift[...]
    turned = lines[...].T[:C2]
    scale = turned[:, 2:3] / jnp.sqrt(turned[:, 1:2] + epsilon)
    moved = turned[:, 3:4] - turned[:, 0:1] * scale
    level = lax.axis_index("level")
    groups = lax.axis_size("level")
    copies = []
    sources = ((own[0], own[1]), (near[0], near[1]), (far0[:C2], far1[:C2]), (back[0], back[1]))
    for distance, (first, second) in enumerate(sources):
        origin = (level + groups - distance) % groups
        named = jnp.where(names[distance] == level.astype(f32), 1.0, 0.0)
        takes0, takes1 = named[:, C : C + 1], named[:, C + 1 : C + 2]
        value0 = jnp.maximum(first.astype(f32) * scale + moved, 0.0)
        value1 = jnp.maximum(second.astype(f32) * scale + moved, 0.0)
        chosen = (
            jnp.where(takes0 > 0, value0, jnp.where(takes1 > 0, value1, 0.0)),
            jnp.where(takes0 * takes1 > 0, value1, 0.0),
        )
        for k in range(CAPC):
            slot = distance * CAPC + k
            ready[slot] = chosen[k].astype(bf16)
            copies.append(
                pltpu.make_async_copy(ready.at[slot], out.at[origin * CAPC + k], sems.at[slot])
            )
            copies[-1].start()
    for copy in copies:
        copy.wait()


def settle(rows, names, tables, gain, shift):
    return pl.pallas_call(
        settle_kernel,
        out_shape=jax.ShapeDtypeStruct((8, C2, 512), bf16),
        in_specs=[VMEM] * 10,
        out_specs=HBM,
        scratch_shapes=[
            pltpu.VMEM((8, 2 * LANES), f32),
            pltpu.VMEM((8, C2, 512), bf16),
            pltpu.SemaphoreType.DMA((8,)),
        ],
        compiler_params=params(12),
        name="settle",
    )(*rows, names, *tables, gain, shift)


def to_all(rows, axes):
    return lax.all_to_all(rows, axes, 0, 0, tiled=True)


def shards(
    features,
    occupancy,
    brick_coords,
    coarse_owner,
    conv_weight,
    conv_gain,
    conv_shift,
    reduce_weight,
    down_gain,
    down_shift,
):
    space_count = lax.axis_size("space")
    level_count = lax.axis_size("level")
    grid_x = space_count // GRID_Y

    def from_tile(block, step_x, step_y):
        route = []
        for s in range(space_count):
            x, y = s // GRID_Y, s % GRID_Y
            route.append(((x + step_x) % grid_x * GRID_Y + (y + step_y) % GRID_Y, s))
        return lax.ppermute(block, "space", route)

    y_low, y_high, coords, gates = pack_sides(brick_coords, features, occupancy)
    y_before = from_tile(y_high, 0, -1)
    y_after = from_tile(y_low, 0, 1)
    act, masks, cover = pack(coords, features, gates)
    x_low, x_high = faces(act, y_before, y_after)
    x_before = from_tile(x_high, -1, 0)
    x_after = from_tile(x_low, 1, 0)
    mid, partial, part, taps = middle(act, masks, y_before, y_after, conv_weight)
    edge, stats = edges(
        masks,
        x_before,
        x_after,
        partial,
        taps,
        part,
        coarse_owner.reshape(1, 2),
        space_count * level_count,
    )
    sent, names, stats2 = section(
        mid,
        edge,
        act,
        to_all(stats, ("level", "space")),
        conv_gain[None],
        conv_shift[None],
        reduce_weight,
        masks,
        cover,
        space_count,
    )
    def up_level(block, distance):
        route = [(g, (g + distance) % level_count) for g in range(level_count)]
        return lax.ppermute(block, "level", route)

    near = up_level(sent, 1)
    back = up_level(sent, -1)
    here, up, down = merge(to_all(stats2, "space"), near, back)
    tables = [here, up_level(here, 2)]
    far0 = up_level(up, 1)
    far1 = up_level(down, -1)
    return settle(
        (sent, near, far0, far1, back), names, tables, down_gain[None], down_shift[None]
    )


def solution(mesh):
    in_specs = (
        P(("level", "space"), None, None),
        P(("level", "space"), None),
        P(None, ("level", "space")),
        P(("level", "space"), None),
        P(),
        P(),
        P(),
        P(),
        P(),
        P(),
    )
    out_specs = P(("level", "space"), None, None)
    return jax.shard_map(shards, mesh=mesh, in_specs=in_specs, out_specs=out_specs, check_vma=False)
```

```python
import functools

import jax
import jax.numpy as jnp
from jax import lax
from jax.experimental import pallas as pl
from jax.experimental.pallas import tpu as pltpu
from jax.sharding import PartitionSpec as P

BRICK = 8
TX = 2
TY = 4
TZ = 2
CAPC = 2
C = 96
C2 = 192
LANES = 128
SX = TX * BRICK
SY = TY * BRICK
SZ = TZ * BRICK
PAIRS = SY // 2
WIDE = 4 * C
GRID_Y = 4
EMPTY = -3e38
epsilon = 1e-05

bf16 = jnp.bfloat16
f32 = jnp.float32
VMEM = pl.BlockSpec(memory_space=pltpu.VMEM)
SMEM = pl.BlockSpec(memory_space=pltpu.SMEM)
HBM = pl.BlockSpec(memory_space=pltpu.HBM)


def params(mib=56):
    return pltpu.CompilerParams(vmem_limit_bytes=mib << 20)


def cell_chooser():
    row = lax.broadcasted_iota(jnp.int32, (256, 256), 0)
    lane = lax.broadcasted_iota(jnp.int32, (256, 256), 1)
    z = 2 * (row & 7) + ((row >> 3) & 1)
    source = ((z >> 3) << 7) + ((row >> 4) << 3) + (z & 7)
    return jnp.where(source == lane, 1.0, 0.0).astype(bf16)


def rows_dot(left, right):
    return lax.dot_general(left, right, (((1,), (1,)), ((), ())), preferred_element_type=f32)


def plain_dot(left, right):
    return lax.dot_general(left, right, (((1,), (0,)), ((), ())), preferred_element_type=f32)


def brick_order(coords, order):
    for n in range(16):
        place = ((coords[0, n] % TX) * TY + coords[1, n] % TY) * TZ + coords[2, n]
        order[place] = n


def gated_brick(n, features, occupancy):
    gate = occupancy[pl.ds(n, 1), :].astype(f32)
    gate = jnp.broadcast_to(gate, (LANES, 512)).astype(bf16)
    return jnp.concatenate([features[n] * gate[:C], gate[C:]], axis=0)


def side_chooser(j):
    row = lax.broadcasted_iota(jnp.int32, (128, 1024), 0)
    lane = lax.broadcasted_iota(jnp.int32, (128, 1024), 1)
    z = 2 * (row & 7) + ((row >> 3) & 1)
    source = ((z >> 3) << 9) + ((row >> 4) << 6) + 8 * j + (z & 7)
    return jnp.where(source == lane, 1.0, 0.0).astype(bf16)


def sides_kernel(
    coords, features, occupancy, y_low, y_high, coords_out, gates, order, places, bricks, sems
):
    copies = [
        pltpu.make_async_copy(coords, places, sems.at[0]),
        pltpu.make_async_copy(occupancy, gates, sems.at[1]),
        pltpu.make_async_copy(features, bricks, sems.at[2]),
        pltpu.make_async_copy(coords, coords_out, sems.at[3]),
    ]
    for copy in copies:
        copy.start()
    choosers = [side_chooser(j) for j in (0, BRICK - 1)]
    for copy in copies:
        copy.wait()
    brick_order(places, order)
    for side, ty, picks in ((y_low, 0, choosers[0]), (y_high, TY - 1, choosers[1])):
        for tx in range(TX):
            first = (tx * TY + ty) * TZ
            source = [gated_brick(order[first + tz], bricks, gates) for tz in range(TZ)]
            cells = rows_dot(picks, jnp.concatenate(source, axis=1))
            side[8 * tx : 8 * tx + 8] = cells.reshape(8, SZ, LANES).astype(bf16)


def pack_sides(coords, features, occupancy):
    side = jax.ShapeDtypeStruct((SX, SZ, LANES), bf16)
    arrays = [pltpu.with_memory_space_constraint(a, pltpu.HBM) for a in (coords, features, occupancy)]
    return pl.pallas_call(
        sides_kernel,
        out_shape=(
            side,
            side,
            jax.ShapeDtypeStruct(coords.shape, jnp.int32),
            jax.ShapeDtypeStruct(occupancy.shape, jnp.int32),
        ),
        in_specs=[HBM] * 3,
        out_specs=(VMEM,) * 4,
        scratch_shapes=[
            pltpu.SMEM((16,), jnp.int32),
            pltpu.SMEM((3, 16), jnp.int32),
            pltpu.VMEM((16, C, 512), bf16),
            pltpu.SemaphoreType.DMA((4,)),
        ],
        compiler_params=params(12),
        name="pack_sides",
    )(*arrays)


def pack_kernel(coords, features, occupancy, act, masks, cover, order):
    brick_order(coords, order)
    picks = cell_chooser()
    for tx in range(TX):
        for ty in range(TY):
            first = (tx * TY + ty) * TZ
            halves = [gated_brick(order[first + tz], features, occupancy) for tz in range(TZ)]
            for h in range(4):
                lanes = slice(128 * h, 128 * h + 128)
                source = jnp.concatenate([half[:, lanes] for half in halves], axis=1)
                cells = rows_dot(picks, source).reshape(2, 4, 2, SZ, LANES)
                x = 8 * tx + 2 * h
                act[x : x + 2, 4 * ty : 4 * ty + 4] = cells.astype(bf16)
    for X in range(SX // 2):
        covers = []
        for x in (2 * X, 2 * X + 1):
            even, odd = mask_of(rows_of([act[x]], 0)), mask_of(rows_of([act[x]], 1))
            masks[x] = jnp.concatenate([even, odd], axis=1).astype(bf16)
            both = jnp.maximum(even, odd).reshape(PAIRS, 2, 8, LANES)
            covers.append(jnp.maximum(both[:, 0], both[:, 1]).reshape(PAIRS * 8, LANES))
        covered = jnp.maximum(covers[0], covers[1])
        cover[X] = jnp.concatenate([covered, covered], axis=1)


def pack(coords, features, occupancy):
    return pl.pallas_call(
        pack_kernel,
        out_shape=(
            jax.ShapeDtypeStruct((SX, PAIRS, 2, SZ, LANES), bf16),
            jax.ShapeDtypeStruct((SX, PAIRS * SZ, 2 * LANES), bf16),
            jax.ShapeDtypeStruct((SX // 2, PAIRS * 8, 2 * LANES), f32),
        ),
        in_specs=[SMEM, VMEM, VMEM],
        out_specs=(VMEM,) * 3,
        scratch_shapes=[pltpu.SMEM((16,), jnp.int32)],
        compiler_params=params(12),
        name="pack",
    )(coords, features, occupancy)


def face_kernel(act, y_before, y_after, low, high):
    tile_y = lax.axis_index("space") % GRID_Y
    for face, x in ((low, 0), (high, SX - 1)):
        face[0] = kept(y_before[x], tile_y > 0)
        face[1 : SY + 1] = act[x].reshape(SY, SZ, LANES)
        face[SY + 1] = kept(y_after[x], tile_y < GRID_Y - 1)


def faces(act, y_before, y_after):
    face = jax.ShapeDtypeStruct((SY + 2, SZ, LANES), bf16)
    return pl.pallas_call(
        face_kernel,
        out_shape=(face, face),
        in_specs=[VMEM] * 3,
        out_specs=(VMEM, VMEM),
        compiler_params=params(8),
        name="faces",
    )(act, y_before, y_after)


def window_forms(a, b, c, d):
    a, b, c, d = (cells.astype(f32) for cells in (a, b, c, d))
    lane = lax.broadcasted_iota(jnp.int32, a.shape, 2)
    b, c, d = pltpu.roll(b, 96, 2), pltpu.roll(c, 64, 2), pltpu.roll(d, 32, 2)
    wide = jnp.concatenate(
        [jnp.where(lane < 96, a, b), jnp.where(lane < 64, b, c), jnp.where(lane < 32, c, d)], axis=2
    ).reshape(PAIRS, 2, 8, WIDE)
    even, odd = wide[:, 0], wide[:, 1]
    place = lax.broadcasted_iota(jnp.int32, odd.shape, 1)
    before = jnp.where(place == 0, 0.0, pltpu.roll(odd, 1, 1))
    after = jnp.where(place == 7, 0.0, pltpu.roll(even, 7, 1))
    pairs = ((before, even), (even, odd), (odd, after))
    return [jnp.stack(pair, axis=1).reshape(PAIRS, SZ, WIDE).astype(bf16) for pair in pairs]


def kept(value, inside):
    return value * jnp.where(inside, 1.0, 0.0).astype(bf16)


def planes_dot(pieces, taps):
    rows = [piece.reshape(-1, WIDE) for piece in pieces]
    return plain_dot(jnp.concatenate(rows, axis=1), taps)


def mask_of(cells):
    return jnp.broadcast_to(cells[:, LANES - 1 :], cells.shape)


def rows_of(planes, parity):
    return jnp.concatenate(
        [plane[:, parity].reshape(PAIRS * SZ, LANES) for plane in planes], axis=0
    ).astype(f32)


def folded(row):
    return row[:, :LANES] + row[:, LANES:]


MID = SX - 2
STEP = 1
GROUP = 2


def merged(first, second):
    (mean0, square0, count0), (mean1, square1, count1) = first, second
    count = count0 + count1
    mean = (mean0 * count0 + mean1 * count1) / jnp.maximum(count, 1.0)
    square = square0 + square1 + count0 * (mean0 - mean) ** 2 + count1 * (mean1 - mean) ** 2
    return mean, square, count


def moments_of(value, mask):
    count = folded(jnp.sum(mask, axis=0, keepdims=True))
    mean = folded(jnp.sum(value * mask, axis=0, keepdims=True)) / jnp.maximum(count, 1.0)
    gap = (value - jnp.concatenate([mean, mean], axis=1)) * mask
    return mean, folded(jnp.sum(gap * gap, axis=0, keepdims=True)), count


def middle_kernel(act, masks, y_before, y_after, weight, out, partial, stats, taps, grid):
    tile_y = lax.axis_index("space") % GRID_Y

    def fill(x):
        before = kept(y_before[x], tile_y > 0)[None]
        after = kept(y_after[x], tile_y < GRID_Y - 1)[None]
        plane = act[x]
        even, odd = plane[:, 0], plane[:, 1]
        forms = window_forms(
            jnp.concatenate([before, odd[:-1]], axis=0),
            even,
            odd,
            jnp.concatenate([even[1:], after], axis=0),
        )
        for c in range(3):
            grid[c, x] = forms[c]

    taps[...] = jnp.zeros(taps.shape, bf16)
    for a in range(3):
        for b in range(3):
            for c in range(3):
                for parity in range(2):
                    first = (a * 3 + c) * WIDE + (b + parity) * C
                    taps[first : first + C, parity * LANES : parity * LANES + C] = weight[(a * 3 + b) * 3 + c].T
    for x in range(STEP + 2):
        fill(x)
    pieces = [grid[c, a] for a in range(2) for c in range(3)]
    partial[0] = planes_dot(pieces, taps[3 * WIDE :])
    zero = jnp.zeros((1, LANES), f32)
    carry = (zero, zero, zero)
    for x in range(0, MID, STEP):
        for later in range(x + STEP + 2, min(x + 2 * STEP + 2, SX)):
            fill(later)
        pieces = [grid[c, x + a : x + a + STEP] for a in range(3) for c in range(3)]
        value = planes_dot(pieces, taps[...])
        out[x : x + STEP] = value.reshape(STEP, PAIRS * SZ, 2 * LANES)
        mask = masks[x + 1 : x + 1 + STEP].reshape(STEP * PAIRS * SZ, 2 * LANES).astype(f32)
        carry = merged(carry, moments_of(value, mask))
    pieces = [grid[c, SX - 2 + a] for a in range(2) for c in range(3)]
    partial[1] = planes_dot(pieces, taps[: 6 * WIDE])
    stats[...] = jnp.concatenate(list(carry) + [jnp.zeros((5, LANES), f32)], axis=0)


def middle(act, masks, y_before, y_after, weight):
    return pl.pallas_call(
        middle_kernel,
        out_shape=(
            pltpu.VMEM((MID, PAIRS * SZ, 2 * LANES), f32),
            jax.ShapeDtypeStruct((2, PAIRS * SZ, 2 * LANES), f32),
            jax.ShapeDtypeStruct((8, LANES), f32),
            jax.ShapeDtypeStruct((9 * WIDE, 2 * LANES), bf16),
        ),
        in_specs=[VMEM] * 5,
        out_specs=(VMEM,) * 4,
        scratch_shapes=[pltpu.VMEM((3, SX, PAIRS, SZ, WIDE), bf16)],
        compiler_params=params(26),
        name="middle",
    )(act, masks, y_before, y_after, weight)


def edge_kernel(masks, x_before, x_after, partial, taps, part, owners, out, stats):
    tile_x = lax.axis_index("space") // GRID_Y
    last_x = lax.axis_size("space") // GRID_Y - 1
    carry = (part[0:1], part[1:2], part[2:3])
    sides = ((x_before, tile_x > 0, 0, 0), (x_after, tile_x < last_x, 6 * WIDE, SX - 1))
    for index, (halo, inside, first, x) in enumerate(sides):
        cells = kept(halo[...], inside).reshape(PAIRS + 1, 2, SZ, LANES)
        forms = window_forms(cells[:-1, 0], cells[:-1, 1], cells[1:, 0], cells[1:, 1])
        value = partial[index] + planes_dot(forms, taps[first : first + 3 * WIDE])
        out[index] = value
        carry = merged(carry, moments_of(value, masks[x].astype(f32)))
    joint, square, both = carry
    lane = lax.broadcasted_iota(jnp.int32, (1, LANES), 1)
    joint = jnp.where(lane == LANES - 1, both, joint)
    for q in range(2):
        joint = jnp.where(lane == C + q, owners[0, q].astype(f32), joint)
    row = jnp.concatenate([joint, square], axis=1)
    stats[...] = jnp.broadcast_to(row[None], stats.shape)


def edges(masks, x_before, x_after, partial, taps, part, owners, devices):
    return pl.pallas_call(
        edge_kernel,
        out_shape=(
            jax.ShapeDtypeStruct((2, PAIRS * SZ, 2 * LANES), f32),
            jax.ShapeDtypeStruct((devices, 1, 2 * LANES), f32),
        ),
        in_specs=[VMEM] * 6 + [SMEM],
        out_specs=(VMEM, VMEM),
        compiler_params=params(16),
        name="edges",
    )(masks, x_before, x_after, partial, taps, part, owners)


def joined(table, width):
    means, squares = table[:, :, :width], table[:, :, width:]
    counts = table[:, :, width - 1 : width]
    whole = jnp.sum(counts, axis=0)
    mean = jnp.sum(means * counts, axis=0) / whole
    gap = means - mean[None]
    return mean, jnp.sum(squares + counts * gap * gap, axis=0) / whole


def section_kernel(
    mid, edge, act, table, gain, shift, weight, masks, cover, sent, names, stats, taps, down, lines
):
    level, groups = lax.axis_index("level"), lax.axis_size("level")
    for distance in range(4):
        origin = (level + groups - distance) % groups
        device = origin * lax.axis_size("space") + lax.axis_index("space")
        names[distance] = table[device][:, :LANES]
    mean, var = joined(table, LANES)
    lines[...] = jnp.zeros(lines.shape, f32)
    lines[0:1, :C] = gain[...]
    lines[1:2, :C] = shift[...]
    real = lax.broadcasted_iota(jnp.int32, (1, LANES), 1) < C
    scale = jnp.where(real, lines[0:1] / jnp.sqrt(var + epsilon), 0.0)
    mean = jnp.where(real, mean, 0.0)
    moved = lines[1:2] - mean * scale
    scale = jnp.concatenate([scale, scale], axis=1)
    moved = jnp.concatenate([moved, moved], axis=1)
    taps[...] = jnp.zeros(taps.shape, bf16)
    for a in range(2):
        for b in range(2):
            for c in range(2):
                first = ((a * 2 + c) * 2 + b) * LANES
                taps[first : first + C, :C2] = weight[(a * 2 + b) * 2 + c].T

    total = count = jnp.zeros((1, 2 * LANES), f32)
    for group in range(0, SX // 2, GROUP):
        blocks = []
        for X in range(group, group + GROUP):
            pieces = []
            for x in (2 * X, 2 * X + 1):
                conv = edge[0] if x == 0 else edge[1] if x == SX - 1 else mid[x - 1]
                active = jnp.concatenate([rows_of([act[x]], 0), rows_of([act[x]], 1)], axis=1)
                gained = masks[x].astype(f32) * jnp.maximum(conv * scale + moved, 0.0)
                section = (active + gained).reshape(PAIRS, 2, 8, 2 * LANES)
                for c in range(2):
                    pieces.append(section[:, c].reshape(PAIRS * 8, 2 * LANES).astype(bf16))
            blocks.append(jnp.concatenate(pieces, axis=1))
        value = plain_dot(jnp.concatenate(blocks, axis=0), taps[...])
        value = value.astype(bf16).astype(f32)
        covered = cover[group : group + GROUP].reshape(GROUP * PAIRS * 8, 2 * LANES)
        down[group : group + GROUP] = value.reshape(GROUP, PAIRS * 8, 2 * LANES)
        total = total + jnp.sum(value * covered, axis=0, keepdims=True)
        count = count + jnp.sum(covered, axis=0, keepdims=True)

    zero = jnp.zeros((1, 2 * LANES), f32)
    mean2 = total / jnp.maximum(count, 1.0)

    def spread_out(X, carry):
        gap = (down[X] - mean2) * cover[X]
        return carry + jnp.sum(gap * gap, axis=0, keepdims=True)

    square = zero
    for X in range(SX // 2):
        square = spread_out(X, square)
    wide_lane = lax.broadcasted_iota(jnp.int32, (1, 2 * LANES), 1)
    row = jnp.concatenate([jnp.where(wide_lane == 2 * LANES - 1, count, mean2), square], axis=1)
    stats[...] = jnp.broadcast_to(row[None], stats.shape)

    half = PAIRS // 2 * 8
    for q in range(2):
        value = down[:, q * half : (q + 1) * half].reshape(SX // 2 * half, 2 * LANES)
        covered = cover[:, q * half : (q + 1) * half].reshape(SX // 2 * half, 2 * LANES)
        coded = jnp.where(covered > 0, value, EMPTY).astype(bf16)
        sent[q] = coded.T[:C2]


def section(mid, edge, act, table, gain, shift, weight, masks, cover, devices):
    return pl.pallas_call(
        section_kernel,
        out_shape=(
            jax.ShapeDtypeStruct((2, C2, 512), bf16),
            jax.ShapeDtypeStruct((4, 1, LANES), f32),
            jax.ShapeDtypeStruct((devices, 1, 4 * LANES), f32),
        ),
        in_specs=[VMEM] * 9,
        out_specs=(VMEM,) * 3,
        scratch_shapes=[
            pltpu.VMEM((8 * LANES, 2 * LANES), bf16),
            pltpu.VMEM((SX // 2, PAIRS * 8, 2 * LANES), f32),
            pltpu.VMEM((8, LANES), f32),
        ],
        compiler_params=params(20),
        name="section",
    )(mid, edge, act, table, gain, shift, weight, masks, cover)


def merge_kernel(table, near, back, out, up, down):
    width = 2 * LANES
    means, squares = table[:, :, :width], table[:, :, width:]
    counts = table[:, :, width - 1 : width]
    whole = jnp.sum(counts, axis=0)
    mean = jnp.sum(means * counts, axis=0) / jnp.maximum(whole, 1.0)
    gap = means - mean[None]
    square = jnp.sum(squares + counts * gap * gap, axis=0)
    lane = lax.broadcasted_iota(jnp.int32, (1, width), 1)
    row = jnp.concatenate([jnp.where(lane == width - 1, whole, mean), square], axis=1)
    out[...] = row[None]
    high = row.astype(bf16).astype(f32)
    middle = (row - high).astype(bf16).astype(f32)
    low = row - high - middle
    rows = jnp.concatenate([high, middle, low, jnp.zeros((13, 2 * width), f32)], axis=0).astype(bf16)
    for block, brick in ((up, near[0]), (down, back[1])):
        block[:C2] = brick
        block[C2:] = rows


def merge(table, near, back):
    block = jax.ShapeDtypeStruct((C2 + 16, 512), bf16)
    return pl.pallas_call(
        merge_kernel,
        out_shape=(jax.ShapeDtypeStruct((1, 1, 4 * LANES), f32), block, block),
        in_specs=[VMEM] * 3,
        out_specs=(VMEM,) * 3,
        compiler_params=params(8),
        name="merge",
    )(table, near, back)


def row_of(block):
    rows = block[C2:].astype(f32)
    return rows[0:1] + rows[1:2] + rows[2:3]


def settle_kernel(
    own, near, far0, far1, back, names, row_here, row_far, gain, shift, out, lines, ready, sems
):
    lines[...] = jnp.zeros(lines.shape, f32)
    rows = (row_here[0], row_of(far0), row_far[0], row_of(far1))
    table = jnp.concatenate([row[None] for row in rows], axis=0)
    mean, var = joined(table, 2 * LANES)
    lines[0:1] = mean
    lines[1:2] = var
    lines[2:3, :C2] = gain[...]
    lines[3:4, :C2] = shift[...]
    turned = lines[...].T[:C2]
    scale = turned[:, 2:3] / jnp.sqrt(turned[:, 1:2] + epsilon)
    moved = turned[:, 3:4] - turned[:, 0:1] * scale
    level = lax.axis_index("level")
    groups = lax.axis_size("level")
    copies = []
    sources = ((own[0], own[1]), (near[0], near[1]), (far0[:C2], far1[:C2]), (back[0], back[1]))
    for distance, (first, second) in enumerate(sources):
        origin = (level + groups - distance) % groups
        named = jnp.where(names[distance] == level.astype(f32), 1.0, 0.0)
        takes0, takes1 = named[:, C : C + 1], named[:, C + 1 : C + 2]
        value0 = jnp.maximum(first.astype(f32) * scale + moved, 0.0)
        value1 = jnp.maximum(second.astype(f32) * scale + moved, 0.0)
        chosen = (
            jnp.where(takes0 > 0, value0, jnp.where(takes1 > 0, value1, 0.0)),
            jnp.where(takes0 * takes1 > 0, value1, 0.0),
        )
        for k in range(CAPC):
            slot = distance * CAPC + k
            ready[slot] = chosen[k].astype(bf16)
            copies.append(
                pltpu.make_async_copy(ready.at[slot], out.at[origin * CAPC + k], sems.at[slot])
            )
            copies[-1].start()
    for copy in copies:
        copy.wait()


def settle(rows, names, tables, gain, shift):
    return pl.pallas_call(
        settle_kernel,
        out_shape=jax.ShapeDtypeStruct((8, C2, 512), bf16),
        in_specs=[VMEM] * 10,
        out_specs=HBM,
        scratch_shapes=[
            pltpu.VMEM((8, 2 * LANES), f32),
            pltpu.VMEM((8, C2, 512), bf16),
            pltpu.SemaphoreType.DMA((8,)),
        ],
        compiler_params=params(12),
        name="settle",
    )(*rows, names, *tables, gain, shift)


def to_all(rows, axes):
    return lax.all_to_all(rows, axes, 0, 0, tiled=True)


def shards(
    features,
    occupancy,
    brick_coords,
    coarse_owner,
    conv_weight,
    conv_gain,
    conv_shift,
    reduce_weight,
    down_gain,
    down_shift,
):
    space_count = lax.axis_size("space")
    level_count = lax.axis_size("level")
    grid_x = space_count // GRID_Y

    def from_tile(block, step_x, step_y):
        route = []
        for s in range(space_count):
            x, y = s // GRID_Y, s % GRID_Y
            route.append(((x + step_x) % grid_x * GRID_Y + (y + step_y) % GRID_Y, s))
        return lax.ppermute(block, "space", route)

    y_low, y_high, coords, gates = pack_sides(brick_coords, features, occupancy)
    y_before = from_tile(y_high, 0, -1)
    y_after = from_tile(y_low, 0, 1)
    act, masks, cover = pack(coords, features, gates)
    x_low, x_high = faces(act, y_before, y_after)
    x_before = from_tile(x_high, -1, 0)
    x_after = from_tile(x_low, 1, 0)
    mid, partial, part, taps = middle(act, masks, y_before, y_after, conv_weight)
    edge, stats = edges(
        masks,
        x_before,
        x_after,
        partial,
        taps,
        part,
        coarse_owner.reshape(1, 2),
        space_count * level_count,
    )
    sent, names, stats2 = section(
        mid,
        edge,
        act,
        to_all(stats, ("level", "space")),
        conv_gain[None],
        conv_shift[None],
        reduce_weight,
        masks,
        cover,
        space_count,
    )
    def up_level(block, distance):
        route = [(g, (g + distance) % level_count) for g in range(level_count)]
        return lax.ppermute(block, "level", route)

    near = up_level(sent, 1)
    back = up_level(sent, -1)
    here, up, down = merge(to_all(stats2, "space"), near, back)
    tables = [here, up_level(here, 2)]
    far0 = up_level(up, 1)
    far1 = up_level(down, -1)
    return settle(
        (sent, near, far0, far1, back), names, tables, down_gain[None], down_shift[None]
    )


def solution(mesh):
    in_specs = (
        P(("level", "space"), None, None),
        P(("level", "space"), None),
        P(None, ("level", "space")),
        P(("level", "space"), None),
        P(),
        P(),
        P(),
        P(),
        P(),
        P(),
    )
    out_specs = P(("level", "space"), None, None)
    return jax.shard_map(shards, mesh=mesh, in_specs=in_specs, out_specs=out_specs, check_vma=False)
```
